32 devices in a mesh: root: 4 (over x, core), col: 8 (over z, y).
Axes of the slice: x: 2, y: 2, z: 4, core: 2. Of those that a mesh axis runs over, the one named last changes fastest.
Arguments:
- coeffs: float32 [4, 3072, 3072], P('root', 'col'), may hold values from -6 to 6
- diagonal: float32 [3072, 3072], P('col'), may hold values from -1 to 1
- shift: float32 [4], P('root'), may hold values from -1 to 1
- rotation: float32 [4, 4], replicated, may hold values from -1 to 1, as said below
- string_blocks: bfloat16 [30720, 128], P('col'), may hold values from -0.15625 to 0.15625
- block_cols: int32 [24, 10], replicated, may hold values from 0 to 23, all different within a row
Outputs:
- filtered: float32 [4, 3072, 3072], P('root', 'col')
The draws below stay inside these ranges and needn't reach their ends.
Inputs may be any that keep to these rules, and one draw needn't show every extreme that they name: `block_cols`: each row names 10 different block columns, and every block column is named by some row. rotation is an orthogonal matrix.
All inputs are finite; a program needn't handle non-finite values.
Results may differ from the reference program's by a relative error of at most 0.0003.
Values may be sent and summed in bfloat16 or wider, within the bound.
No kernel may reach another device: no remote copies, remote signals or barrier semaphores. Data moves between devices by JAX's collectives and lax.ppermute only.
A program may use at most 192 MiB of HBM per device.

```python
import jax
import jax.numpy as jnp
from jax import lax

STRINGS = 3072
BLK = 128
FILL = 10
NBLK = 24
ROOTS = 4


def draw_rotation(key, part):
    raw = jax.random.normal(jax.random.fold_in(key, 17), (ROOTS, ROOTS), jnp.float32)
    vectors = []
    for index in range(ROOTS):
        current = raw[index]
        for earlier in vectors:
            current = current - jnp.dot(earlier, current) * earlier
        current = current / jnp.sqrt(jnp.sum(current * current))
        vectors.append(current)
    return jnp.stack(vectors, axis=0)


def steps_of(key, dims, shards, smallest, high):
    def one(dim, blocks):
        steps = jax.random.uniform(jax.random.fold_in(jax.random.fold_in(key, 6), dim), (blocks,), jnp.float32, smallest / len(shards), high / len(shards))
        return jnp.repeat(jnp.exp(steps), dims[dim] // blocks).reshape((-1,) + (1,) * (len(dims) - dim - 1))

    loudness = one(*shards[0])
    for cut in shards[1:]:
        loudness = loudness * one(*cut)
    return loudness


def picks_of(stream_key, rows, number_of, top, lift):
    order = jax.random.permutation(jax.random.fold_in(stream_key, 1), number_of)
    boost = order
    for power in range(3):
        boost = boost * boost // number_of
    boost = boost * lift // number_of
    lots = jax.random.randint(jax.random.fold_in(stream_key, 2), (rows, number_of), 0, 4096) + boost
    sure = jax.random.permutation(jax.random.fold_in(stream_key, 3), rows)[jnp.arange(number_of) % rows]
    lots = jnp.where(jnp.arange(rows)[:, None] == sure[None, :], 1 << 14, lots)
    priority = lots * number_of + jnp.arange(number_of)
    return lax.top_k(priority.astype(jnp.int32), top)[1].astype(jnp.int32)


def gaussian(key, extent, spread, bound, split=(), dtype=jnp.bfloat16):
    gain = steps_of(key, extent, split, -0.22, 0.18) if split else 1.0
    entries = jax.random.normal(key, extent, jnp.float32) * spread * gain
    return jnp.minimum(jnp.maximum(entries, -bound), bound).astype(dtype)


def setup_inputs(seed: int = 0) -> dict:
    arg_keys = jax.random.split(jax.random.key(seed), 7)
    coeffs = gaussian(arg_keys[0], (ROOTS, STRINGS, STRINGS), 1.0, 6.0, ((0, 4), (1, 8)), jnp.float32)
    diagonal = jnp.clip(jax.random.uniform(arg_keys[1], (STRINGS, STRINGS), jnp.float32, -1.0, 1.0) * steps_of(arg_keys[1], (STRINGS, STRINGS), ((0, 8),), -0.4, 0.0), -1.0, 1.0)
    shift = jnp.clip(jax.random.uniform(arg_keys[2], (ROOTS,), jnp.float32, -1.0, 1.0) * steps_of(arg_keys[2], (ROOTS,), ((0, 4),), -0.4, 0.0), -1.0, 1.0)
    rotation = draw_rotation(jax.random.fold_in(arg_keys[6], 71), 0)
    string_blocks = gaussian(arg_keys[4], (NBLK * FILL * BLK, BLK), (FILL * BLK) ** -0.5, 0.15625, ((0, 8),))
    block_cols = picks_of(arg_keys[5], NBLK, NBLK, FILL, 0)
    return {"coeffs": coeffs, "diagonal": diagonal, "shift": shift, "rotation": rotation, "string_blocks": string_blocks, "block_cols": block_cols}


def apply_blocks(matrix, string_blocks, block_cols):
    height, breadth = matrix.shape
    nblocks, filled = block_cols.shape
    blocksize = breadth // nblocks
    grouped = matrix.reshape(height, nblocks, blocksize)
    picked = jnp.take(grouped, block_cols, axis=1).astype(jnp.float32)
    tiles = string_blocks.reshape(nblocks, filled, blocksize, blocksize).astype(jnp.float32)
    result = jnp.einsum("rifk,ifjk->rij", picked, tiles, precision=lax.Precision.HIGHEST)
    return result.reshape(height, breadth)


def apply_rows(matrix, string_blocks, block_cols):
    breadth = matrix.shape[1]
    stacked = matrix.reshape(-1, 256, breadth)
    result = lax.map(lambda piece: apply_blocks(piece, string_blocks, block_cols), stacked)
    return result.reshape(-1, breadth)


def sigma(vector, diagonal, string_blocks, block_cols):
    alpha_part = apply_rows(vector, string_blocks, block_cols)
    beta_part = apply_rows(vector.T, string_blocks, block_cols).T
    return alpha_part + beta_part + diagonal * vector


def reference(coeffs, diagonal, shift, rotation, string_blocks, block_cols):
    seconds = []
    for index in range(ROOTS):
        start = coeffs[index]
        energy = shift[index]
        first = 0.5 * (sigma(start, diagonal, string_blocks, block_cols) - energy * start)
        second = (sigma(first, diagonal, string_blocks, block_cols) - energy * first) - start
        seconds.append(second)
    stacked = jnp.stack(seconds, axis=0)
    return jnp.einsum("rs,sba->rba", rotation, stacked, precision=lax.Precision.HIGHEST)
```

```python
import functools

import jax
import jax.numpy as jnp
from jax import lax
from jax.experimental import pallas as pl
from jax.experimental.pallas import tpu as pltpu
from jax.sharding import PartitionSpec as P

LANES = 128
PAD = 16
TOP = 32764.0
LIMIT = 56 * 1024 * 1024


def scale_of(mantissa, exponent):
    return mantissa * jnp.exp2(exponent - 7.0) * (1.0 / TOP)


def encode(piece):
    width = piece.shape[1]
    top = jnp.maximum(jnp.max(jnp.abs(piece), axis=0, keepdims=True), 1e-25)
    exponent = jnp.floor(jnp.log2(top))
    mantissa = jnp.floor(top * jnp.exp2(7.0 - exponent)) + 1.0
    codes = jnp.floor(piece * (1.0 / scale_of(mantissa, exponent)) + 0.5)
    codes = codes.astype(jnp.int32).astype(jnp.int16)
    row = lax.broadcasted_iota(jnp.int32, (PAD, width), 0)
    tail = jnp.where(row == 0, mantissa, jnp.where(row == 1, exponent, 0.0))
    return codes, tail.astype(jnp.int32).astype(jnp.int16)


def put(ref, index, piece):
    height = piece.shape[0]
    codes, tail = encode(piece)
    ref[index, pl.ds(0, height), :] = codes
    ref[index, pl.ds(height, PAD), :] = tail


def decode(coded):
    height = coded.shape[0] - PAD
    tail = coded[height:].astype(jnp.int32).astype(jnp.float32)
    codes = coded[:height].astype(jnp.int32).astype(jnp.float32)
    return codes * scale_of(tail[0:1], tail[1:2])


def split_into(halves, block, value):
    rows = value.shape[0]
    high = value.astype(jnp.bfloat16)
    halves[block, pl.ds(0, rows), :] = high
    low = value - high.astype(jnp.float32)
    halves[block, pl.ds(rows, rows), :] = low.astype(jnp.bfloat16)


def apply_row(halves, tiles, place, cols, block, fill, blk):
    rows = halves.shape[1] // 2
    total = jnp.zeros((2 * rows, blk), jnp.float32)
    for first in range(0, fill, 2):
        terms = range(first, min(first + 2, fill))
        left = [halves[cols[block, f]] for f in terms]
        right = [tiles[pl.ds((place * fill + f) * blk, blk), :] for f in terms]
        total += lax.dot_general(
            jnp.concatenate(left, axis=1),
            jnp.concatenate(right, axis=1),
            (((1,), (1,)), ((), ())),
            preferred_element_type=jnp.float32,
        )
    return total[:rows] + total[rows:]


def pack_kernel(v_ref, out_ref):
    put(out_ref, 0, v_ref[...].T)


def right_first_kernel(dims, cols, shift, v_ref, d_ref, tiles, w_ref, u_ref, halves, turned):
    nblk, fill, blk, per = dims
    step = pl.program_id(0)

    @pl.when(step == 0)
    def _():
        for b in range(nblk):
            split_into(halves, b, v_ref[:, b * blk : (b + 1) * blk])

    for t in range(per):
        lanes = slice(t * blk, (t + 1) * blk)
        block = step * per + t
        here = v_ref[:, pl.ds(pl.multiple_of(block * blk, blk), blk)]
        moved = apply_row(halves, tiles, t, cols, block, fill, blk)
        whole = moved + (d_ref[:, lanes] - shift[0, 0]) * here
        w_ref[:, lanes] = whole
        turned[lanes, :] = (moved + whole).T
    put(u_ref, 0, turned[...])


def left_first_kernel(dims, cols, tv_ref, tiles, y_ref, halves):
    nblk, fill, blk, per = dims
    step = pl.program_id(0)

    @pl.when(step == 0)
    def _():
        for p in range(nblk // per):
            value = decode(tv_ref[p])
            for t in range(per):
                split_into(halves, p * per + t, value[:, t * blk : (t + 1) * blk])

    for t in range(per):
        y_ref[:, t * blk : (t + 1) * blk] = apply_row(halves, tiles, t, cols, step * per + t, fill, blk)


def right_second_kernel(dims, cols, shift, w_ref, v_ref, d_ref, tiles, p_ref, halves):
    nblk, fill, blk, per = dims
    step = pl.program_id(0)

    @pl.when(step == 0)
    def _():
        for b in range(nblk):
            split_into(halves, b, w_ref[:, b * blk : (b + 1) * blk])

    for t in range(per):
        lanes = slice(t * blk, (t + 1) * blk)
        block = step * per + t
        here = w_ref[:, pl.ds(pl.multiple_of(block * blk, blk), blk)]
        moved = apply_row(halves, tiles, t, cols, block, fill, blk)
        p_ref[:, lanes] = 0.5 * (moved + (d_ref[:, lanes] - shift[0, 0]) * here) - v_ref[:, lanes]


def left_second_kernel(dims, cols, shift, tu_ref, y_ref, dt_ref, tiles, *rest):
    nblk, fill, blk, per = dims
    outs, halves, turned = rest[:-2], rest[-2], rest[-1]
    step = pl.program_id(0)
    slab = dt_ref.shape[2]

    @pl.when(step == 0)
    def _():
        for p in range(nblk // per):
            value = decode(tu_ref[p]) + y_ref[:, p * per * blk : (p + 1) * per * blk]
            for t in range(per):
                split_into(halves, p * per + t, value[:, t * blk : (t + 1) * blk])

    for t in range(per):
        lanes = slice(t * blk, (t + 1) * blk)
        block = step * per + t
        here = y_ref[:, pl.ds(pl.multiple_of(block * blk, blk), blk)]
        diagonal = [
            dt_ref[r, 0, :, lanes].astype(jnp.int32).astype(jnp.float32)
            for r in range(dt_ref.shape[0])
        ]
        diagonal = jnp.concatenate(diagonal, axis=0) * (1.0 / 32767.0)
        moved = apply_row(halves, tiles, t, cols, block, fill, blk)
        turned[lanes, :] = (moved + (diagonal - shift[0, 0]) * here).T
    width = turned.shape[1] // len(outs)
    for k, out in enumerate(outs):
        put(out, 0, turned[:, k * width : (k + 1) * width])


def second_kernel(z_ref, p_ref, out_ref):
    put(out_ref, 0, 0.5 * decode(z_ref[0]) + p_ref[...])


def rotate_kernel(chunks, weights, *refs):
    ins, out_ref = refs[:-1], refs[-1]
    members = len(ins) // chunks
    width = out_ref.shape[2] // chunks
    for k in range(chunks):
        total = jnp.zeros((out_ref.shape[1], width), jnp.float32)
        for m in range(members):
            total += weights[0, m] * decode(ins[k * members + m][0])
        out_ref[0, :, k * width : (k + 1) * width] = total


def smem():
    return pl.BlockSpec(memory_space=pltpu.SMEM)


def call(kernel, grid, in_specs, out_specs, out_shape, scratch, flops, moved):
    return pl.pallas_call(
        kernel,
        grid=(grid,),
        in_specs=in_specs,
        out_specs=out_specs,
        out_shape=out_shape,
        scratch_shapes=scratch,
        compiler_params=pltpu.CompilerParams(
            dimension_semantics=("arbitrary",), vmem_limit_bytes=LIMIT
        ),
        cost_estimate=pl.CostEstimate(flops=flops, bytes_accessed=moved, transcendentals=0),
    )


def blocked_shards(sizes, coeffs, diagonal, shift, rotation, string_blocks, block_cols):
    roots, groups = sizes
    start = coeffs[0]
    rows, strings = start.shape
    nblk, fill = block_cols.shape
    blk = strings // nblk
    width = strings // groups
    per = width // blk
    chunks = per
    dims = (nblk, fill, blk, per)
    energy = shift.reshape(1, 1)
    root = lax.axis_index("root")
    f32, i16 = jnp.float32, jnp.int16

    def swap(pieces):
        return lax.all_to_all(pieces, "col", split_axis=0, concat_axis=0, tiled=True)

    piece = pl.BlockSpec((rows, width), lambda q: (0, q))
    whole = pl.BlockSpec((rows, strings), lambda q: (0, 0), pipeline_mode=pl.Buffered(1))
    tall = pl.BlockSpec((width, strings), lambda q: (0, 0), pipeline_mode=pl.Buffered(1))
    coded = pl.BlockSpec((1, width + PAD, rows), lambda q: (q, 0, 0))
    all_coded = pl.BlockSpec((groups, width + PAD, rows), lambda q: (0, 0, 0), pipeline_mode=pl.Buffered(1))
    tile_spec = pl.BlockSpec((per * fill * blk, blk), lambda q: (q, 0))
    codes_shape = jax.ShapeDtypeStruct((groups, width + PAD, rows), i16)
    row_shape = jax.ShapeDtypeStruct((rows, strings), f32)
    row_halves = pltpu.VMEM((nblk, 2 * rows, blk), jnp.bfloat16)
    col_halves = pltpu.VMEM((nblk, 2 * width, blk), jnp.bfloat16)
    work = 2 * 2 * rows * strings * fill * blk
    size = 4 * rows * strings

    share = string_blocks.shape[0] // roots
    mine = lax.dynamic_slice_in_dim(string_blocks, root * share, share, 0)
    tiles = lax.all_gather(mine, ("col", "root"), axis=0, tiled=True)

    tv = call(pack_kernel, groups, [piece], coded, codes_shape, [], 0, size * 3 // 2)(start)
    tv = swap(tv)

    slab = width // roots
    codes = jnp.round(diagonal * 32767.0).astype(jnp.int32).astype(i16)
    codes = codes.reshape(rows, groups, roots, slab)
    codes = lax.dynamic_index_in_dim(codes, root, 2, keepdims=False)
    codes = swap(codes.transpose(1, 2, 0))
    turned_diagonal = lax.all_gather(codes, "root", axis=0, tiled=False)

    w, tu = call(
        functools.partial(right_first_kernel, dims),
        groups,
        [smem(), smem(), whole, piece, tile_spec],
        [piece, coded],
        [row_shape, codes_shape],
        [row_halves, pltpu.VMEM((width, rows), f32)],
        work,
        size * 4 + size // 2,
    )(block_cols, energy, start, diagonal, tiles)
    tu = swap(tu)

    y = call(
        functools.partial(left_first_kernel, dims),
        groups,
        [smem(), all_coded, tile_spec],
        pl.BlockSpec((width, width), lambda q: (0, q)),
        jax.ShapeDtypeStruct((width, strings), f32),
        [col_halves],
        work,
        size * 3,
    )(block_cols, tv, tiles)

    base = call(
        functools.partial(right_second_kernel, dims),
        groups,
        [smem(), smem(), whole, piece, piece, tile_spec],
        piece,
        row_shape,
        [row_halves],
        work,
        size * 5,
    )(block_cols, energy, w, start, diagonal, tiles)

    part = width // chunks
    chunk_coded = pl.BlockSpec((1, rows + PAD, part), lambda q: (q, 0, 0))
    chunk_shape = jax.ShapeDtypeStruct((groups, rows + PAD, part), i16)
    tz = call(
        functools.partial(left_second_kernel, dims),
        groups,
        [
            smem(),
            smem(),
            all_coded,
            tall,
            pl.BlockSpec((roots, 1, slab, rows), lambda q: (0, q, 0, 0)),
            tile_spec,
        ],
        [chunk_coded] * chunks,
        [chunk_shape] * chunks,
        [col_halves, pltpu.VMEM((rows, width), f32)],
        work,
        size * 4,
    )(block_cols, energy, tu, y, turned_diagonal, tiles)

    masks = [0]
    held = []
    for k in range(chunks):
        z = swap(tz[k])
        second = call(
            second_kernel,
            groups,
            [chunk_coded, pl.BlockSpec((rows, part), lambda q, k=k: (0, q * chunks + k))],
            chunk_coded,
            chunk_shape,
            [],
            0,
            size * 2 // chunks,
        )(z, base)
        have, masks, bit = [second], [0], roots // 2
        while bit:
            pairs = [(r, r ^ bit) for r in range(roots)]
            have = have + [lax.ppermute(h, "root", pairs) for h in have]
            masks = masks + [m ^ bit for m in masks]
            bit //= 2
        held += have
    weights = rotation[root][jnp.bitwise_xor(root, jnp.array(masks, jnp.int32))]
    return call(
        functools.partial(rotate_kernel, chunks),
        groups,
        [smem()] + [chunk_coded] * len(held),
        pl.BlockSpec((1, rows, width), lambda q: (0, 0, q)),
        jax.ShapeDtypeStruct((1, rows, strings), f32),
        [],
        0,
        size * 3,
    )(weights.reshape(1, -1), *held)


def plain_blocks(matrix, operator_blocks, block_cols):
    height, breadth = matrix.shape
    nblocks, filled = block_cols.shape
    blocksize = breadth // nblocks
    grouped = matrix.reshape(height, nblocks, blocksize)
    picked = jnp.take(grouped, block_cols, axis=1)
    tiles = operator_blocks.reshape(nblocks, filled, blocksize, blocksize).astype(jnp.float32)
    result = jnp.einsum("rifk,ifjk->rij", picked, tiles, precision=lax.Precision.HIGHEST)
    return result.reshape(height, breadth)


def plain_swap(matrix):
    height, breadth = matrix.shape
    pieces = matrix.reshape(height, breadth // height, height).transpose(1, 2, 0)
    moved = lax.all_to_all(pieces, "col", split_axis=0, concat_axis=0, tiled=True)
    return moved.transpose(1, 0, 2).reshape(height, breadth)


def plain_shards(coeffs, diagonal, shift, rotation, string_blocks, block_cols):
    start = coeffs[0]
    energy = shift[0]
    operator_blocks = lax.all_gather(string_blocks, "col", axis=0, tiled=True)

    def sigma(vector):
        beta = plain_swap(plain_blocks(plain_swap(vector), operator_blocks, block_cols))
        return plain_blocks(vector, operator_blocks, block_cols) + beta + diagonal * vector

    first = 0.5 * (sigma(start) - energy * start)
    second = sigma(first) - energy * first - start
    weights = lax.dynamic_index_in_dim(rotation, lax.axis_index("root"), 1, keepdims=False)
    terms = weights[:, None, None] * second[None]
    return lax.psum_scatter(terms, "root", scatter_dimension=0, tiled=True)


def solution(mesh):
    roots, groups = mesh.shape["root"], mesh.shape["col"]

    def shards(coeffs, diagonal, shift, rotation, string_blocks, block_cols):
        rows, strings = coeffs.shape[1:]
        blk = strings // block_cols.shape[0]
        width = strings // groups
        regular = blk % LANES == 0 and width % blk == 0 and rows == width
        regular = regular and roots & (roots - 1) == 0 and width % (16 * roots) == 0
        args = (coeffs, diagonal, shift, rotation, string_blocks, block_cols)
        if regular and string_blocks.shape[0] % (16 * roots) == 0:
            return blocked_shards((roots, groups), *args)
        return plain_shards(*args)

    return jax.shard_map(
        shards,
        mesh=mesh,
        in_specs=(P("root", "col", None), P("col", None), P("root"), P(), P("col", None), P()),
        out_specs=P("root", "col", None),
        check_vma=False,
    )
```

```python
import functools

import jax
import jax.numpy as jnp
from jax import lax
from jax.experimental import pallas as pl
from jax.experimental.pallas import tpu as pltpu
from jax.sharding import PartitionSpec as P

LANES = 128
PAD = 16
TOP = 32764.0
LIMIT = 56 * 1024 * 1024


def scale_of(mantissa, exponent):
    return mantissa * jnp.exp2(exponent - 7.0) * (1.0 / TOP)


def encode(piece):
    width = piece.shape[1]
    top = jnp.maximum(jnp.max(jnp.abs(piece), axis=0, keepdims=True), 1e-25)
    exponent = jnp.floor(jnp.log2(top))
    mantissa = jnp.floor(top * jnp.exp2(7.0 - exponent)) + 1.0
    codes = jnp.floor(piece * (1.0 / scale_of(mantissa, exponent)) + 0.5)
    codes = codes.astype(jnp.int32).astype(jnp.int16)
    row = lax.broadcasted_iota(jnp.int32, (PAD, width), 0)
    tail = jnp.where(row == 0, mantissa, jnp.where(row == 1, exponent, 0.0))
    return codes, tail.astype(jnp.int32).astype(jnp.int16)


def put(ref, index, piece):
    height = piece.shape[0]
    codes, tail = encode(piece)
    ref[index, pl.ds(0, height), :] = codes
    ref[index, pl.ds(height, PAD), :] = tail


def decode(codes, tail):
    tail = tail.astype(jnp.int32).astype(jnp.float32)
    return codes.astype(jnp.int32).astype(jnp.float32) * scale_of(tail[0:1], tail[1:2])


def take(ref, index):
    height = ref.shape[1] - PAD
    return decode(ref[index, pl.ds(0, height), :], ref[index, pl.ds(height, PAD), :])


def split_into(halves, block, value):
    rows = value.shape[0]
    high = value.astype(jnp.bfloat16)
    halves[block, pl.ds(0, rows), :] = high
    low = value - high.astype(jnp.float32)
    halves[block, pl.ds(rows, rows), :] = low.astype(jnp.bfloat16)


def apply_row(halves, tiles, place, cols, block, fill, blk):
    rows = halves.shape[1] // 2
    total = jnp.zeros((2 * rows, blk), jnp.float32)
    for first in range(0, fill, 2):
        terms = range(first, min(first + 2, fill))
        left = [halves[cols[block, f]] for f in terms]
        right = [tiles[pl.ds((place * fill + f) * blk, blk), :] for f in terms]
        total += lax.dot_general(
            jnp.concatenate(left, axis=1),
            jnp.concatenate(right, axis=1),
            (((1,), (1,)), ((), ())),
            preferred_element_type=jnp.float32,
        )
    return total[:rows] + total[rows:]


def pack_kernel(v_ref, out_ref):
    put(out_ref, 0, v_ref[...].T)


def right_first_kernel(dims, cols, shift, place, v_ref, d_ref, own, *rest):
    nblk, fill, blk, per = dims
    shards, (w_ref, u_ref, tiles_ref, halves, turned, tiles) = rest[:-6], rest[-6:]
    step = pl.program_id(0)
    size = own.shape[0]

    @pl.when(step == 0)
    def _():
        for b in range(nblk):
            split_into(halves, b, v_ref[:, b * blk : (b + 1) * blk])
        tiles[pl.ds(pl.multiple_of(place[0, 0] * size, size), size), :] = own[...]

        @pl.loop(0, size // blk)
        def _(b):
            for k, shard in enumerate(shards):
                share = shard.shape[1]
                base = place[0, 1 + k] * size + place[1, 1 + k] * share
                at = pl.multiple_of(base + b * blk, share)
                tiles[pl.ds(at, share), :] = shard[b]

    here_tiles = tiles.at[pl.ds(pl.multiple_of(step * size, size), size), :]
    tiles_ref[...] = here_tiles[...]
    for t in range(per):
        lanes = slice(t * blk, (t + 1) * blk)
        block = step * per + t
        here = v_ref[:, pl.ds(pl.multiple_of(block * blk, blk), blk)]
        moved = apply_row(halves, here_tiles, t, cols, block, fill, blk)
        whole = moved + (d_ref[:, lanes] - shift[0, 0]) * here
        w_ref[:, lanes] = whole
        turned[lanes, :] = (moved + whole).T
    put(u_ref, 0, turned[...])


def left_first_kernel(dims, cols, tv_ref, tiles, y_ref, halves):
    nblk, fill, blk, per = dims
    step = pl.program_id(0)

    @pl.when(step == 0)
    def _():
        for p in range(nblk // per):
            value = take(tv_ref, p)
            for t in range(per):
                split_into(halves, p * per + t, value[:, t * blk : (t + 1) * blk])

    for t in range(per):
        y_ref[:, t * blk : (t + 1) * blk] = apply_row(halves, tiles, t, cols, step * per + t, fill, blk)


def right_second_kernel(dims, cols, shift, w_ref, v_ref, d_ref, tiles, p_ref, halves, part):
    nblk, fill, blk, per = dims
    step = pl.program_id(0)

    @pl.when(step == 0)
    def _():
        for b in range(nblk):
            split_into(halves, b, w_ref[:, b * blk : (b + 1) * blk])

    for t in range(per):
        lanes = slice(t * blk, (t + 1) * blk)
        block = step * per + t
        here = w_ref[:, pl.ds(pl.multiple_of(block * blk, blk), blk)]
        moved = apply_row(halves, tiles, t, cols, block, fill, blk)
        part[:, lanes] = 0.5 * (moved + (d_ref[:, lanes] - shift[0, 0]) * here) - v_ref[:, lanes]
    put(p_ref, 0, part[...])


def left_second_kernel(dims, chunk, cols, shift, tu_ref, tail_ref, y_ref, dt_ref, tiles, after, out, halves):
    nblk, fill, blk, per = dims
    del after
    step = pl.program_id(0)
    part = y_ref.shape[0]

    @pl.when(step == 0)
    def _():
        for p in range(nblk // per):
            value = decode(tu_ref[p], tail_ref[p]) + y_ref[:, p * per * blk : (p + 1) * per * blk]
            for t in range(per):
                split_into(halves, p * per + t, value[:, t * blk : (t + 1) * blk])

    done = []
    for t in range(per):
        lanes = slice(t * blk, (t + 1) * blk)
        block = step * per + t
        here = y_ref[:, pl.ds(pl.multiple_of(block * blk, blk), blk)]
        diagonal = [
            dt_ref[r, 0, :, lanes].astype(jnp.int32).astype(jnp.float32)
            for r in range(dt_ref.shape[0])
        ]
        diagonal = jnp.concatenate(diagonal, axis=0)[chunk * part : (chunk + 1) * part]
        moved = apply_row(halves, tiles, t, cols, block, fill, blk)
        done.append((0.5 * (moved + (diagonal * (1.0 / 32767.0) - shift[0, 0]) * here)).T)
    put(out, 0, jnp.concatenate(done, axis=0))


def rotate_kernel(weights, *refs):
    ins, out_ref = refs[:-1], refs[-1]
    total = weights[0, 0] * take(ins[0], 0)
    for m in range(1, len(ins)):
        total += weights[0, m] * take(ins[m], 0)
    out_ref[0] = total


def finish_kernel(weights, base_ref, *refs):
    ins, out_ref = refs[:-1], refs[-1]
    total = base_ref[0]
    for m in range(len(ins)):
        total += weights[0, m] * take(ins[m], 0)
    out_ref[0] = total


def smem():
    return pl.BlockSpec(memory_space=pltpu.SMEM)


def call(kernel, grid, in_specs, out_specs, out_shape, scratch, flops, moved, aliases={}):
    return pl.pallas_call(
        kernel,
        grid=(grid,),
        in_specs=in_specs,
        out_specs=out_specs,
        out_shape=out_shape,
        scratch_shapes=scratch,
        input_output_aliases=aliases,
        compiler_params=pltpu.CompilerParams(
            dimension_semantics=("arbitrary",), vmem_limit_bytes=LIMIT
        ),
        cost_estimate=pl.CostEstimate(flops=flops, bytes_accessed=moved, transcendentals=0),
    )


def blocked_shards(sizes, coeffs, diagonal, shift, rotation, string_blocks, block_cols):
    roots, groups = sizes
    start = coeffs[0]
    rows, strings = start.shape
    nblk, fill = block_cols.shape
    blk = strings // nblk
    width = strings // groups
    per = width // blk
    chunks = per
    dims = (nblk, fill, blk, per)
    energy = shift.reshape(1, 1)
    root = lax.axis_index("root")
    f32, i16 = jnp.float32, jnp.int16

    def swap(pieces):
        return lax.all_to_all(pieces, "col", split_axis=0, concat_axis=0, tiled=True)

    piece = pl.BlockSpec((rows, width), lambda q: (0, q))
    whole = pl.BlockSpec((rows, strings), lambda q: (0, 0), pipeline_mode=pl.Buffered(1))
    coded = pl.BlockSpec((1, width + PAD, rows), lambda q: (q, 0, 0))
    all_coded = pl.BlockSpec((groups, width + PAD, rows), lambda q: (0, 0, 0), pipeline_mode=pl.Buffered(1))
    tile_spec = pl.BlockSpec((per * fill * blk, blk), lambda q: (q, 0))
    codes_shape = jax.ShapeDtypeStruct((groups, width + PAD, rows), i16)
    row_shape = jax.ShapeDtypeStruct((rows, strings), f32)
    row_halves = pltpu.VMEM((nblk, 2 * rows, blk), jnp.bfloat16)
    col_halves = pltpu.VMEM((nblk, 2 * width, blk), jnp.bfloat16)
    work = 2 * 2 * rows * strings * fill * blk
    size = 4 * rows * strings

    def exchange(value):
        have, bit = [value], roots // 2
        while bit:
            pairs = [(r, r ^ bit) for r in range(roots)]
            have = have + [lax.ppermute(h, "root", pairs) for h in have]
            bit //= 2
        return have

    masks, bit = [0], roots // 2
    while bit:
        masks = masks + [m ^ bit for m in masks]
        bit //= 2
    far = jnp.bitwise_xor(root, jnp.array(masks, jnp.int32))

    ring = list(range(0, groups, 2)) + list(range(1, groups, 2))[::-1]
    spot = jnp.array([ring.index(c) for c in range(groups)], jnp.int32)[lax.axis_index("col")]
    share = blk // roots
    mine = string_blocks.reshape(-1, blk, blk)
    mine = lax.dynamic_slice_in_dim(mine, root * share, share, 1)
    shards, owners, forth, back = [], [0], mine, mine
    for hop in range(1, groups // 2 + 1):
        for way in (1, -1) if 2 * hop < groups else (1,):
            pairs = [(ring[s], ring[(s + way) % groups]) for s in range(groups)]
            moved = lax.ppermute(forth if way == 1 else back, "col", pairs)
            forth, back = (moved, back) if way == 1 else (forth, moved)
            shards += exchange(moved)
            owners += [-way * hop] * roots
    place = jnp.array(ring, jnp.int32)[(spot + jnp.array(owners, jnp.int32)) % groups]
    place = jnp.stack([place, jnp.concatenate([far[:1]] + [far] * (groups - 1))])

    tv = call(pack_kernel, groups, [piece], coded, codes_shape, [], 0, size * 3 // 2)(start)
    diagonal_later, tv = lax.optimization_barrier((diagonal, tv))
    tv = swap(tv)

    slab = width // roots
    codes = jnp.round(diagonal_later * 32767.0).astype(jnp.int32).astype(i16)
    codes = codes.reshape(rows, groups, roots, slab)
    codes = lax.dynamic_index_in_dim(codes, root, 2, keepdims=False)
    codes = swap(codes.transpose(1, 2, 0))
    turned_diagonal = lax.all_gather(codes, "root", axis=0, tiled=False)

    once = pl.Buffered(1)
    shard_spec = pl.BlockSpec(mine.shape, lambda q: (0, 0, 0), pipeline_mode=once)
    w, tu, tiles = call(
        functools.partial(right_first_kernel, dims),
        groups,
        [smem(), smem(), smem(), whole, piece]
        + [pl.BlockSpec(string_blocks.shape, lambda q: (0, 0), pipeline_mode=once)]
        + [shard_spec] * len(shards),
        [piece, coded, tile_spec],
        [
            row_shape,
            codes_shape,
            jax.ShapeDtypeStruct((nblk * fill * blk, blk), string_blocks.dtype),
        ],
        [
            row_halves,
            pltpu.VMEM((width, rows), f32),
            pltpu.VMEM((nblk * fill * blk, blk), string_blocks.dtype),
        ],
        work,
        size * 6,
    )(block_cols, energy, place, start, diagonal, string_blocks, *shards)
    tu = swap(tu)

    base = call(
        functools.partial(right_second_kernel, dims),
        groups,
        [smem(), smem(), whole, piece, piece, tile_spec],
        pl.BlockSpec((1, rows + PAD, width), lambda q: (q, 0, 0)),
        jax.ShapeDtypeStruct((groups, rows + PAD, width), i16),
        [row_halves, pltpu.VMEM((rows, width), f32)],
        work,
        size * 5,
    )(block_cols, energy, w, start, diagonal, tiles)

    y = call(
        functools.partial(left_first_kernel, dims),
        groups,
        [smem(), all_coded, tile_spec],
        pl.BlockSpec((width, width), lambda q: (0, q)),
        jax.ShapeDtypeStruct((width, strings), f32),
        [col_halves],
        work,
        size * 3,
    )(block_cols, tv, tiles)

    weights = rotation[root][far].reshape(1, -1)
    out = call(
        rotate_kernel,
        groups,
        [smem()] + [pl.BlockSpec((1, rows + PAD, width), lambda q: (q, 0, 0))] * roots,
        pl.BlockSpec((1, rows, width), lambda q: (0, 0, q)),
        jax.ShapeDtypeStruct((1, rows, strings), f32),
        [],
        0,
        size * 3,
    )(weights, *exchange(base))

    part = width // chunks
    chunk_coded = pl.BlockSpec((1, rows + PAD, part), lambda q: (q, 0, 0))
    for k in range(chunks):
        z = call(
            functools.partial(left_second_kernel, dims, k),
            groups,
            [
                smem(),
                smem(),
                pl.BlockSpec((groups, part, rows), lambda q, k=k: (0, k, 0), pipeline_mode=once),
                pl.BlockSpec((groups, PAD, rows), lambda q: (0, width // PAD, 0), pipeline_mode=once),
                pl.BlockSpec((part, strings), lambda q, k=k: (k, 0), pipeline_mode=once),
                pl.BlockSpec((roots, 1, slab, rows), lambda q: (0, q, 0, 0)),
                tile_spec,
                pl.BlockSpec(memory_space=pl.ANY),
            ],
            chunk_coded,
            jax.ShapeDtypeStruct((groups, rows + PAD, part), i16),
            [pltpu.VMEM((nblk, 2 * part, blk), jnp.bfloat16)],
            work // chunks,
            size * 4 // chunks,
        )(block_cols, energy, tu, tu, y, turned_diagonal, tiles, base)
        slot = pl.BlockSpec((1, rows, part), lambda q, k=k: (0, 0, q * chunks + k))
        out = call(
            finish_kernel,
            groups,
            [smem(), slot] + [chunk_coded] * roots,
            slot,
            jax.ShapeDtypeStruct((1, rows, strings), f32),
            [],
            0,
            size * 3 // chunks,
            {1: 0},
        )(weights, out, *exchange(swap(z)))
    return out


def plain_blocks(matrix, operator_blocks, block_cols):
    height, breadth = matrix.shape
    nblocks, filled = block_cols.shape
    blocksize = breadth // nblocks
    grouped = matrix.reshape(height, nblocks, blocksize)
    picked = jnp.take(grouped, block_cols, axis=1)
    tiles = operator_blocks.reshape(nblocks, filled, blocksize, blocksize).astype(jnp.float32)
    result = jnp.einsum("rifk,ifjk->rij", picked, tiles, precision=lax.Precision.HIGHEST)
    return result.reshape(height, breadth)


def plain_swap(matrix):
    height, breadth = matrix.shape
    pieces = matrix.reshape(height, breadth // height, height).transpose(1, 2, 0)
    moved = lax.all_to_all(pieces, "col", split_axis=0, concat_axis=0, tiled=True)
    return moved.transpose(1, 0, 2).reshape(height, breadth)


def plain_shards(coeffs, diagonal, shift, rotation, string_blocks, block_cols):
    start = coeffs[0]
    energy = shift[0]
    operator_blocks = lax.all_gather(string_blocks, "col", axis=0, tiled=True)

    def sigma(vector):
        beta = plain_swap(plain_blocks(plain_swap(vector), operator_blocks, block_cols))
        return plain_blocks(vector, operator_blocks, block_cols) + beta + diagonal * vector

    first = 0.5 * (sigma(start) - energy * start)
    second = sigma(first) - energy * first - start
    weights = lax.dynamic_index_in_dim(rotation, lax.axis_index("root"), 1, keepdims=False)
    terms = weights[:, None, None] * second[None]
    return lax.psum_scatter(terms, "root", scatter_dimension=0, tiled=True)


def solution(mesh):
    roots, groups = mesh.shape["root"], mesh.shape["col"]

    def shards(coeffs, diagonal, shift, rotation, string_blocks, block_cols):
        rows, strings = coeffs.shape[1:]
        blk = strings // block_cols.shape[0]
        width = strings // groups
        regular = blk % LANES == 0 and width % blk == 0 and rows == width
        regular = regular and roots & (roots - 1) == 0 and width % (16 * roots) == 0
        regular = regular and groups % 2 == 0 and blk % (16 * roots) == 0
        args = (coeffs, diagonal, shift, rotation, string_blocks, block_cols)
        if regular:
            return blocked_shards((roots, groups), *args)
        return plain_shards(*args)

    return jax.shard_map(
        shards,
        mesh=mesh,
        in_specs=(P("root", "col", None), P("col", None), P("root"), P(), P("col", None), P()),
        out_specs=P("root", "col", None),
        check_vma=False,
    )
```

```python
import functools

import jax
import jax.numpy as jnp
from jax import lax
from jax.experimental import pallas as pl
from jax.experimental.pallas import tpu as pltpu
from jax.sharding import PartitionSpec as P

LANES = 128
PAD = 16
TOP = 32764.0
LIMIT = 56 * 1024 * 1024


def scale_of(mantissa, exponent):
    return mantissa * jnp.exp2(exponent - 7.0) * (1.0 / TOP)


def encode(piece):
    width = piece.shape[1]
    top = jnp.maximum(jnp.max(jnp.abs(piece), axis=0, keepdims=True), 1e-25)
    exponent = jnp.floor(jnp.log2(top))
    mantissa = jnp.floor(top * jnp.exp2(7.0 - exponent)) + 1.0
    codes = jnp.floor(piece * (1.0 / scale_of(mantissa, exponent)) + 0.5)
    codes = codes.astype(jnp.int32).astype(jnp.int16)
    row = lax.broadcasted_iota(jnp.int32, (PAD, width), 0)
    tail = jnp.where(row == 0, mantissa, jnp.where(row == 1, exponent, 0.0))
    return codes, tail.astype(jnp.int32).astype(jnp.int16)


def put(ref, index, piece):
    height = piece.shape[0]
    codes, tail = encode(piece)
    ref[index, pl.ds(0, height), :] = codes
    ref[index, pl.ds(height, PAD), :] = tail


def decode(codes, tail):
    tail = tail.astype(jnp.int32).astype(jnp.float32)
    return codes.astype(jnp.int32).astype(jnp.float32) * scale_of(tail[0:1], tail[1:2])


def take(ref, index):
    height = ref.shape[1] - PAD
    return decode(ref[index, pl.ds(0, height), :], ref[index, pl.ds(height, PAD), :])


def split_into(halves, block, value):
    rows = value.shape[0]
    high = value.astype(jnp.bfloat16)
    halves[block, pl.ds(0, rows), :] = high
    low = value - high.astype(jnp.float32)
    halves[block, pl.ds(rows, rows), :] = low.astype(jnp.bfloat16)


def apply_row(halves, tiles, place, cols, block, fill, blk):
    rows = halves.shape[1] // 2
    total = jnp.zeros((2 * rows, blk), jnp.float32)
    for first in range(0, fill, 2):
        terms = range(first, min(first + 2, fill))
        left = [halves[cols[block, f]] for f in terms]
        right = [tiles[pl.ds((place * fill + f) * blk, blk), :] for f in terms]
        total += lax.dot_general(
            jnp.concatenate(left, axis=1),
            jnp.concatenate(right, axis=1),
            (((1,), (1,)), ((), ())),
            preferred_element_type=jnp.float32,
        )
    return total[:rows] + total[rows:]


def pack_kernel(far, v_ref, d_ref, out_ref, turned):
    put(out_ref, 0, v_ref[...].T)
    turned[...] = d_ref[...].T
    width, rows = turned.shape
    slab = out_ref.shape[1] - width - PAD
    here = turned[pl.ds(pl.multiple_of(far[0, 0] * slab, slab), slab), :]
    codes = jnp.floor(here * 32767.0 + 0.5)
    out_ref[0, pl.ds(width + PAD, slab), :] = codes.astype(jnp.int32).astype(jnp.int16)


def right_first_kernel(dims, cols, shift, far, v_ref, d_ref, *rest):
    nblk, fill, blk, per = dims
    shares, (w_ref, u_ref, tiles, halves, turned) = rest[:-5], rest[-5:]
    step = pl.program_id(0)

    @pl.when(step == 0)
    def _():
        for b in range(nblk):
            split_into(halves, b, v_ref[:, b * blk : (b + 1) * blk])

    roots = far.shape[1]
    for n, share in enumerate(shares):
        count, height = share.shape[:2]
        for b in range(count):
            at = ((n // roots) * count + b) * blk + far[0, n % roots] * height
            tiles[pl.ds(pl.multiple_of(at, height), height), :] = share[b]
    for t in range(per):
        lanes = slice(t * blk, (t + 1) * blk)
        block = step * per + t
        here = v_ref[:, pl.ds(pl.multiple_of(block * blk, blk), blk)]
        moved = apply_row(halves, tiles, t, cols, block, fill, blk)
        whole = moved + (d_ref[:, lanes] - shift[0, 0]) * here
        w_ref[:, lanes] = whole
        turned[lanes, :] = (moved + whole).T
    put(u_ref, 0, turned[...])


def left_first_kernel(dims, cols, tv_ref, tiles, y_ref, halves):
    nblk, fill, blk, per = dims
    step = pl.program_id(0)

    @pl.when(step == 0)
    def _():
        for p in range(nblk // per):
            value = take(tv_ref, p)
            for t in range(per):
                split_into(halves, p * per + t, value[:, t * blk : (t + 1) * blk])

    for t in range(per):
        y_ref[:, t * blk : (t + 1) * blk] = apply_row(halves, tiles, t, cols, step * per + t, fill, blk)


def right_second_kernel(dims, cols, shift, w_ref, v_ref, d_ref, tiles, p_ref, halves, part):
    nblk, fill, blk, per = dims
    step = pl.program_id(0)

    @pl.when(step == 0)
    def _():
        for b in range(nblk):
            split_into(halves, b, w_ref[:, b * blk : (b + 1) * blk])

    for t in range(per):
        lanes = slice(t * blk, (t + 1) * blk)
        block = step * per + t
        here = w_ref[:, pl.ds(pl.multiple_of(block * blk, blk), blk)]
        moved = apply_row(halves, tiles, t, cols, block, fill, blk)
        part[:, lanes] = 0.5 * (moved + (d_ref[:, lanes] - shift[0, 0]) * here) - v_ref[:, lanes]
    put(p_ref, 0, part[...])


def left_second_kernel(dims, chunk, cols, shift, far, tu_ref, tail_ref, y_ref, tiles, *rest):
    nblk, fill, blk, per = dims
    slabs, (_, out, halves, turned) = rest[:-4], rest[-4:]
    step = pl.program_id(0)
    part = y_ref.shape[0]

    @pl.when(step == 0)
    def _():
        for p in range(nblk // per):
            value = decode(tu_ref[p], tail_ref[p]) + y_ref[:, p * per * blk : (p + 1) * per * blk]
            for t in range(per):
                split_into(halves, p * per + t, value[:, t * blk : (t + 1) * blk])

    for m, slab in enumerate(slabs):
        height = slab.shape[1]
        at = pl.multiple_of(far[0, m] * height, height)
        turned[pl.ds(at, height), :] = slab[0].astype(jnp.int32).astype(jnp.float32)
    done = []
    for t in range(per):
        block = step * per + t
        here = y_ref[:, pl.ds(pl.multiple_of(block * blk, blk), blk)]
        diagonal = turned[chunk * part : (chunk + 1) * part, t * blk : (t + 1) * blk]
        moved = apply_row(halves, tiles, t, cols, block, fill, blk)
        done.append((0.5 * (moved + (diagonal * (1.0 / 32767.0) - shift[0, 0]) * here)).T)
    put(out, 0, jnp.concatenate(done, axis=0))


def rotate_kernel(weights, *refs):
    ins, out_ref = refs[:-1], refs[-1]
    total = weights[0, 0] * take(ins[0], 0)
    for m in range(1, len(ins)):
        total += weights[0, m] * take(ins[m], 0)
    out_ref[0] = total


def finish_kernel(weights, base_ref, *refs):
    ins, out_ref = refs[:-1], refs[-1]
    total = base_ref[0]
    for m in range(len(ins)):
        total += weights[0, m] * take(ins[m], 0)
    out_ref[0] = total


def smem():
    return pl.BlockSpec(memory_space=pltpu.SMEM)


def call(kernel, grid, in_specs, out_specs, out_shape, scratch, flops, moved, aliases={}):
    return pl.pallas_call(
        kernel,
        grid=(grid,),
        in_specs=in_specs,
        out_specs=out_specs,
        out_shape=out_shape,
        scratch_shapes=scratch,
        input_output_aliases=aliases,
        compiler_params=pltpu.CompilerParams(
            dimension_semantics=("arbitrary",), vmem_limit_bytes=LIMIT
        ),
        cost_estimate=pl.CostEstimate(flops=flops, bytes_accessed=moved, transcendentals=0),
    )


def blocked_shards(sizes, coeffs, diagonal, shift, rotation, string_blocks, block_cols):
    roots, groups = sizes
    start = coeffs[0]
    rows, strings = start.shape
    nblk, fill = block_cols.shape
    blk = strings // nblk
    width = strings // groups
    per = width // blk
    chunks = per
    dims = (nblk, fill, blk, per)
    energy = shift.reshape(1, 1)
    root = lax.axis_index("root")
    f32, i16 = jnp.float32, jnp.int16

    def swap(pieces):
        return lax.all_to_all(pieces, "col", split_axis=0, concat_axis=0, tiled=True)

    piece = pl.BlockSpec((rows, width), lambda q: (0, q))
    whole = pl.BlockSpec((rows, strings), lambda q: (0, 0), pipeline_mode=pl.Buffered(1))
    coded = pl.BlockSpec((1, width + PAD, rows), lambda q: (q, 0, 0))
    all_coded = pl.BlockSpec((groups, width + PAD, rows), lambda q: (0, 0, 0), pipeline_mode=pl.Buffered(1))
    tile_spec = pl.BlockSpec((per * fill * blk, blk), lambda q: (q, 0))
    codes_shape = jax.ShapeDtypeStruct((groups, width + PAD, rows), i16)
    row_shape = jax.ShapeDtypeStruct((rows, strings), f32)
    row_halves = pltpu.VMEM((nblk, 2 * rows, blk), jnp.bfloat16)
    col_halves = pltpu.VMEM((nblk, 2 * width, blk), jnp.bfloat16)
    work = 2 * 2 * rows * strings * fill * blk
    size = 4 * rows * strings

    def exchange(value, late=None):
        have, bit = [value], roots // 2
        while bit:
            pairs = [(r, r ^ bit) for r in range(roots)]
            have = have + [lax.ppermute(h, "root", pairs) for h in have]
            if late is not None:
                have = list(lax.optimization_barrier(tuple(have) + (late,)))[:-1]
                late = None
            bit //= 2
        return have

    masks, bit = [0], roots // 2
    while bit:
        masks = masks + [m ^ bit for m in masks]
        bit //= 2
    far = jnp.bitwise_xor(root, jnp.array(masks, jnp.int32))
    weights = rotation[root][far].reshape(1, -1)
    far = far.reshape(1, -1)

    share = blk // roots
    local = string_blocks.shape[0] // blk
    parts = 2 if local % 2 == 0 else 1
    count = local // parts
    mine = string_blocks.reshape(local, blk, blk)
    mine = lax.dynamic_slice_in_dim(mine, root * share, share, 1)
    shares = []
    for n in range(parts):
        shares += exchange(lax.all_gather(mine[n * count : (n + 1) * count], "col", axis=0, tiled=True))

    slab = width // roots
    height = width + PAD + slab
    tv = call(
        pack_kernel,
        groups,
        [smem(), piece, piece],
        pl.BlockSpec((1, height, rows), lambda q: (q, 0, 0)),
        jax.ShapeDtypeStruct((groups, height, rows), i16),
        [pltpu.VMEM((width, rows), f32)],
        0,
        size * 3,
    )(far, start, diagonal)
    tv = swap(tv)

    once = pl.Buffered(1)
    share_spec = pl.BlockSpec((count, share, blk), lambda q: (q, 0, 0))
    w, tu, tiles = call(
        functools.partial(right_first_kernel, dims),
        groups,
        [smem(), smem(), smem(), whole, piece]
        + [share_spec] * len(shares),
        [piece, coded, tile_spec],
        [
            row_shape,
            codes_shape,
            jax.ShapeDtypeStruct((nblk * fill * blk, blk), string_blocks.dtype),
        ],
        [row_halves, pltpu.VMEM((width, rows), f32)],
        work,
        size * 6,
    )(block_cols, energy, far, start, diagonal, *shares)
    tu = swap(tu)
    slabs = exchange(tv[:, width + PAD :])

    base = call(
        functools.partial(right_second_kernel, dims),
        groups,
        [smem(), smem(), whole, piece, piece, tile_spec],
        pl.BlockSpec((1, rows + PAD, width), lambda q: (q, 0, 0)),
        jax.ShapeDtypeStruct((groups, rows + PAD, width), i16),
        [row_halves, pltpu.VMEM((rows, width), f32)],
        work,
        size * 5,
    )(block_cols, energy, w, start, diagonal, tiles)

    y = call(
        functools.partial(left_first_kernel, dims),
        groups,
        [smem(), all_coded, tile_spec],
        pl.BlockSpec((width, width), lambda q: (0, q)),
        jax.ShapeDtypeStruct((width, strings), f32),
        [col_halves],
        work,
        size * 3,
    )(block_cols, tv, tiles)

    part = width // chunks
    chunk_coded = pl.BlockSpec((1, rows + PAD, part), lambda q: (q, 0, 0))
    turned = []
    for k in range(chunks):
        z = call(
            functools.partial(left_second_kernel, dims, k),
            groups,
            [
                smem(),
                smem(),
                smem(),
                pl.BlockSpec((groups, part, rows), lambda q, k=k: (0, k, 0), pipeline_mode=once),
                pl.BlockSpec((groups, PAD, rows), lambda q: (0, width // PAD, 0), pipeline_mode=once),
                pl.BlockSpec((part, strings), lambda q, k=k: (k, 0), pipeline_mode=once),
                tile_spec,
            ]
            + [pl.BlockSpec((1, slab, rows), lambda q: (q, 0, 0))] * roots
            + [pl.BlockSpec(memory_space=pl.ANY)],
            chunk_coded,
            jax.ShapeDtypeStruct((groups, rows + PAD, part), i16),
            [pltpu.VMEM((nblk, 2 * part, blk), jnp.bfloat16), pltpu.VMEM((width, rows), f32)],
            work // chunks,
            size * 4 // chunks,
        )(block_cols, energy, far, tu, tu, y, tiles, *slabs, base)
        turned.append(z)

    out = call(
        rotate_kernel,
        groups,
        [smem()] + [pl.BlockSpec((1, rows + PAD, width), lambda q: (q, 0, 0))] * roots,
        pl.BlockSpec((1, rows, width), lambda q: (0, 0, q)),
        jax.ShapeDtypeStruct((1, rows, strings), f32),
        [],
        0,
        size * 3,
    )(weights, *exchange(base, turned[-1]))

    for k in range(chunks):
        back, late = swap(turned[k]), None
        if k == chunks - 1:
            late = out
        slot = pl.BlockSpec((1, rows, part), lambda q, k=k: (0, 0, q * chunks + k))
        out = call(
            finish_kernel,
            groups,
            [smem(), slot] + [chunk_coded] * roots,
            slot,
            jax.ShapeDtypeStruct((1, rows, strings), f32),
            [],
            0,
            size * 3 // chunks,
            {1: 0},
        )(weights, out, *exchange(back, late))
    return out


def plain_blocks(matrix, operator_blocks, block_cols):
    height, breadth = matrix.shape
    nblocks, filled = block_cols.shape
    blocksize = breadth // nblocks
    grouped = matrix.reshape(height, nblocks, blocksize)
    picked = jnp.take(grouped, block_cols, axis=1)
    tiles = operator_blocks.reshape(nblocks, filled, blocksize, blocksize).astype(jnp.float32)
    result = jnp.einsum("rifk,ifjk->rij", picked, tiles, precision=lax.Precision.HIGHEST)
    return result.reshape(height, breadth)


def plain_swap(matrix):
    height, breadth = matrix.shape
    pieces = matrix.reshape(height, breadth // height, height).transpose(1, 2, 0)
    moved = lax.all_to_all(pieces, "col", split_axis=0, concat_axis=0, tiled=True)
    return moved.transpose(1, 0, 2).reshape(height, breadth)


def plain_shards(coeffs, diagonal, shift, rotation, string_blocks, block_cols):
    start = coeffs[0]
    energy = shift[0]
    operator_blocks = lax.all_gather(string_blocks, "col", axis=0, tiled=True)

    def sigma(vector):
        beta = plain_swap(plain_blocks(plain_swap(vector), operator_blocks, block_cols))
        return plain_blocks(vector, operator_blocks, block_cols) + beta + diagonal * vector

    first = 0.5 * (sigma(start) - energy * start)
    second = sigma(first) - energy * first - start
    weights = lax.dynamic_index_in_dim(rotation, lax.axis_index("root"), 1, keepdims=False)
    terms = weights[:, None, None] * second[None]
    return lax.psum_scatter(terms, "root", scatter_dimension=0, tiled=True)


def solution(mesh):
    roots, groups = mesh.shape["root"], mesh.shape["col"]

    def shards(coeffs, diagonal, shift, rotation, string_blocks, block_cols):
        rows, strings = coeffs.shape[1:]
        blk = strings // block_cols.shape[0]
        width = strings // groups
        regular = blk % LANES == 0 and width % blk == 0 and rows == width
        regular = regular and roots & (roots - 1) == 0 and width % (16 * roots) == 0
        regular = regular and groups % 2 == 0 and blk % (16 * roots) == 0
        args = (coeffs, diagonal, shift, rotation, string_blocks, block_cols)
        if regular:
            return blocked_shards((roots, groups), *args)
        return plain_shards(*args)

    return jax.shard_map(
        shards,
        mesh=mesh,
        in_specs=(P("root", "col", None), P("col", None), P("root"), P(), P("col", None), P()),
        out_specs=P("root", "col", None),
        check_vma=False,
    )
```

```python
import functools

import jax
import jax.numpy as jnp
from jax import lax
from jax.experimental import pallas as pl
from jax.experimental.pallas import tpu as pltpu
from jax.sharding import PartitionSpec as P

LANES = 128
PAD = 16
TOP = 32764.0
LIMIT = 56 * 1024 * 1024


def scale_of(mantissa, exponent):
    return mantissa * jnp.exp2(exponent - 7.0) * (1.0 / TOP)


def encode(piece):
    width = piece.shape[1]
    top = jnp.maximum(jnp.max(jnp.abs(piece), axis=0, keepdims=True), 1e-25)
    exponent = jnp.floor(jnp.log2(top))
    mantissa = jnp.floor(top * jnp.exp2(7.0 - exponent)) + 1.0
    codes = jnp.floor(piece * (1.0 / scale_of(mantissa, exponent)) + 0.5)
    codes = codes.astype(jnp.int32).astype(jnp.int16)
    row = lax.broadcasted_iota(jnp.int32, (PAD, width), 0)
    tail = jnp.where(row == 0, mantissa, jnp.where(row == 1, exponent, 0.0))
    return codes, tail.astype(jnp.int32).astype(jnp.int16)


def put(ref, index, piece):
    height = piece.shape[0]
    codes, tail = encode(piece)
    ref[index, pl.ds(0, height), :] = codes
    ref[index, pl.ds(height, PAD), :] = tail


def decode(codes, tail):
    tail = tail.astype(jnp.int32).astype(jnp.float32)
    return codes.astype(jnp.int32).astype(jnp.float32) * scale_of(tail[0:1], tail[1:2])


def take(ref, index):
    height = ref.shape[1] - PAD
    return decode(ref[index, pl.ds(0, height), :], ref[index, pl.ds(height, PAD), :])


def split_into(halves, block, value):
    rows = value.shape[0]
    high = value.astype(jnp.bfloat16)
    halves[block, pl.ds(0, rows), :] = high
    low = value - high.astype(jnp.float32)
    halves[block, pl.ds(rows, rows), :] = low.astype(jnp.bfloat16)


def apply_row(halves, tiles, place, cols, block, fill, blk):
    rows = halves.shape[1] // 2
    total = jnp.zeros((2 * rows, blk), jnp.float32)
    for first in range(0, fill, 2):
        terms = range(first, min(first + 2, fill))
        left = [halves[cols[block, f]] for f in terms]
        right = [tiles[pl.ds((place * fill + f) * blk, blk), :] for f in terms]
        total += lax.dot_general(
            jnp.concatenate(left, axis=1),
            jnp.concatenate(right, axis=1),
            (((1,), (1,)), ((), ())),
            preferred_element_type=jnp.float32,
        )
    return total[:rows] + total[rows:]


def pack_kernel(far, v_ref, d_ref, out_ref, turned):
    put(out_ref, 0, v_ref[...].T)
    turned[...] = d_ref[...].T
    width, rows = turned.shape
    slab = out_ref.shape[1] - width - PAD
    here = turned[pl.ds(pl.multiple_of(far[0, 0] * slab, slab), slab), :]
    codes = jnp.floor(here * 32767.0 + 0.5)
    out_ref[0, pl.ds(width + PAD, slab), :] = codes.astype(jnp.int32).astype(jnp.int16)


def right_first_kernel(dims, cols, shift, place, v_ref, d_ref, own, *rest):
    nblk, fill, blk, per = dims
    shards, (w_ref, u_ref, tiles_ref, halves, turned, tiles) = rest[:-6], rest[-6:]
    step = pl.program_id(0)
    size = own.shape[0]

    @pl.when(step == 0)
    def _():
        for b in range(nblk):
            split_into(halves, b, v_ref[:, b * blk : (b + 1) * blk])
        tiles[pl.ds(pl.multiple_of(place[0, 0] * size, size), size), :] = own[...]

        @pl.loop(0, size // blk)
        def _(b):
            for k, shard in enumerate(shards):
                share = shard.shape[1]
                base = place[0, 1 + k] * size + place[1, 1 + k] * share
                at = pl.multiple_of(base + b * blk, share)
                tiles[pl.ds(at, share), :] = shard[b]

    here_tiles = tiles.at[pl.ds(pl.multiple_of(step * size, size), size), :]
    tiles_ref[...] = here_tiles[...]
    for t in range(per):
        lanes = slice(t * blk, (t + 1) * blk)
        block = step * per + t
        here = v_ref[:, pl.ds(pl.multiple_of(block * blk, blk), blk)]
        moved = apply_row(halves, here_tiles, t, cols, block, fill, blk)
        whole = moved + (d_ref[:, lanes] - shift[0, 0]) * here
        w_ref[:, lanes] = whole
        turned[lanes, :] = (moved + whole).T
    put(u_ref, 0, turned[...])


def left_first_kernel(dims, cols, tv_ref, tiles, y_ref, halves):
    nblk, fill, blk, per = dims
    step = pl.program_id(0)

    @pl.when(step == 0)
    def _():
        for p in range(nblk // per):
            value = take(tv_ref, p)
            for t in range(per):
                split_into(halves, p * per + t, value[:, t * blk : (t + 1) * blk])

    for t in range(per):
        y_ref[:, t * blk : (t + 1) * blk] = apply_row(halves, tiles, t, cols, step * per + t, fill, blk)


def right_second_kernel(dims, cols, shift, w_ref, v_ref, d_ref, tiles, p_ref, halves):
    nblk, fill, blk, per = dims
    step = pl.program_id(0)

    @pl.when(step == 0)
    def _():
        for b in range(nblk):
            split_into(halves, b, w_ref[:, b * blk : (b + 1) * blk])

    for t in range(per):
        lanes = slice(t * blk, (t + 1) * blk)
        block = step * per + t
        here = w_ref[:, pl.ds(pl.multiple_of(block * blk, blk), blk)]
        moved = apply_row(halves, tiles, t, cols, block, fill, blk)
        p_ref[:, lanes] = 0.5 * (moved + (d_ref[:, lanes] - shift[0, 0]) * here) - v_ref[:, lanes]


def left_second_kernel(dims, chunk, cols, shift, far, tu_ref, tail_ref, y_ref, tiles, *rest):
    nblk, fill, blk, per = dims
    slabs, (_, out, halves, turned) = rest[:-4], rest[-4:]
    step = pl.program_id(0)
    part = y_ref.shape[0]

    @pl.when(step == 0)
    def _():
        for p in range(nblk // per):
            value = decode(tu_ref[p], tail_ref[p]) + y_ref[:, p * per * blk : (p + 1) * per * blk]
            for t in range(per):
                split_into(halves, p * per + t, value[:, t * blk : (t + 1) * blk])

    for m, slab in enumerate(slabs):
        height = slab.shape[1]
        at = pl.multiple_of(far[0, m] * height, height)
        turned[pl.ds(at, height), :] = slab[0].astype(jnp.int32).astype(jnp.float32)
    done = []
    for t in range(per):
        block = step * per + t
        here = y_ref[:, pl.ds(pl.multiple_of(block * blk, blk), blk)]
        diagonal = turned[chunk * part : (chunk + 1) * part, t * blk : (t + 1) * blk]
        moved = apply_row(halves, tiles, t, cols, block, fill, blk)
        done.append((0.5 * (moved + (diagonal * (1.0 / 32767.0) - shift[0, 0]) * here)).T)
    put(out, 0, jnp.concatenate(done, axis=0))


def second_kernel(z_ref, p_ref, out_ref):
    put(out_ref, 0, take(z_ref, 0) + p_ref[...])


def rotate_kernel(aliased, weights, *refs):
    ins, out_ref = refs[aliased:-1], refs[-1]
    total = weights[0, 0] * take(ins[0], 0)
    for m in range(1, len(ins)):
        total += weights[0, m] * take(ins[m], 0)
    out_ref[0] = total


def smem():
    return pl.BlockSpec(memory_space=pltpu.SMEM)


def call(kernel, grid, in_specs, out_specs, out_shape, scratch, flops, moved, aliases={}):
    return pl.pallas_call(
        kernel,
        grid=(grid,),
        in_specs=in_specs,
        out_specs=out_specs,
        out_shape=out_shape,
        scratch_shapes=scratch,
        input_output_aliases=aliases,
        compiler_params=pltpu.CompilerParams(
            dimension_semantics=("arbitrary",), vmem_limit_bytes=LIMIT
        ),
        cost_estimate=pl.CostEstimate(flops=flops, bytes_accessed=moved, transcendentals=0),
    )


def blocked_shards(sizes, coeffs, diagonal, shift, rotation, string_blocks, block_cols):
    roots, groups = sizes
    start = coeffs[0]
    rows, strings = start.shape
    nblk, fill = block_cols.shape
    blk = strings // nblk
    width = strings // groups
    per = width // blk
    chunks = per
    dims = (nblk, fill, blk, per)
    energy = shift.reshape(1, 1)
    root = lax.axis_index("root")
    f32, i16 = jnp.float32, jnp.int16

    def swap(pieces):
        return lax.all_to_all(pieces, "col", split_axis=0, concat_axis=0, tiled=True)

    piece = pl.BlockSpec((rows, width), lambda q: (0, q))
    whole = pl.BlockSpec((rows, strings), lambda q: (0, 0), pipeline_mode=pl.Buffered(1))
    coded = pl.BlockSpec((1, width + PAD, rows), lambda q: (q, 0, 0))
    all_coded = pl.BlockSpec((groups, width + PAD, rows), lambda q: (0, 0, 0), pipeline_mode=pl.Buffered(1))
    tile_spec = pl.BlockSpec((per * fill * blk, blk), lambda q: (q, 0))
    codes_shape = jax.ShapeDtypeStruct((groups, width + PAD, rows), i16)
    row_shape = jax.ShapeDtypeStruct((rows, strings), f32)
    row_halves = pltpu.VMEM((nblk, 2 * rows, blk), jnp.bfloat16)
    col_halves = pltpu.VMEM((nblk, 2 * width, blk), jnp.bfloat16)
    work = 2 * 2 * rows * strings * fill * blk
    size = 4 * rows * strings

    def exchange(value, late=None):
        have, bit = [value], roots // 2
        while bit:
            pairs = [(r, r ^ bit) for r in range(roots)]
            have = have + [lax.ppermute(h, "root", pairs) for h in have]
            if late is not None:
                have = list(lax.optimization_barrier(tuple(have) + (late,)))[:-1]
                late = None
            bit //= 2
        return have

    masks, bit = [0], roots // 2
    while bit:
        masks = masks + [m ^ bit for m in masks]
        bit //= 2
    far = jnp.bitwise_xor(root, jnp.array(masks, jnp.int32))
    weights = rotation[root][far].reshape(1, -1)
    far = far.reshape(1, -1)

    ring = list(range(0, groups, 2)) + list(range(1, groups, 2))[::-1]
    spot = jnp.array([ring.index(c) for c in range(groups)], jnp.int32)[lax.axis_index("col")]
    share = blk // roots
    mine = string_blocks.reshape(-1, blk, blk)
    mine = lax.dynamic_slice_in_dim(mine, root * share, share, 1)
    shards, owners, forth, back = [], [0], mine, mine
    started = start, diagonal
    for hop in range(1, groups // 2 + 1):
        both = 2 * hop < groups
        for way in (1, -1) if both else (1,):
            pairs = [(ring[s], ring[(s + way) % groups]) for s in range(groups)]
            moved = lax.ppermute(forth if way == 1 else back, "col", pairs)
            forth, back = (moved, back) if way == 1 else (forth, moved)
            shards += exchange(moved)
            owners += [-way * hop] * roots
        if hop == 1:
            started = lax.optimization_barrier((start, diagonal, forth, back))[:2]
    place = jnp.array(ring, jnp.int32)[(spot + jnp.array(owners, jnp.int32)) % groups]
    place = jnp.stack([place, jnp.concatenate([far[0, :1]] + [far[0]] * (groups - 1))])

    slab = width // roots
    height = width + PAD + slab
    tv = call(
        pack_kernel,
        groups,
        [smem(), piece, piece],
        pl.BlockSpec((1, height, rows), lambda q: (q, 0, 0)),
        jax.ShapeDtypeStruct((groups, height, rows), i16),
        [pltpu.VMEM((width, rows), f32)],
        0,
        size * 3,
    )(far, *started)
    tv = swap(lax.optimization_barrier((tv, forth, back))[0])

    once = pl.Buffered(1)
    shard_spec = pl.BlockSpec(mine.shape, lambda q: (0, 0, 0), pipeline_mode=once)
    w, tu, tiles = call(
        functools.partial(right_first_kernel, dims),
        groups,
        [smem(), smem(), smem(), whole, piece]
        + [pl.BlockSpec(string_blocks.shape, lambda q: (0, 0), pipeline_mode=once)]
        + [shard_spec] * len(shards),
        [piece, coded, tile_spec],
        [
            row_shape,
            codes_shape,
            jax.ShapeDtypeStruct((nblk * fill * blk, blk), string_blocks.dtype),
        ],
        [
            row_halves,
            pltpu.VMEM((width, rows), f32),
            pltpu.VMEM((nblk * fill * blk, blk), string_blocks.dtype),
        ],
        work,
        size * 6,
    )(block_cols, energy, place, start, diagonal, string_blocks, *shards)
    tu = swap(tu)

    base = call(
        functools.partial(right_second_kernel, dims),
        groups,
        [smem(), smem(), whole, piece, piece, tile_spec],
        piece,
        row_shape,
        [row_halves],
        work,
        size * 5,
    )(block_cols, energy, w, start, diagonal, tiles)

    y = call(
        functools.partial(left_first_kernel, dims),
        groups,
        [smem(), all_coded, tile_spec],
        pl.BlockSpec((width, width), lambda q: (0, q)),
        jax.ShapeDtypeStruct((width, strings), f32),
        [col_halves],
        work,
        size * 3,
    )(block_cols, tv, tiles)

    slabs = exchange(tv[:, width + PAD :], y)
    part = width // chunks
    chunk_coded = pl.BlockSpec((1, rows + PAD, part), lambda q: (q, 0, 0))
    turned = []
    for k in range(chunks):
        z = call(
            functools.partial(left_second_kernel, dims, k),
            groups,
            [
                smem(),
                smem(),
                smem(),
                pl.BlockSpec((groups, part, rows), lambda q, k=k: (0, k, 0), pipeline_mode=once),
                pl.BlockSpec((groups, PAD, rows), lambda q: (0, width // PAD, 0), pipeline_mode=once),
                pl.BlockSpec((part, strings), lambda q, k=k: (k, 0), pipeline_mode=once),
                tile_spec,
            ]
            + [pl.BlockSpec((1, slab, rows), lambda q: (q, 0, 0))] * roots
            + [pl.BlockSpec(memory_space=pl.ANY)],
            chunk_coded,
            jax.ShapeDtypeStruct((groups, rows + PAD, part), i16),
            [pltpu.VMEM((nblk, 2 * part, blk), jnp.bfloat16), pltpu.VMEM((width, rows), f32)],
            work // chunks,
            size * 4 // chunks,
        )(block_cols, energy, far, tu, tu, y, tiles, *slabs, base)
        turned.append(z)

    seconds = []
    for k in range(chunks):
        slot = pl.BlockSpec((rows, part), lambda q, k=k: (0, q * chunks + k))
        second = call(
            second_kernel,
            groups,
            [chunk_coded, slot],
            chunk_coded,
            jax.ShapeDtypeStruct((groups, rows + PAD, part), i16),
            [],
            0,
            size * 2 // chunks,
        )(swap(turned[k]), base)
        seconds.append(second)
    out = []
    for k in range(chunks):
        late = seconds[-1] if k < chunks - 1 else out[0] if out else None
        slot = pl.BlockSpec((1, rows, part), lambda q, k=k: (0, 0, q * chunks + k))
        out = [
            call(
                functools.partial(rotate_kernel, len(out)),
                groups,
                [smem()] + [pl.BlockSpec(memory_space=pl.ANY)] * len(out) + [chunk_coded] * roots,
                slot,
                jax.ShapeDtypeStruct((1, rows, strings), f32),
                [],
                0,
                size * 3 // chunks,
                {1: 0} if out else {},
            )(weights, *out, *exchange(seconds[k], late))
        ]
    return out[0]


def plain_blocks(matrix, operator_blocks, block_cols):
    height, breadth = matrix.shape
    nblocks, filled = block_cols.shape
    blocksize = breadth // nblocks
    grouped = matrix.reshape(height, nblocks, blocksize)
    picked = jnp.take(grouped, block_cols, axis=1)
    tiles = operator_blocks.reshape(nblocks, filled, blocksize, blocksize).astype(jnp.float32)
    result = jnp.einsum("rifk,ifjk->rij", picked, tiles, precision=lax.Precision.HIGHEST)
    return result.reshape(height, breadth)


def plain_swap(matrix):
    height, breadth = matrix.shape
    pieces = matrix.reshape(height, breadth // height, height).transpose(1, 2, 0)
    moved = lax.all_to_all(pieces, "col", split_axis=0, concat_axis=0, tiled=True)
    return moved.transpose(1, 0, 2).reshape(height, breadth)


def plain_shards(coeffs, diagonal, shift, rotation, string_blocks, block_cols):
    start = coeffs[0]
    energy = shift[0]
    operator_blocks = lax.all_gather(string_blocks, "col", axis=0, tiled=True)

    def sigma(vector):
        beta = plain_swap(plain_blocks(plain_swap(vector), operator_blocks, block_cols))
        return plain_blocks(vector, operator_blocks, block_cols) + beta + diagonal * vector

    first = 0.5 * (sigma(start) - energy * start)
    second = sigma(first) - energy * first - start
    weights = lax.dynamic_index_in_dim(rotation, lax.axis_index("root"), 1, keepdims=False)
    terms = weights[:, None, None] * second[None]
    return lax.psum_scatter(terms, "root", scatter_dimension=0, tiled=True)


def solution(mesh):
    roots, groups = mesh.shape["root"], mesh.shape["col"]

    def shards(coeffs, diagonal, shift, rotation, string_blocks, block_cols):
        rows, strings = coeffs.shape[1:]
        blk = strings // block_cols.shape[0]
        width = strings // groups
        regular = blk % LANES == 0 and width % blk == 0 and rows == width
        regular = regular and roots & (roots - 1) == 0 and width % (16 * roots) == 0
        regular = regular and groups % 2 == 0 and blk % (16 * roots) == 0
        args = (coeffs, diagonal, shift, rotation, string_blocks, block_cols)
        if regular:
            return blocked_shards((roots, groups), *args)
        return plain_shards(*args)

    return jax.shard_map(
        shards,
        mesh=mesh,
        in_specs=(P("root", "col", None), P("col", None), P("root"), P(), P("col", None), P()),
        out_specs=P("root", "col", None),
        check_vma=False,
    )
```

```python
import functools

import jax
import jax.numpy as jnp
from jax import lax
from jax.experimental import pallas as pl
from jax.experimental.pallas import tpu as pltpu
from jax.sharding import PartitionSpec as P

LANES = 128
PAD = 16
TOP = 32764.0
LIMIT = 56 * 1024 * 1024


def scale_of(mantissa, exponent):
    return mantissa * jnp.exp2(exponent - 7.0) * (1.0 / TOP)


def encode(piece):
    width = piece.shape[1]
    top = jnp.maximum(jnp.max(jnp.abs(piece), axis=0, keepdims=True), 1e-25)
    exponent = jnp.floor(jnp.log2(top))
    mantissa = jnp.floor(top * jnp.exp2(7.0 - exponent)) + 1.0
    codes = jnp.floor(piece * (1.0 / scale_of(mantissa, exponent)) + 0.5)
    codes = codes.astype(jnp.int32).astype(jnp.int16)
    row = lax.broadcasted_iota(jnp.int32, (PAD, width), 0)
    tail = jnp.where(row == 0, mantissa, jnp.where(row == 1, exponent, 0.0))
    return codes, tail.astype(jnp.int32).astype(jnp.int16)


def put(ref, index, piece):
    height = piece.shape[0]
    codes, tail = encode(piece)
    ref[index, pl.ds(0, height), :] = codes
    ref[index, pl.ds(height, PAD), :] = tail


def decode(codes, tail):
    tail = tail.astype(jnp.int32).astype(jnp.float32)
    return codes.astype(jnp.int32).astype(jnp.float32) * scale_of(tail[0:1], tail[1:2])


def take(ref, index):
    height = ref.shape[1] - PAD
    return decode(ref[index, pl.ds(0, height), :], ref[index, pl.ds(height, PAD), :])


def split_into(halves, block, value):
    rows = value.shape[0]
    high = value.astype(jnp.bfloat16)
    halves[block, pl.ds(0, rows), :] = high
    low = value - high.astype(jnp.float32)
    halves[block, pl.ds(rows, rows), :] = low.astype(jnp.bfloat16)


def apply_row(halves, tiles, place, cols, block, fill, blk):
    rows = halves.shape[1] // 2
    total = jnp.zeros((2 * rows, blk), jnp.float32)
    for first in range(0, fill, 2):
        terms = range(first, min(first + 2, fill))
        left = [halves[cols[block, f]] for f in terms]
        right = tiles[pl.ds((place * fill + first) * blk, len(left) * blk), :]
        total += lax.dot_general(
            jnp.concatenate(left, axis=1),
            right,
            (((1,), (0,)), ((), ())),
            preferred_element_type=jnp.float32,
        )
    return total[:rows] + total[rows:]


def pack_kernel(cols, place, v_ref, d_ref, out_ref, turned):
    del cols
    put(out_ref, 0, v_ref[...].T)
    turned[...] = d_ref[...].T
    width, rows = turned.shape
    slab = out_ref.shape[1] - width - PAD
    here = turned[pl.ds(pl.multiple_of(place[1, 0] * slab, slab), slab), :]
    codes = jnp.floor(here * 32767.0 + 0.5)
    out_ref[0, pl.ds(width + PAD, slab), :] = codes.astype(jnp.int32).astype(jnp.int16)


def right_first_kernel(dims, cols, shift, place, v_ref, d_ref, own, *rest):
    nblk, fill, blk, per = dims
    shards, (w_ref, u_ref, tiles_ref, halves, turned, tiles) = rest[:-6], rest[-6:]
    step = pl.program_id(0)
    size = own.shape[0]

    @pl.when(step == 0)
    def _():
        for b in range(nblk):
            split_into(halves, b, v_ref[:, b * blk : (b + 1) * blk])
        tiles[pl.ds(pl.multiple_of(place[0, 0] * size, size), size), :] = own[...]

        @pl.loop(0, size // blk)
        def _(b):
            for k, shard in enumerate(shards):
                share = shard.shape[1]
                base = place[0, 1 + k] * size + place[1, 1 + k] * share
                at = pl.multiple_of(base + b * blk, share)
                tiles[pl.ds(at, share), :] = shard[b]

    here_tiles = tiles.at[pl.ds(pl.multiple_of(step * size, size), size), :]
    tiles_ref[...] = here_tiles[...]
    for t in range(per):
        lanes = slice(t * blk, (t + 1) * blk)
        block = step * per + t
        here = v_ref[:, pl.ds(pl.multiple_of(block * blk, blk), blk)]
        moved = apply_row(halves, here_tiles, t, cols, block, fill, blk)
        whole = moved + (d_ref[:, lanes] - shift[0, 0]) * here
        w_ref[:, lanes] = whole
        turned[lanes, :] = (moved + whole).T
    put(u_ref, 0, turned[...])


def left_first_kernel(dims, cols, tv_ref, tiles, y_ref, halves):
    nblk, fill, blk, per = dims
    step = pl.program_id(0)

    @pl.when(step == 0)
    def _():
        for p in range(nblk // per):
            value = take(tv_ref, p)
            for t in range(per):
                split_into(halves, p * per + t, value[:, t * blk : (t + 1) * blk])

    for t in range(per):
        y_ref[:, t * blk : (t + 1) * blk] = apply_row(halves, tiles, t, cols, step * per + t, fill, blk)


def right_second_kernel(dims, cols, shift, w_ref, v_ref, d_ref, tiles, *rest):
    nblk, fill, blk, per = dims
    outs, halves = rest[:-1], rest[-1]
    step = pl.program_id(0)

    @pl.when(step == 0)
    def _():
        for b in range(nblk):
            split_into(halves, b, w_ref[:, b * blk : (b + 1) * blk])

    for t in range(per):
        lanes = slice(t * blk, (t + 1) * blk)
        block = step * per + t
        here = w_ref[:, pl.ds(pl.multiple_of(block * blk, blk), blk)]
        moved = apply_row(halves, tiles, t, cols, block, fill, blk)
        outs[t][...] = 0.5 * (moved + (d_ref[:, lanes] - shift[0, 0]) * here) - v_ref[:, lanes]


def left_second_kernel(dims, chunk, cols, shift, far, tu_ref, tail_ref, y_ref, tiles, *rest):
    nblk, fill, blk, per = dims
    slabs, (_, out, halves, turned) = rest[:-4], rest[-4:]
    step = pl.program_id(0)
    part = y_ref.shape[0]

    @pl.when(step == 0)
    def _():
        for p in range(nblk // per):
            value = decode(tu_ref[p], tail_ref[p]) + y_ref[:, p * per * blk : (p + 1) * per * blk]
            for t in range(per):
                split_into(halves, p * per + t, value[:, t * blk : (t + 1) * blk])

    for m, slab in enumerate(slabs):
        height = slab.shape[1]
        at = pl.multiple_of(far[0, m] * height, height)
        turned[pl.ds(at, height), :] = slab[0].astype(jnp.int32).astype(jnp.float32)
    done = []
    for t in range(per):
        block = step * per + t
        here = y_ref[:, pl.ds(pl.multiple_of(block * blk, blk), blk)]
        diagonal = turned[chunk * part : (chunk + 1) * part, t * blk : (t + 1) * blk]
        moved = apply_row(halves, tiles, t, cols, block, fill, blk)
        done.append((0.5 * (moved + (diagonal * (1.0 / 32767.0) - shift[0, 0]) * here)).T)
    put(out, 0, jnp.concatenate(done, axis=0))


def second_kernel(weights, z_ref, p_ref, out_ref):
    del weights
    part = z_ref.shape[2]
    for n in range(z_ref.shape[0]):
        put(out_ref, n, take(z_ref, n) + p_ref[:, n * part : (n + 1) * part])


def rotate_kernel(aliased, weights, *refs):
    ins, out_ref = refs[aliased:-1], refs[-1]
    total = weights[0, 0] * take(ins[0], 0)
    for m in range(1, len(ins)):
        total += weights[0, m] * take(ins[m], 0)
    out_ref[0] = total


def smem():
    return pl.BlockSpec(memory_space=pltpu.SMEM)


def call(kernel, grid, in_specs, out_specs, out_shape, scratch, flops, moved, aliases={}):
    return pl.pallas_call(
        kernel,
        grid=(grid,),
        in_specs=in_specs,
        out_specs=out_specs,
        out_shape=out_shape,
        scratch_shapes=scratch,
        input_output_aliases=aliases,
        compiler_params=pltpu.CompilerParams(
            dimension_semantics=("arbitrary",), vmem_limit_bytes=LIMIT
        ),
        cost_estimate=pl.CostEstimate(flops=flops, bytes_accessed=moved, transcendentals=0),
    )


def blocked_shards(sizes, coeffs, diagonal, shift, rotation, string_blocks, block_cols):
    roots, groups = sizes
    start = coeffs[0]
    rows, strings = start.shape
    nblk, fill = block_cols.shape
    blk = strings // nblk
    width = strings // groups
    per = width // blk
    chunks = per
    dims = (nblk, fill, blk, per)
    energy = shift.reshape(1, 1)
    root = lax.axis_index("root")
    f32, i16 = jnp.float32, jnp.int16

    def swap(pieces):
        return lax.all_to_all(pieces, "col", split_axis=0, concat_axis=0, tiled=True)

    piece = pl.BlockSpec((rows, width), lambda q: (0, q))
    whole = pl.BlockSpec((rows, strings), lambda q: (0, 0), pipeline_mode=pl.Buffered(1))
    coded = pl.BlockSpec((1, width + PAD, rows), lambda q: (q, 0, 0))
    all_coded = pl.BlockSpec((groups, width + PAD, rows), lambda q: (0, 0, 0), pipeline_mode=pl.Buffered(1))
    tile_spec = pl.BlockSpec((per * fill * blk, blk), lambda q: (q, 0))
    codes_shape = jax.ShapeDtypeStruct((groups, width + PAD, rows), i16)
    row_shape = jax.ShapeDtypeStruct((rows, strings), f32)
    row_halves = pltpu.VMEM((nblk, 2 * rows, blk), jnp.bfloat16)
    col_halves = pltpu.VMEM((nblk, 2 * width, blk), jnp.bfloat16)
    work = 2 * 2 * rows * strings * fill * blk
    size = 4 * rows * strings

    def exchange(value, late=None):
        have, bit = [value], roots // 2
        while bit:
            pairs = [(r, r ^ bit) for r in range(roots)]
            have = have + [lax.ppermute(h, "root", pairs) for h in have]
            if late is not None:
                have = list(lax.optimization_barrier(tuple(have) + (late,)))[:-1]
                late = None
            bit //= 2
        return have

    masks, bit = [0], roots // 2
    while bit:
        masks = masks + [m ^ bit for m in masks]
        bit //= 2
    far = jnp.bitwise_xor(root, jnp.array(masks, jnp.int32))
    weights = rotation[root][far].reshape(1, -1)
    far = far.reshape(1, -1)

    ring = list(range(0, groups, 2)) + list(range(1, groups, 2))[::-1]
    spot = jnp.array([ring.index(c) for c in range(groups)], jnp.int32)[lax.axis_index("col")]
    share = blk // roots
    owners = [0]
    for hop in range(1, groups // 2 + 1):
        owners += [-hop] * roots + ([hop] * roots if 2 * hop < groups else [])
    place = jnp.array(ring, jnp.int32)[(spot + jnp.array(owners, jnp.int32)) % groups]
    place = jnp.stack([place, jnp.concatenate([far[0, :1]] + [far[0]] * (groups - 1))])

    slab = width // roots
    height = width + PAD + slab

    def pack(start, diagonal):
        return call(
            pack_kernel,
            groups,
            [smem(), smem(), piece, piece],
            pl.BlockSpec((1, height, rows), lambda q: (q, 0, 0)),
            jax.ShapeDtypeStruct((groups, height, rows), i16),
            [pltpu.VMEM((width, rows), f32)],
            0,
            size * 3,
        )(block_cols, place, start, diagonal)

    own = jnp.swapaxes(string_blocks.reshape(-1, blk, blk), 1, 2)
    mine = lax.dynamic_slice_in_dim(own, root * share, share, 1)
    shards, crossed, tv, forth, back = [], [], None, mine, mine
    for hop in range(1, groups // 2 + 1):
        if hop == 3:
            forth, back = lax.optimization_barrier((forth, back, tv, *crossed[:2]))[:2]
        for way in (1, -1) if 2 * hop < groups else (1,):
            pairs = [(ring[s], ring[(s + way) % groups]) for s in range(groups)]
            moved = lax.ppermute(forth if way == 1 else back, "col", pairs)
            forth, back = (moved, back) if way == 1 else (forth, moved)
            shards += exchange(moved)
            crossed.append(shards[1 - roots])
        if hop == 1:
            tv = pack(*lax.optimization_barrier((start, diagonal, forth, back))[:2])
    tv = swap(lax.optimization_barrier((tv, forth, back, *crossed[2:4]))[0])
    own = own.reshape(string_blocks.shape)

    once = pl.Buffered(1)
    shard_spec = pl.BlockSpec(mine.shape, lambda q: (0, 0, 0), pipeline_mode=once)
    w, tu, tiles = call(
        functools.partial(right_first_kernel, dims),
        groups,
        [smem(), smem(), smem(), whole, piece]
        + [pl.BlockSpec(string_blocks.shape, lambda q: (0, 0), pipeline_mode=once)]
        + [shard_spec] * len(shards),
        [piece, coded, tile_spec],
        [
            row_shape,
            codes_shape,
            jax.ShapeDtypeStruct((nblk * fill * blk, blk), string_blocks.dtype),
        ],
        [
            row_halves,
            pltpu.VMEM((width, rows), f32),
            pltpu.VMEM((nblk * fill * blk, blk), string_blocks.dtype),
        ],
        work,
        size * 6,
    )(block_cols, energy, place, start, diagonal, own, *shards)
    tu = swap(tu)

    base = call(
        functools.partial(right_second_kernel, dims),
        groups,
        [smem(), smem(), whole, piece, piece, tile_spec],
        [pl.BlockSpec((rows, blk), lambda q: (0, q))] * chunks,
        [jax.ShapeDtypeStruct((rows, groups * blk), f32)] * chunks,
        [row_halves],
        work,
        size * 5,
    )(block_cols, energy, w, start, diagonal, tiles)

    y = call(
        functools.partial(left_first_kernel, dims),
        groups,
        [smem(), all_coded, tile_spec],
        pl.BlockSpec((width, width), lambda q: (0, q)),
        jax.ShapeDtypeStruct((width, strings), f32),
        [col_halves],
        work,
        size * 3,
    )(block_cols, tv, tiles)

    slabs = exchange(tv[:, width + PAD :], y)
    part = width // chunks
    chunk_coded = pl.BlockSpec((1, rows + PAD, part), lambda q: (q, 0, 0))
    many = 4 if groups % 4 == 0 else 1
    many_coded = pl.BlockSpec((many, rows + PAD, part), lambda q: (q, 0, 0))
    seconds = []
    for k in range(chunks):
        z = call(
            functools.partial(left_second_kernel, dims, k),
            groups,
            [
                smem(),
                smem(),
                smem(),
                pl.BlockSpec((groups, part, rows), lambda q, k=k: (0, k, 0), pipeline_mode=once),
                pl.BlockSpec((groups, PAD, rows), lambda q: (0, width // PAD, 0), pipeline_mode=once),
                pl.BlockSpec((part, strings), lambda q, k=k: (k, 0), pipeline_mode=once),
                tile_spec,
            ]
            + [pl.BlockSpec((1, slab, rows), lambda q: (q, 0, 0))] * roots
            + [pl.BlockSpec(memory_space=pl.ANY)],
            chunk_coded,
            jax.ShapeDtypeStruct((groups, rows + PAD, part), i16),
            [pltpu.VMEM((nblk, 2 * part, blk), jnp.bfloat16), pltpu.VMEM((width, rows), f32)],
            work // chunks,
            size * 4 // chunks,
        )(block_cols, energy, far, tu, tu, y, tiles, *slabs, base[0] if k < 2 else seconds[k - 2])
        second = call(
            second_kernel,
            groups // many,
            [smem(), many_coded, pl.BlockSpec((rows, many * part), lambda q: (0, q))],
            many_coded,
            jax.ShapeDtypeStruct((groups, rows + PAD, part), i16),
            [],
            0,
            size * 2 // chunks,
        )(weights, swap(z), base[k])
        seconds.append(second)
    out = []
    for k in range(chunks):
        late = seconds[k + 1] if k < chunks - 1 else out[0] if out else None
        slot = pl.BlockSpec((1, rows, part), lambda q, k=k: (0, 0, q * chunks + k))
        out = [
            call(
                functools.partial(rotate_kernel, len(out)),
                groups,
                [smem()] + [pl.BlockSpec(memory_space=pl.ANY)] * len(out) + [chunk_coded] * roots,
                slot,
                jax.ShapeDtypeStruct((1, rows, strings), f32),
                [],
                0,
                size * 3 // chunks,
                {1: 0} if out else {},
            )(weights, *out, *exchange(seconds[k], late))
        ]
    return out[0]


def plain_blocks(matrix, operator_blocks, block_cols):
    height, breadth = matrix.shape
    nblocks, filled = block_cols.shape
    blocksize = breadth // nblocks
    grouped = matrix.reshape(height, nblocks, blocksize)
    picked = jnp.take(grouped, block_cols, axis=1)
    tiles = operator_blocks.reshape(nblocks, filled, blocksize, blocksize).astype(jnp.float32)
    result = jnp.einsum("rifk,ifjk->rij", picked, tiles, precision=lax.Precision.HIGHEST)
    return result.reshape(height, breadth)


def plain_swap(matrix):
    height, breadth = matrix.shape
    pieces = matrix.reshape(height, breadth // height, height).transpose(1, 2, 0)
    moved = lax.all_to_all(pieces, "col", split_axis=0, concat_axis=0, tiled=True)
    return moved.transpose(1, 0, 2).reshape(height, breadth)


def plain_shards(coeffs, diagonal, shift, rotation, string_blocks, block_cols):
    start = coeffs[0]
    energy = shift[0]
    operator_blocks = lax.all_gather(string_blocks, "col", axis=0, tiled=True)

    def sigma(vector):
        beta = plain_swap(plain_blocks(plain_swap(vector), operator_blocks, block_cols))
        return plain_blocks(vector, operator_blocks, block_cols) + beta + diagonal * vector

    first = 0.5 * (sigma(start) - energy * start)
    second = sigma(first) - energy * first - start
    weights = lax.dynamic_index_in_dim(rotation, lax.axis_index("root"), 1, keepdims=False)
    terms = weights[:, None, None] * second[None]
    return lax.psum_scatter(terms, "root", scatter_dimension=0, tiled=True)


def solution(mesh):
    roots, groups = mesh.shape["root"], mesh.shape["col"]

    def shards(coeffs, diagonal, shift, rotation, string_blocks, block_cols):
        rows, strings = coeffs.shape[1:]
        blk = strings // block_cols.shape[0]
        width = strings // groups
        regular = blk % LANES == 0 and width % blk == 0 and rows == width
        regular = regular and roots & (roots - 1) == 0 and width % (16 * roots) == 0
        regular = regular and groups % 2 == 0 and blk % (16 * roots) == 0
        args = (coeffs, diagonal, shift, rotation, string_blocks, block_cols)
        if regular:
            return blocked_shards((roots, groups), *args)
        return plain_shards(*args)

    return jax.shard_map(
        shards,
        mesh=mesh,
        in_specs=(P("root", "col", None), P("col", None), P("root"), P(), P("col", None), P()),
        out_specs=P("root", "col", None),
        check_vma=False,
    )
```

```python
import functools

import jax
import jax.numpy as jnp
from jax import lax
from jax.experimental import pallas as pl
from jax.experimental.pallas import tpu as pltpu
from jax.sharding import PartitionSpec as P

LANES = 128
PAD = 16
TOP = 32764.0
LIMIT = 56 * 1024 * 1024


def scale_of(mantissa, exponent):
    return mantissa * jnp.exp2(exponent - 7.0) * (1.0 / TOP)


def encode(piece):
    width = piece.shape[1]
    top = jnp.maximum(jnp.max(jnp.abs(piece), axis=0, keepdims=True), 1e-25)
    exponent = jnp.floor(jnp.log2(top))
    mantissa = jnp.floor(top * jnp.exp2(7.0 - exponent)) + 1.0
    codes = jnp.floor(piece * (1.0 / scale_of(mantissa, exponent)) + 0.5)
    codes = codes.astype(jnp.int32).astype(jnp.int16)
    row = lax.broadcasted_iota(jnp.int32, (PAD, width), 0)
    tail = jnp.where(row == 0, mantissa, jnp.where(row == 1, exponent, 0.0))
    return codes, tail.astype(jnp.int32).astype(jnp.int16)


def put(ref, index, piece):
    height = piece.shape[0]
    codes, tail = encode(piece)
    ref[index, pl.ds(0, height), :] = codes
    ref[index, pl.ds(height, PAD), :] = tail


def decode(codes, tail):
    tail = tail.astype(jnp.int32).astype(jnp.float32)
    return codes.astype(jnp.int32).astype(jnp.float32) * scale_of(tail[0:1], tail[1:2])


def take(ref, index):
    height = ref.shape[1] - PAD
    return decode(ref[index, pl.ds(0, height), :], ref[index, pl.ds(height, PAD), :])


def split_into(halves, block, value):
    rows = value.shape[0]
    high = value.astype(jnp.bfloat16)
    halves[block, pl.ds(0, rows), :] = high
    low = value - high.astype(jnp.float32)
    halves[block, pl.ds(rows, rows), :] = low.astype(jnp.bfloat16)


def apply_row(halves, tiles, place, cols, block, fill, blk):
    rows = halves.shape[1] // 2
    total = jnp.zeros((2 * rows, blk), jnp.float32)
    for first in range(0, fill, 2):
        terms = range(first, min(first + 2, fill))
        left = [halves[cols[block, f]] for f in terms]
        right = tiles[pl.ds((place * fill + first) * blk, len(left) * blk), :]
        total += lax.dot_general(
            jnp.concatenate(left, axis=1),
            right,
            (((1,), (0,)), ((), ())),
            preferred_element_type=jnp.float32,
        )
    return total[:rows] + total[rows:]


def pack_kernel(here, v_ref, d_ref, out_ref, turned):
    put(out_ref, 0, v_ref[...].T)
    turned[...] = d_ref[...].T
    width, rows = turned.shape
    slab = out_ref.shape[1] - width - PAD
    mine = turned[pl.ds(pl.multiple_of(here[0, 0] * slab, slab), slab), :]
    codes = jnp.floor(mine * 32767.0 + 0.5)
    out_ref[0, pl.ds(width + PAD, slab), :] = codes.astype(jnp.int32).astype(jnp.int16)


def ring_at(spot, groups):
    return jnp.where(spot * 2 < groups, 2 * spot, 2 * (groups - 1 - spot) + 1)


def ring_spot(col, groups):
    half = jnp.right_shift(col, 1)
    return jnp.where(jnp.bitwise_and(col, 1) == 0, half, groups - 1 - half)


def right_first_kernel(dims, groups, owners, masks, cols, shift, place, v_ref, d_ref, own, *rest):
    nblk, fill, blk, per = dims
    shards, (w_ref, u_ref, tiles_ref, halves, turned, tiles) = rest[:-6], rest[-6:]
    step = pl.program_id(0)
    size = own.shape[0]

    @pl.when(step == 0)
    def _():
        for b in range(nblk):
            split_into(halves, b, v_ref[:, b * blk : (b + 1) * blk])
        root, col = place[0, 0], place[0, 1]
        tiles[pl.ds(pl.multiple_of(col * size, size), size), :] = own[...]
        spot = ring_spot(col, groups)
        bases = [
            ring_at(lax.rem(spot + (owner + groups), groups), groups) * size
            + jnp.bitwise_xor(root, mask) * shards[0].shape[1]
            for owner in owners
            for mask in masks
        ]

        @pl.loop(0, size // blk)
        def _(b):
            for k, shard in enumerate(shards):
                share = shard.shape[1]
                at = pl.multiple_of(bases[k] + b * blk, share)
                tiles[pl.ds(at, share), :] = shard[b]

    here_tiles = tiles.at[pl.ds(pl.multiple_of(step * size, size), size), :]
    tiles_ref[...] = here_tiles[...]
    for t in range(per):
        lanes = slice(t * blk, (t + 1) * blk)
        block = step * per + t
        here = v_ref[:, pl.ds(pl.multiple_of(block * blk, blk), blk)]
        moved = apply_row(halves, here_tiles, t, cols, block, fill, blk)
        whole = moved + (d_ref[:, lanes] - shift[0, 0]) * here
        w_ref[:, lanes] = whole
        turned[lanes, :] = (moved + whole).T
    put(u_ref, 0, turned[...])


def left_first_kernel(dims, cols, tv_ref, tiles, y_ref, halves):
    nblk, fill, blk, per = dims
    step = pl.program_id(0)

    @pl.when(step == 0)
    def _():
        for p in range(nblk // per):
            value = take(tv_ref, p)
            for t in range(per):
                split_into(halves, p * per + t, value[:, t * blk : (t + 1) * blk])

    for t in range(per):
        y_ref[:, t * blk : (t + 1) * blk] = apply_row(halves, tiles, t, cols, step * per + t, fill, blk)


def right_second_kernel(dims, cols, shift, w_ref, v_ref, d_ref, tiles, *rest):
    nblk, fill, blk, per = dims
    outs, halves = rest[:-1], rest[-1]
    step = pl.program_id(0)

    @pl.when(step == 0)
    def _():
        for b in range(nblk):
            split_into(halves, b, w_ref[:, b * blk : (b + 1) * blk])

    for t in range(per):
        lanes = slice(t * blk, (t + 1) * blk)
        block = step * per + t
        here = w_ref[:, pl.ds(pl.multiple_of(block * blk, blk), blk)]
        moved = apply_row(halves, tiles, t, cols, block, fill, blk)
        outs[t][...] = 0.5 * (moved + (d_ref[:, lanes] - shift[0, 0]) * here) - v_ref[:, lanes]


def left_second_kernel(dims, chunk, masks, cols, shift, place, tu_ref, tail_ref, y_ref, tiles, *rest):
    nblk, fill, blk, per = dims
    slabs, (_, out, halves, turned) = rest[:-4], rest[-4:]
    step = pl.program_id(0)
    part = y_ref.shape[0]

    @pl.when(step == 0)
    def _():
        for p in range(nblk // per):
            value = decode(tu_ref[p], tail_ref[p]) + y_ref[:, p * per * blk : (p + 1) * per * blk]
            for t in range(per):
                split_into(halves, p * per + t, value[:, t * blk : (t + 1) * blk])

    for m, slab in enumerate(slabs):
        height = slab.shape[1]
        at = pl.multiple_of(jnp.bitwise_xor(place[0, 0], masks[m]) * height, height)
        turned[pl.ds(at, height), :] = slab[0].astype(jnp.int32).astype(jnp.float32)
    done = []
    for t in range(per):
        block = step * per + t
        here = y_ref[:, pl.ds(pl.multiple_of(block * blk, blk), blk)]
        diagonal = turned[chunk * part : (chunk + 1) * part, t * blk : (t + 1) * blk]
        moved = apply_row(halves, tiles, t, cols, block, fill, blk)
        done.append((0.5 * (moved + (diagonal * (1.0 / 32767.0) - shift[0, 0]) * here)).T)
    put(out, 0, jnp.concatenate(done, axis=0))


def second_kernel(weights, z_ref, p_ref, out_ref):
    del weights
    part = z_ref.shape[2]
    for n in range(z_ref.shape[0]):
        put(out_ref, n, take(z_ref, n) + p_ref[:, n * part : (n + 1) * part])


def rotate_kernel(aliased, weights, *refs):
    ins, out_ref = refs[aliased:-1], refs[-1]
    total = weights[0, 0] * take(ins[0], 0)
    for m in range(1, len(ins)):
        total += weights[0, m] * take(ins[m], 0)
    out_ref[0] = total


def smem():
    return pl.BlockSpec(memory_space=pltpu.SMEM)


def call(kernel, grid, in_specs, out_specs, out_shape, scratch, flops, moved, aliases={}):
    return pl.pallas_call(
        kernel,
        grid=(grid,),
        in_specs=in_specs,
        out_specs=out_specs,
        out_shape=out_shape,
        scratch_shapes=scratch,
        input_output_aliases=aliases,
        compiler_params=pltpu.CompilerParams(
            dimension_semantics=("arbitrary",), vmem_limit_bytes=LIMIT
        ),
        cost_estimate=pl.CostEstimate(flops=flops, bytes_accessed=moved, transcendentals=0),
    )


def blocked_shards(sizes, coeffs, diagonal, shift, rotation, string_blocks, block_cols):
    roots, groups = sizes
    start = coeffs[0]
    rows, strings = start.shape
    nblk, fill = block_cols.shape
    blk = strings // nblk
    width = strings // groups
    per = width // blk
    chunks = per
    dims = (nblk, fill, blk, per)
    energy = shift.reshape(1, 1)
    root = lax.axis_index("root")
    f32, i16 = jnp.float32, jnp.int16

    def swap(pieces):
        return lax.all_to_all(pieces, "col", split_axis=0, concat_axis=0, tiled=True)

    piece = pl.BlockSpec((rows, width), lambda q: (0, q))
    whole = pl.BlockSpec((rows, strings), lambda q: (0, 0), pipeline_mode=pl.Buffered(1))
    coded = pl.BlockSpec((1, width + PAD, rows), lambda q: (q, 0, 0))
    all_coded = pl.BlockSpec((groups, width + PAD, rows), lambda q: (0, 0, 0), pipeline_mode=pl.Buffered(1))
    tile_spec = pl.BlockSpec((per * fill * blk, blk), lambda q: (q, 0))
    codes_shape = jax.ShapeDtypeStruct((groups, width + PAD, rows), i16)
    row_shape = jax.ShapeDtypeStruct((rows, strings), f32)
    row_halves = pltpu.VMEM((nblk, 2 * rows, blk), jnp.bfloat16)
    col_halves = pltpu.VMEM((nblk, 2 * width, blk), jnp.bfloat16)
    work = 2 * 2 * rows * strings * fill * blk
    size = 4 * rows * strings

    def exchange(value, late=None):
        have, bit = [value], roots // 2
        while bit:
            pairs = [(r, r ^ bit) for r in range(roots)]
            have = have + [lax.ppermute(h, "root", pairs) for h in have]
            if late is not None:
                have = list(lax.optimization_barrier(tuple(have) + (late,)))[:-1]
                late = None
            bit //= 2
        return have

    masks, bit = [0], roots // 2
    while bit:
        masks = masks + [m ^ bit for m in masks]
        bit //= 2
    far = jnp.bitwise_xor(root, jnp.array(masks, jnp.int32))
    weights = rotation[root][far].reshape(1, -1)
    place = jnp.stack([root, lax.axis_index("col")]).astype(jnp.int32).reshape(1, 2)

    ring = list(range(0, groups, 2)) + list(range(1, groups, 2))[::-1]
    share = blk // roots
    owners = []
    for hop in range(1, groups // 2 + 1):
        owners += [-hop, hop] if 2 * hop < groups else [-hop]

    slab = width // roots
    height = width + PAD + slab

    def pack(start, diagonal):
        return call(
            pack_kernel,
            groups,
            [smem(), piece, piece],
            pl.BlockSpec((1, height, rows), lambda q: (q, 0, 0)),
            jax.ShapeDtypeStruct((groups, height, rows), i16),
            [pltpu.VMEM((width, rows), f32)],
            0,
            size * 3,
        )(place, start, diagonal)

    own = jnp.swapaxes(string_blocks.reshape(-1, blk, blk), 1, 2)
    mine = lax.dynamic_slice_in_dim(own, root * share, share, 1)
    shards, crossed, tv, forth, back = [], [], None, mine, mine
    for hop in range(1, groups // 2 + 1):
        if hop == 3:
            forth, back = lax.optimization_barrier((forth, back, tv, *crossed[:2]))[:2]
        for way in (1, -1) if 2 * hop < groups else (1,):
            pairs = [(ring[s], ring[(s + way) % groups]) for s in range(groups)]
            moved = lax.ppermute(forth if way == 1 else back, "col", pairs)
            forth, back = (moved, back) if way == 1 else (forth, moved)
            shards += exchange(moved)
            crossed.append(shards[1 - roots])
        if hop == 1:
            tv = pack(*lax.optimization_barrier((start, diagonal, forth, back))[:2])
    tv = swap(lax.optimization_barrier((tv, forth, back))[0])
    own = own.reshape(string_blocks.shape)

    once = pl.Buffered(1)
    shard_spec = pl.BlockSpec(mine.shape, lambda q: (0, 0, 0), pipeline_mode=once)
    w, tu, tiles = call(
        functools.partial(right_first_kernel, dims, groups, owners, masks),
        groups,
        [smem(), smem(), smem(), whole, piece]
        + [pl.BlockSpec(string_blocks.shape, lambda q: (0, 0), pipeline_mode=once)]
        + [shard_spec] * len(shards),
        [piece, coded, tile_spec],
        [
            row_shape,
            codes_shape,
            jax.ShapeDtypeStruct((nblk * fill * blk, blk), string_blocks.dtype),
        ],
        [
            row_halves,
            pltpu.VMEM((width, rows), f32),
            pltpu.VMEM((nblk * fill * blk, blk), string_blocks.dtype),
        ],
        work,
        size * 6,
    )(block_cols, energy, place, start, diagonal, own, *shards)
    tu = swap(tu)

    base = call(
        functools.partial(right_second_kernel, dims),
        groups,
        [smem(), smem(), whole, piece, piece, tile_spec],
        [pl.BlockSpec((rows, blk), lambda q: (0, q))] * chunks,
        [jax.ShapeDtypeStruct((rows, groups * blk), f32)] * chunks,
        [row_halves],
        work,
        size * 5,
    )(block_cols, energy, w, start, diagonal, tiles)

    y = call(
        functools.partial(left_first_kernel, dims),
        groups,
        [smem(), all_coded, tile_spec],
        pl.BlockSpec((width, width), lambda q: (0, q)),
        jax.ShapeDtypeStruct((width, strings), f32),
        [col_halves],
        work,
        size * 3,
    )(block_cols, tv, tiles)

    slabs = exchange(tv[:, width + PAD :], y)
    part = width // chunks
    chunk_coded = pl.BlockSpec((1, rows + PAD, part), lambda q: (q, 0, 0))
    many = 4 if groups % 4 == 0 else 1
    many_coded = pl.BlockSpec((many, rows + PAD, part), lambda q: (q, 0, 0))
    seconds = []
    for k in range(chunks):
        z = call(
            functools.partial(left_second_kernel, dims, k, masks),
            groups,
            [
                smem(),
                smem(),
                smem(),
                pl.BlockSpec((groups, part, rows), lambda q, k=k: (0, k, 0), pipeline_mode=once),
                pl.BlockSpec((groups, PAD, rows), lambda q: (0, width // PAD, 0), pipeline_mode=once),
                pl.BlockSpec((part, strings), lambda q, k=k: (k, 0), pipeline_mode=once),
                tile_spec,
            ]
            + [pl.BlockSpec((1, slab, rows), lambda q: (q, 0, 0))] * roots
            + [pl.BlockSpec(memory_space=pl.ANY)],
            chunk_coded,
            jax.ShapeDtypeStruct((groups, rows + PAD, part), i16),
            [pltpu.VMEM((nblk, 2 * part, blk), jnp.bfloat16), pltpu.VMEM((width, rows), f32)],
            work // chunks if k < 2 else 1,
            size * 4 // chunks if k < 2 else 1,
        )(block_cols, energy, place, tu, tu, y, tiles, *slabs, base[0] if k < 2 else seconds[k - 2])
        second = call(
            second_kernel,
            groups // many,
            [smem(), many_coded, pl.BlockSpec((rows, many * part), lambda q: (0, q))],
            many_coded,
            jax.ShapeDtypeStruct((groups, rows + PAD, part), i16),
            [],
            0,
            1,
        )(weights, swap(z), base[k])
        seconds.append(second)
    out = []
    for k in range(chunks):
        late = seconds[k + 1] if k < chunks - 1 else out[0] if out else None
        slot = pl.BlockSpec((1, rows, part), lambda q, k=k: (0, 0, q * chunks + k))
        out = [
            call(
                functools.partial(rotate_kernel, len(out)),
                groups,
                [smem()] + [pl.BlockSpec(memory_space=pl.ANY)] * len(out) + [chunk_coded] * roots,
                slot,
                jax.ShapeDtypeStruct((1, rows, strings), f32),
                [],
                0,
                1,
                {1: 0} if out else {},
            )(weights, *out, *exchange(seconds[k], late))
        ]
    return out[0]


def plain_blocks(matrix, operator_blocks, block_cols):
    height, breadth = matrix.shape
    nblocks, filled = block_cols.shape
    blocksize = breadth // nblocks
    grouped = matrix.reshape(height, nblocks, blocksize)
    picked = jnp.take(grouped, block_cols, axis=1)
    tiles = operator_blocks.reshape(nblocks, filled, blocksize, blocksize).astype(jnp.float32)
    result = jnp.einsum("rifk,ifjk->rij", picked, tiles, precision=lax.Precision.HIGHEST)
    return result.reshape(height, breadth)


def plain_swap(matrix):
    height, breadth = matrix.shape
    pieces = matrix.reshape(height, breadth // height, height).transpose(1, 2, 0)
    moved = lax.all_to_all(pieces, "col", split_axis=0, concat_axis=0, tiled=True)
    return moved.transpose(1, 0, 2).reshape(height, breadth)


def plain_shards(coeffs, diagonal, shift, rotation, string_blocks, block_cols):
    start = coeffs[0]
    energy = shift[0]
    operator_blocks = lax.all_gather(string_blocks, "col", axis=0, tiled=True)

    def sigma(vector):
        beta = plain_swap(plain_blocks(plain_swap(vector), operator_blocks, block_cols))
        return plain_blocks(vector, operator_blocks, block_cols) + beta + diagonal * vector

    first = 0.5 * (sigma(start) - energy * start)
    second = sigma(first) - energy * first - start
    weights = lax.dynamic_index_in_dim(rotation, lax.axis_index("root"), 1, keepdims=False)
    terms = weights[:, None, None] * second[None]
    return lax.psum_scatter(terms, "root", scatter_dimension=0, tiled=True)


def solution(mesh):
    roots, groups = mesh.shape["root"], mesh.shape["col"]

    def shards(coeffs, diagonal, shift, rotation, string_blocks, block_cols):
        rows, strings = coeffs.shape[1:]
        blk = strings // block_cols.shape[0]
        width = strings // groups
        regular = blk % LANES == 0 and width % blk == 0 and rows == width
        regular = regular and roots & (roots - 1) == 0 and width % (16 * roots) == 0
        regular = regular and groups % 2 == 0 and blk % (16 * roots) == 0
        args = (coeffs, diagonal, shift, rotation, string_blocks, block_cols)
        if regular:
            return blocked_shards((roots, groups), *args)
        return plain_shards(*args)

    return jax.shard_map(
        shards,
        mesh=mesh,
        in_specs=(P("root", "col", None), P("col", None), P("root"), P(), P("col", None), P()),
        out_specs=P("root", "col", None),
        check_vma=False,
    )
```

```python
import functools

import jax
import jax.numpy as jnp
from jax import lax
from jax.experimental import pallas as pl
from jax.experimental.pallas import tpu as pltpu
from jax.sharding import PartitionSpec as P

LANES = 128
PAD = 16
TOP = 32764.0
LIMIT = 56 * 1024 * 1024


def scale_of(mantissa, exponent):
    return mantissa * jnp.exp2(exponent - 7.0) * (1.0 / TOP)


def encode(piece):
    width = piece.shape[1]
    top = jnp.maximum(jnp.max(jnp.abs(piece), axis=0, keepdims=True), 1e-25)
    exponent = jnp.floor(jnp.log2(top))
    mantissa = jnp.floor(top * jnp.exp2(7.0 - exponent)) + 1.0
    codes = jnp.floor(piece * (1.0 / scale_of(mantissa, exponent)) + 0.5)
    codes = codes.astype(jnp.int32).astype(jnp.int16)
    row = lax.broadcasted_iota(jnp.int32, (PAD, width), 0)
    tail = jnp.where(row == 0, mantissa, jnp.where(row == 1, exponent, 0.0))
    return codes, tail.astype(jnp.int32).astype(jnp.int16)


def put(ref, index, piece):
    height = piece.shape[0]
    codes, tail = encode(piece)
    ref[index, pl.ds(0, height), :] = codes
    ref[index, pl.ds(height, PAD), :] = tail


def decode(codes, tail):
    tail = tail.astype(jnp.int32).astype(jnp.float32)
    return codes.astype(jnp.int32).astype(jnp.float32) * scale_of(tail[0:1], tail[1:2])


def take(ref, index):
    height = ref.shape[1] - PAD
    return decode(ref[index, pl.ds(0, height), :], ref[index, pl.ds(height, PAD), :])


def split_into(halves, block, value):
    rows = value.shape[0]
    high = value.astype(jnp.bfloat16)
    halves[block, pl.ds(0, rows), :] = high
    low = value - high.astype(jnp.float32)
    halves[block, pl.ds(rows, rows), :] = low.astype(jnp.bfloat16)


def apply_row(halves, tiles, place, cols, block, fill, blk):
    rows = halves.shape[1] // 2
    total = jnp.zeros((2 * rows, blk), jnp.float32)
    for first in range(0, fill, 2):
        terms = range(first, min(first + 2, fill))
        left = [halves[cols[block, f]] for f in terms]
        right = tiles[pl.ds((place * fill + first) * blk, len(left) * blk), :]
        total += lax.dot_general(
            jnp.concatenate(left, axis=1),
            right,
            (((1,), (0,)), ((), ())),
            preferred_element_type=jnp.float32,
        )
    return total[:rows] + total[rows:]


def pack_kernel(here, v_ref, d_ref, out_ref):
    many, rows = out_ref.shape[0], out_ref.shape[2]
    width = v_ref.shape[1] // many
    slab = out_ref.shape[1] - width - PAD
    at = pl.multiple_of(here[0, 0] * slab, slab)
    for n in range(many):
        put(out_ref, n, v_ref[:, n * width : (n + 1) * width].T)
        mine = d_ref[pl.ds(at, slab), n * width : (n + 1) * width]
        codes = jnp.floor(mine * 32767.0 + 0.5)
        out_ref[n, pl.ds(width + PAD, slab), :] = codes.astype(jnp.int32).astype(jnp.int16)


def ring_at(spot, groups):
    return jnp.where(spot * 2 < groups, 2 * spot, 2 * (groups - 1 - spot) + 1)


def ring_spot(col, groups):
    half = jnp.right_shift(col, 1)
    return jnp.where(jnp.bitwise_and(col, 1) == 0, half, groups - 1 - half)


def right_first_kernel(dims, groups, owners, masks, cols, shift, place, v_ref, d_ref, own, *rest):
    nblk, fill, blk, per = dims
    shards, (w_ref, u_ref, tiles_ref, halves, turned, tiles) = rest[:-6], rest[-6:]
    step = pl.program_id(0)
    size = own.shape[0]

    @pl.when(step == 0)
    def _():
        for b in range(nblk):
            split_into(halves, b, v_ref[:, b * blk : (b + 1) * blk])
        root, col = place[0, 0], place[0, 1]
        tiles[pl.ds(pl.multiple_of(col * size, size), size), :] = own[...]
        spot = ring_spot(col, groups)
        bases = [
            ring_at(lax.rem(spot + (owner + groups), groups), groups) * size
            + jnp.bitwise_xor(root, mask) * shards[0].shape[1]
            for owner in owners
            for mask in masks
        ]

        @pl.loop(0, size // blk)
        def _(b):
            for k, shard in enumerate(shards):
                share = shard.shape[1]
                at = pl.multiple_of(bases[k] + b * blk, share)
                tiles[pl.ds(at, share), :] = shard[b]

    here_tiles = tiles.at[pl.ds(pl.multiple_of(step * size, size), size), :]
    tiles_ref[...] = here_tiles[...]
    for t in range(per):
        lanes = slice(t * blk, (t + 1) * blk)
        block = step * per + t
        here = v_ref[:, pl.ds(pl.multiple_of(block * blk, blk), blk)]
        moved = apply_row(halves, here_tiles, t, cols, block, fill, blk)
        whole = moved + (d_ref[:, lanes] - shift[0, 0]) * here
        w_ref[:, lanes] = whole
        turned[lanes, :] = (moved + whole).T
    put(u_ref, 0, turned[...])


def left_first_kernel(dims, cols, tv_ref, tiles, y_ref, halves):
    nblk, fill, blk, per = dims
    step = pl.program_id(0)

    @pl.when(step == 0)
    def _():
        for p in range(nblk // per):
            value = take(tv_ref, p)
            for t in range(per):
                split_into(halves, p * per + t, value[:, t * blk : (t + 1) * blk])

    for t in range(per):
        y_ref[:, t * blk : (t + 1) * blk] = apply_row(halves, tiles, t, cols, step * per + t, fill, blk)


def right_second_kernel(dims, cols, shift, w_ref, v_ref, d_ref, tiles, *rest):
    nblk, fill, blk, per = dims
    outs, halves = rest[:-1], rest[-1]
    step = pl.program_id(0)

    @pl.when(step == 0)
    def _():
        for b in range(nblk):
            split_into(halves, b, w_ref[:, b * blk : (b + 1) * blk])

    for t in range(per):
        lanes = slice(t * blk, (t + 1) * blk)
        block = step * per + t
        here = w_ref[:, pl.ds(pl.multiple_of(block * blk, blk), blk)]
        moved = apply_row(halves, tiles, t, cols, block, fill, blk)
        outs[t][...] = 0.5 * (moved + (d_ref[:, lanes] - shift[0, 0]) * here) - v_ref[:, lanes]


def left_second_kernel(dims, masks, cols, shift, place, tu_ref, tail_ref, y_ref, tiles, *rest):
    nblk, fill, blk, per = dims
    slabs, (_, out, halves, turned) = rest[:-4], rest[-4:]
    step = pl.program_id(0)
    part = y_ref.shape[0]

    @pl.when(step == 0)
    def _():
        for p in range(nblk // per):
            value = decode(tu_ref[p], tail_ref[p]) + y_ref[:, p * per * blk : (p + 1) * per * blk]
            for t in range(per):
                split_into(halves, p * per + t, value[:, t * blk : (t + 1) * blk])

    for m, slab in enumerate(slabs):
        height = slab.shape[1]
        at = pl.multiple_of(jnp.bitwise_xor(place[0, 0], masks[m]) * height, height)
        turned[pl.ds(at, height), :] = slab[0].astype(jnp.int32).astype(jnp.float32)
    done = []
    for t in range(per):
        block = step * per + t
        here = y_ref[:, pl.ds(pl.multiple_of(block * blk, blk), blk)]
        diagonal = turned[t * blk : (t + 1) * blk, :].T
        moved = apply_row(halves, tiles, t, cols, block, fill, blk)
        done.append((0.5 * (moved + (diagonal * (1.0 / 32767.0) - shift[0, 0]) * here)).T)
    put(out, 0, jnp.concatenate(done, axis=0))


def second_kernel(weights, z_ref, p_ref, out_ref):
    del weights
    part = z_ref.shape[2]
    for n in range(z_ref.shape[0]):
        put(out_ref, n, take(z_ref, n) + p_ref[:, n * part : (n + 1) * part])


def rotate_kernel(aliased, weights, *refs):
    ins, out_ref = refs[aliased:-1], refs[-1]
    total = weights[0, 0] * take(ins[0], 0)
    for m in range(1, len(ins)):
        total += weights[0, m] * take(ins[m], 0)
    out_ref[0] = total


def smem():
    return pl.BlockSpec(memory_space=pltpu.SMEM)


def call(kernel, grid, in_specs, out_specs, out_shape, scratch, flops, moved, aliases={}):
    return pl.pallas_call(
        kernel,
        grid=(grid,),
        in_specs=in_specs,
        out_specs=out_specs,
        out_shape=out_shape,
        scratch_shapes=scratch,
        input_output_aliases=aliases,
        compiler_params=pltpu.CompilerParams(
            dimension_semantics=("arbitrary",), vmem_limit_bytes=LIMIT
        ),
        cost_estimate=pl.CostEstimate(flops=flops, bytes_accessed=moved, transcendentals=0),
    )


def blocked_shards(sizes, coeffs, diagonal, shift, rotation, string_blocks, block_cols):
    roots, groups = sizes
    start = coeffs[0]
    rows, strings = start.shape
    nblk, fill = block_cols.shape
    blk = strings // nblk
    width = strings // groups
    per = width // blk
    chunks = per
    dims = (nblk, fill, blk, per)
    energy = shift.reshape(1, 1)
    root = lax.axis_index("root")
    f32, i16 = jnp.float32, jnp.int16

    def swap(pieces):
        return lax.all_to_all(pieces, "col", split_axis=0, concat_axis=0, tiled=True)

    piece = pl.BlockSpec((rows, width), lambda q: (0, q))
    whole = pl.BlockSpec((rows, strings), lambda q: (0, 0), pipeline_mode=pl.Buffered(1))
    coded = pl.BlockSpec((1, width + PAD, rows), lambda q: (q, 0, 0))
    all_coded = pl.BlockSpec((groups, width + PAD, rows), lambda q: (0, 0, 0), pipeline_mode=pl.Buffered(1))
    tile_spec = pl.BlockSpec((per * fill * blk, blk), lambda q: (q, 0))
    codes_shape = jax.ShapeDtypeStruct((groups, width + PAD, rows), i16)
    row_shape = jax.ShapeDtypeStruct((rows, strings), f32)
    row_halves = pltpu.VMEM((nblk, 2 * rows, blk), jnp.bfloat16)
    col_halves = pltpu.VMEM((nblk, 2 * width, blk), jnp.bfloat16)
    work = 2 * 2 * rows * strings * fill * blk
    size = 4 * rows * strings

    def cross(have, bit):
        pairs = [(r, r ^ bit) for r in range(roots)]
        return have + [lax.ppermute(h, "root", pairs) for h in have]

    def exchange(have, bit=roots // 2, late=None):
        if late is not None:
            have = list(lax.optimization_barrier((*have, late)))[:-1]
        while bit:
            have = cross(have, bit)
            bit //= 2
        return have

    masks, bit = [0], roots // 2
    while bit:
        masks = masks + [m ^ bit for m in masks]
        bit //= 2
    far = jnp.bitwise_xor(root, jnp.array(masks, jnp.int32))
    weights = rotation[root][far].reshape(1, -1)
    place = jnp.stack([root, lax.axis_index("col")]).astype(jnp.int32).reshape(1, 2)

    ring = list(range(0, groups, 2)) + list(range(1, groups, 2))[::-1]
    share = blk // roots
    owners = []
    for hop in range(1, groups // 2 + 1):
        owners += [-hop, hop] if 2 * hop < groups else [-hop]

    slab = rows // roots
    height = width + PAD + slab

    def pack(start, diagonal):
        pair = 2 if groups % 2 == 0 else 1
        pieces = pl.BlockSpec((rows, pair * width), lambda q: (0, q))
        return call(
            pack_kernel,
            groups // pair,
            [smem(), pieces, pieces],
            pl.BlockSpec((pair, height, rows), lambda q: (q, 0, 0)),
            jax.ShapeDtypeStruct((groups, height, rows), i16),
            [],
            0,
            size * 3,
        )(place, start, diagonal)

    own = jnp.swapaxes(string_blocks.reshape(-1, blk, blk), 1, 2)
    mine = lax.dynamic_slice_in_dim(own, root * share, share, 1)
    shards, crossed, tv, forth, back = [], [], None, mine, mine
    for hop in range(1, groups // 2 + 1):
        if hop == 3:
            forth, back = lax.optimization_barrier((forth, back, tv, *crossed[:2]))[:2]
        for way in (1, -1) if 2 * hop < groups else (1,):
            pairs = [(ring[s], ring[(s + way) % groups]) for s in range(groups)]
            moved = lax.ppermute(forth if way == 1 else back, "col", pairs)
            forth, back = (moved, back) if way == 1 else (forth, moved)
            shards += exchange([moved])
            crossed.append(shards[1 - roots])
        if hop == 1:
            tv = pack(*lax.optimization_barrier((start, diagonal, forth, back))[:2])
    tv = swap(lax.optimization_barrier((tv, forth, back))[0])
    own = own.reshape(string_blocks.shape)

    once = pl.Buffered(1)
    shard_spec = pl.BlockSpec(mine.shape, lambda q: (0, 0, 0), pipeline_mode=once)
    w, tu, tiles = call(
        functools.partial(right_first_kernel, dims, groups, owners, masks),
        groups,
        [smem(), smem(), smem(), whole, piece]
        + [pl.BlockSpec(string_blocks.shape, lambda q: (0, 0), pipeline_mode=once)]
        + [shard_spec] * len(shards),
        [piece, coded, tile_spec],
        [
            row_shape,
            codes_shape,
            jax.ShapeDtypeStruct((nblk * fill * blk, blk), string_blocks.dtype),
        ],
        [
            row_halves,
            pltpu.VMEM((width, rows), f32),
            pltpu.VMEM((nblk * fill * blk, blk), string_blocks.dtype),
        ],
        work,
        size * 6,
    )(block_cols, energy, place, start, diagonal, own, *shards)
    tu = swap(tu)

    base = call(
        functools.partial(right_second_kernel, dims),
        groups,
        [smem(), smem(), whole, piece, piece, tile_spec],
        [pl.BlockSpec((rows, blk), lambda q: (0, q))] * chunks,
        [jax.ShapeDtypeStruct((rows, groups * blk), f32)] * chunks,
        [row_halves],
        work,
        size * 5,
    )(block_cols, energy, w, start, diagonal, tiles)

    y = call(
        functools.partial(left_first_kernel, dims),
        groups,
        [smem(), all_coded, tile_spec],
        pl.BlockSpec((width, width), lambda q: (0, q)),
        jax.ShapeDtypeStruct((width, strings), f32),
        [col_halves],
        work,
        size * 3,
    )(block_cols, tv, tiles)

    half = roots // 2
    slabs = exchange(cross([tv[:, width + PAD :]], half), half // 2, y)
    part = width // chunks
    chunk_coded = pl.BlockSpec((1, rows + PAD, part), lambda q: (q, 0, 0))
    many = 4 if groups % 4 == 0 else 1
    many_coded = pl.BlockSpec((many, rows + PAD, part), lambda q: (q, 0, 0))
    seconds, crossings = [], []
    for k in range(chunks):
        z = call(
            functools.partial(left_second_kernel, dims, masks),
            groups,
            [
                smem(),
                smem(),
                smem(),
                pl.BlockSpec((groups, part, rows), lambda q, k=k: (0, k, 0), pipeline_mode=once),
                pl.BlockSpec((groups, PAD, rows), lambda q: (0, width // PAD, 0), pipeline_mode=once),
                pl.BlockSpec((part, strings), lambda q, k=k: (k, 0), pipeline_mode=once),
                tile_spec,
            ]
            + [pl.BlockSpec((1, slab, part), lambda q, k=k: (q, 0, k))] * roots
            + [pl.BlockSpec(memory_space=pl.ANY)],
            chunk_coded,
            jax.ShapeDtypeStruct((groups, rows + PAD, part), i16),
            [pltpu.VMEM((nblk, 2 * part, blk), jnp.bfloat16), pltpu.VMEM((rows, part), f32)],
            work // chunks,
            size * 4 // chunks,
        )(block_cols, energy, place, tu, tu, y, tiles, *slabs, base[0] if k < 2 else seconds[k - 2])
        if k > 1:
            z = lax.optimization_barrier((z, *crossings[k - 2]))[0]
        second = call(
            second_kernel,
            groups // many,
            [smem(), many_coded, pl.BlockSpec((rows, many * part), lambda q: (0, q))],
            many_coded,
            jax.ShapeDtypeStruct((groups, rows + PAD, part), i16),
            [],
            0,
            1,
        )(weights, swap(z), base[k])
        seconds.append(second)
        crossings.append(cross([second], half))
    out = []
    for k in range(chunks):
        late = seconds[k + 1] if k < chunks - 1 else out[0] if out else None
        slot = pl.BlockSpec((1, rows, part), lambda q, k=k: (0, 0, q * chunks + k))
        out = [
            call(
                functools.partial(rotate_kernel, len(out)),
                groups,
                [smem()] + [pl.BlockSpec(memory_space=pl.ANY)] * len(out) + [chunk_coded] * roots,
                slot,
                jax.ShapeDtypeStruct((1, rows, strings), f32),
                [],
                0,
                1,
                {1: 0} if out else {},
            )(weights, *out, *exchange(crossings[k], half // 2, late))
        ]
    return out[0]


def plain_blocks(matrix, operator_blocks, block_cols):
    height, breadth = matrix.shape
    nblocks, filled = block_cols.shape
    blocksize = breadth // nblocks
    grouped = matrix.reshape(height, nblocks, blocksize)
    picked = jnp.take(grouped, block_cols, axis=1)
    tiles = operator_blocks.reshape(nblocks, filled, blocksize, blocksize).astype(jnp.float32)
    result = jnp.einsum("rifk,ifjk->rij", picked, tiles, precision=lax.Precision.HIGHEST)
    return result.reshape(height, breadth)


def plain_swap(matrix):
    height, breadth = matrix.shape
    pieces = matrix.reshape(height, breadth // height, height).transpose(1, 2, 0)
    moved = lax.all_to_all(pieces, "col", split_axis=0, concat_axis=0, tiled=True)
    return moved.transpose(1, 0, 2).reshape(height, breadth)


def plain_shards(coeffs, diagonal, shift, rotation, string_blocks, block_cols):
    start = coeffs[0]
    energy = shift[0]
    operator_blocks = lax.all_gather(string_blocks, "col", axis=0, tiled=True)

    def sigma(vector):
        beta = plain_swap(plain_blocks(plain_swap(vector), operator_blocks, block_cols))
        return plain_blocks(vector, operator_blocks, block_cols) + beta + diagonal * vector

    first = 0.5 * (sigma(start) - energy * start)
    second = sigma(first) - energy * first - start
    weights = lax.dynamic_index_in_dim(rotation, lax.axis_index("root"), 1, keepdims=False)
    terms = weights[:, None, None] * second[None]
    return lax.psum_scatter(terms, "root", scatter_dimension=0, tiled=True)


def solution(mesh):
    roots, groups = mesh.shape["root"], mesh.shape["col"]

    def shards(coeffs, diagonal, shift, rotation, string_blocks, block_cols):
        rows, strings = coeffs.shape[1:]
        blk = strings // block_cols.shape[0]
        width = strings // groups
        regular = blk % LANES == 0 and width % blk == 0 and rows == width
        regular = regular and roots > 1 and roots & (roots - 1) == 0 and width % (16 * roots) == 0
        regular = regular and groups % 2 == 0 and blk % (16 * roots) == 0
        args = (coeffs, diagonal, shift, rotation, string_blocks, block_cols)
        if regular:
            return blocked_shards((roots, groups), *args)
        return plain_shards(*args)

    return jax.shard_map(
        shards,
        mesh=mesh,
        in_specs=(P("root", "col", None), P("col", None), P("root"), P(), P("col", None), P()),
        out_specs=P("root", "col", None),
        check_vma=False,
    )
```

```python
import functools

import jax
import jax.numpy as jnp
from jax import lax
from jax.experimental import pallas as pl
from jax.experimental.pallas import tpu as pltpu
from jax.sharding import PartitionSpec as P

LANES = 128
PAD = 16
TOP = 32764.0
LIMIT = 56 * 1024 * 1024


def scale_of(mantissa, exponent):
    return mantissa * jnp.exp2(exponent - 7.0) * (1.0 / TOP)


def encode(piece):
    width = piece.shape[1]
    top = jnp.maximum(jnp.max(jnp.abs(piece), axis=0, keepdims=True), 1e-25)
    exponent = jnp.floor(jnp.log2(top))
    mantissa = jnp.floor(top * jnp.exp2(7.0 - exponent)) + 1.0
    codes = jnp.floor(piece * (1.0 / scale_of(mantissa, exponent)) + 0.5)
    codes = codes.astype(jnp.int32).astype(jnp.int16)
    row = lax.broadcasted_iota(jnp.int32, (PAD, width), 0)
    tail = jnp.where(row == 0, mantissa, jnp.where(row == 1, exponent, 0.0))
    return codes, tail.astype(jnp.int32).astype(jnp.int16)


def put(ref, index, piece):
    height = piece.shape[0]
    codes, tail = encode(piece)
    ref[index, pl.ds(0, height), :] = codes
    ref[index, pl.ds(height, PAD), :] = tail


def decode(codes, tail):
    tail = tail.astype(jnp.int32).astype(jnp.float32)
    return codes.astype(jnp.int32).astype(jnp.float32) * scale_of(tail[0:1], tail[1:2])


def take(ref, index):
    height = ref.shape[1] - PAD
    return decode(ref[index, pl.ds(0, height), :], ref[index, pl.ds(height, PAD), :])


def split_into(halves, block, value):
    rows = value.shape[0]
    high = value.astype(jnp.bfloat16)
    halves[block, pl.ds(0, rows), :] = high
    low = value - high.astype(jnp.float32)
    halves[block, pl.ds(rows, rows), :] = low.astype(jnp.bfloat16)


def apply_row(halves, tiles, place, cols, block, fill, blk):
    rows = halves.shape[1] // 2
    total = jnp.zeros((2 * rows, blk), jnp.float32)
    for first in range(0, fill, 2):
        terms = range(first, min(first + 2, fill))
        left = [halves[cols[block, f]] for f in terms]
        right = tiles[pl.ds((place * fill + first) * blk, len(left) * blk), :]
        total += lax.dot_general(
            jnp.concatenate(left, axis=1),
            right,
            (((1,), (0,)), ((), ())),
            preferred_element_type=jnp.float32,
        )
    return total[:rows] + total[rows:]


def pack_kernel(here, v_ref, d_ref, out_ref):
    many, rows = out_ref.shape[0], out_ref.shape[2]
    width = v_ref.shape[1] // many
    slab = out_ref.shape[1] - width - PAD
    at = pl.multiple_of(here[0, 0] * slab, slab)
    for n in range(many):
        put(out_ref, n, v_ref[:, n * width : (n + 1) * width].T)
        mine = d_ref[pl.ds(at, slab), n * width : (n + 1) * width]
        codes = jnp.floor(mine * 32767.0 + 0.5)
        out_ref[n, pl.ds(width + PAD, slab), :] = codes.astype(jnp.int32).astype(jnp.int16)


def ring_at(spot, groups):
    return jnp.where(spot * 2 < groups, 2 * spot, 2 * (groups - 1 - spot) + 1)


def ring_spot(col, groups):
    half = jnp.right_shift(col, 1)
    return jnp.where(jnp.bitwise_and(col, 1) == 0, half, groups - 1 - half)


def right_first_kernel(dims, groups, owners, masks, cols, shift, place, v_ref, d_ref, own, *rest):
    nblk, fill, blk, per = dims
    shards, (w_ref, u_ref, tiles_ref, halves, turned, tiles) = rest[:-6], rest[-6:]
    step = pl.program_id(0)
    size = own.shape[0]

    @pl.when(step == 0)
    def _():
        for b in range(nblk):
            split_into(halves, b, v_ref[:, b * blk : (b + 1) * blk])
        root, col = place[0, 0], place[0, 1]
        tiles[pl.ds(pl.multiple_of(col * size, size), size), :] = own[...]
        spot = ring_spot(col, groups)
        bases = [
            ring_at(lax.rem(spot + (owner + groups), groups), groups) * size
            + jnp.bitwise_xor(root, mask) * shards[0].shape[1]
            for owner in owners
            for mask in masks
        ]

        @pl.loop(0, size // blk)
        def _(b):
            for k, shard in enumerate(shards):
                share = shard.shape[1]
                at = pl.multiple_of(bases[k] + b * blk, share)
                tiles[pl.ds(at, share), :] = shard[b]

    here_tiles = tiles.at[pl.ds(pl.multiple_of(step * size, size), size), :]
    tiles_ref[...] = here_tiles[...]
    for t in range(per):
        lanes = slice(t * blk, (t + 1) * blk)
        block = step * per + t
        here = v_ref[:, pl.ds(pl.multiple_of(block * blk, blk), blk)]
        moved = apply_row(halves, here_tiles, t, cols, block, fill, blk)
        whole = moved + (d_ref[:, lanes] - shift[0, 0]) * here
        w_ref[:, lanes] = whole
        turned[lanes, :] = (moved + whole).T
    put(u_ref, 0, turned[...])


def left_first_kernel(dims, cols, tv_ref, tiles, y_ref, halves):
    nblk, fill, blk, per = dims
    step = pl.program_id(0)

    @pl.when(step == 0)
    def _():
        for p in range(nblk // per):
            value = take(tv_ref, p)
            for t in range(per):
                split_into(halves, p * per + t, value[:, t * blk : (t + 1) * blk])

    for t in range(per):
        y_ref[:, t * blk : (t + 1) * blk] = apply_row(halves, tiles, t, cols, step * per + t, fill, blk)


def right_second_kernel(dims, cols, shift, w_ref, v_ref, d_ref, tiles, *rest):
    nblk, fill, blk, per = dims
    outs, halves = rest[:-1], rest[-1]
    step = pl.program_id(0)

    @pl.when(step == 0)
    def _():
        for b in range(nblk):
            split_into(halves, b, w_ref[:, b * blk : (b + 1) * blk])

    for t in range(per):
        lanes = slice(t * blk, (t + 1) * blk)
        block = step * per + t
        here = w_ref[:, pl.ds(pl.multiple_of(block * blk, blk), blk)]
        moved = apply_row(halves, tiles, t, cols, block, fill, blk)
        outs[t][...] = 0.5 * (moved + (d_ref[:, lanes] - shift[0, 0]) * here) - v_ref[:, lanes]


def left_second_kernel(dims, masks, place, cols, shift, tu_ref, tail_ref, y_ref, tiles, *rest):
    nblk, fill, blk, per = dims
    groups = nblk // per
    slabs, outs, (halves, turned) = rest[: len(masks)], rest[len(masks) + 1 : -2], rest[-2:]
    step = pl.program_id(0)
    to = jnp.bitwise_xor(place[0, 1], step)

    @pl.when(step == 0)
    def _():
        for p in range(groups):
            value = decode(tu_ref[p], tail_ref[p]) + y_ref[:, p * per * blk : (p + 1) * per * blk]
            for t in range(per):
                split_into(halves, p * per + t, value[:, t * blk : (t + 1) * blk])

    for m, slab in enumerate(slabs):
        height = slab.shape[1]
        at = pl.multiple_of(jnp.bitwise_xor(place[0, 0], masks[m]) * height, height)
        turned[pl.ds(at, height), :] = slab[0].astype(jnp.int32).astype(jnp.float32)
    done = []
    for t in range(per):
        block = to * per + t
        here = y_ref[:, pl.ds(pl.multiple_of(block * blk, blk), blk)]
        diagonal = turned[t * blk : (t + 1) * blk, :].T
        moved = apply_row(halves, tiles, t, cols, block, fill, blk)
        done.append((0.5 * (moved + (diagonal * (1.0 / 32767.0) - shift[0, 0]) * here)).T)
    codes, tail = encode(jnp.concatenate(done, axis=0))
    for m, out in enumerate(outs):

        @pl.when(step == m)
        def _(out=out):
            out[pl.ds(0, codes.shape[0]), :] = codes
            out[pl.ds(codes.shape[0], PAD), :] = tail


def second_kernel(place, weights, p_ref, after, *refs):
    del weights, after
    pieces, out_ref = refs[:-1], refs[-1]
    part = out_ref.shape[2]
    height = out_ref.shape[1] - PAD
    for n, piece in enumerate(pieces):
        m = len(pieces) - 1 - n
        at = pl.multiple_of(jnp.bitwise_xor(place[0, 1], m) * part, part)
        value = decode(piece[pl.ds(0, height), :], piece[pl.ds(height, PAD), :])
        put(out_ref, m, value + p_ref[:, pl.ds(at, part)])


def rotate_kernel(aliased, place, weights, *refs):
    del place
    ins, out_ref = refs[aliased:-1], refs[-1]
    total = weights[0, 0] * take(ins[0], 0)
    for m in range(1, len(ins)):
        total += weights[0, m] * take(ins[m], 0)
    out_ref[0] = total


def smem():
    return pl.BlockSpec(memory_space=pltpu.SMEM)


def call(kernel, grid, in_specs, out_specs, out_shape, scratch, flops, moved, aliases={}, ahead=0):
    return pl.pallas_call(
        kernel,
        grid_spec=pltpu.PrefetchScalarGridSpec(
            num_scalar_prefetch=ahead,
            grid=(grid,),
            in_specs=in_specs,
            out_specs=out_specs,
            scratch_shapes=scratch,
        ),
        out_shape=out_shape,
        input_output_aliases=aliases,
        compiler_params=pltpu.CompilerParams(
            dimension_semantics=("arbitrary",), vmem_limit_bytes=LIMIT
        ),
        cost_estimate=pl.CostEstimate(flops=flops, bytes_accessed=moved, transcendentals=0),
    )


def blocked_shards(sizes, coeffs, diagonal, shift, rotation, string_blocks, block_cols):
    roots, groups = sizes
    start = coeffs[0]
    rows, strings = start.shape
    nblk, fill = block_cols.shape
    blk = strings // nblk
    width = strings // groups
    per = width // blk
    chunks = per
    dims = (nblk, fill, blk, per)
    energy = shift.reshape(1, 1)
    root = lax.axis_index("root")
    f32, i16 = jnp.float32, jnp.int16

    def swap(pieces):
        return lax.all_to_all(pieces, "col", split_axis=0, concat_axis=0, tiled=True)

    piece = pl.BlockSpec((rows, width), lambda q: (0, q))
    whole = pl.BlockSpec((rows, strings), lambda q: (0, 0), pipeline_mode=pl.Buffered(1))
    coded = pl.BlockSpec((1, width + PAD, rows), lambda q: (q, 0, 0))
    all_coded = pl.BlockSpec((groups, width + PAD, rows), lambda q: (0, 0, 0), pipeline_mode=pl.Buffered(1))
    tile_spec = pl.BlockSpec((per * fill * blk, blk), lambda q: (q, 0))
    codes_shape = jax.ShapeDtypeStruct((groups, width + PAD, rows), i16)
    row_shape = jax.ShapeDtypeStruct((rows, strings), f32)
    row_halves = pltpu.VMEM((nblk, 2 * rows, blk), jnp.bfloat16)
    col_halves = pltpu.VMEM((nblk, 2 * width, blk), jnp.bfloat16)
    work = 2 * 2 * rows * strings * fill * blk
    size = 4 * rows * strings

    def cross(have, bit):
        pairs = [(r, r ^ bit) for r in range(roots)]
        return have + [lax.ppermute(h, "root", pairs) for h in have]

    def exchange(have, bit=roots // 2, late=None):
        if late is not None:
            have = list(lax.optimization_barrier((*have, late)))[:-1]
        while bit:
            have = cross(have, bit)
            bit //= 2
        return have

    masks, bit = [0], roots // 2
    while bit:
        masks = masks + [m ^ bit for m in masks]
        bit //= 2
    far = jnp.bitwise_xor(root, jnp.array(masks, jnp.int32))
    weights = rotation[root][far].reshape(1, -1)
    place = jnp.stack([root, lax.axis_index("col")]).astype(jnp.int32).reshape(1, 2)

    ring = list(range(0, groups, 2)) + list(range(1, groups, 2))[::-1]
    share = blk // roots
    owners = []
    for hop in range(1, groups // 2 + 1):
        owners += [-hop, hop] if 2 * hop < groups else [-hop]

    slab = rows // roots
    height = width + PAD + slab

    def pack(start, diagonal):
        pair = 2 if groups % 2 == 0 else 1
        pieces = pl.BlockSpec((rows, pair * width), lambda q: (0, q))
        return call(
            pack_kernel,
            groups // pair,
            [smem(), pieces, pieces],
            pl.BlockSpec((pair, height, rows), lambda q: (q, 0, 0)),
            jax.ShapeDtypeStruct((groups, height, rows), i16),
            [],
            0,
            size * 3,
        )(place, start, diagonal)

    own = jnp.swapaxes(string_blocks.reshape(-1, blk, blk), 1, 2)
    mine = lax.dynamic_slice_in_dim(own, root * share, share, 1)
    shards, crossed, tv, forth, back = [], [], None, mine, mine
    for hop in range(1, groups // 2 + 1):
        if hop == 3:
            forth, back = lax.optimization_barrier((forth, back, tv, *crossed[:2]))[:2]
        for way in (1, -1) if 2 * hop < groups else (1,):
            pairs = [(ring[s], ring[(s + way) % groups]) for s in range(groups)]
            moved = lax.ppermute(forth if way == 1 else back, "col", pairs)
            forth, back = (moved, back) if way == 1 else (forth, moved)
            shards += exchange([moved])
            crossed.append(shards[1 - roots])
        if hop == 1:
            tv = pack(*lax.optimization_barrier((start, diagonal, forth, back))[:2])
    tv = swap(lax.optimization_barrier((tv, forth, back))[0])
    own = own.reshape(string_blocks.shape)

    once = pl.Buffered(1)
    shard_spec = pl.BlockSpec(mine.shape, lambda q: (0, 0, 0), pipeline_mode=once)
    w, tu, tiles = call(
        functools.partial(right_first_kernel, dims, groups, owners, masks),
        groups,
        [smem(), smem(), smem(), whole, piece]
        + [pl.BlockSpec(string_blocks.shape, lambda q: (0, 0), pipeline_mode=once)]
        + [shard_spec] * len(shards),
        [piece, coded, tile_spec],
        [
            row_shape,
            codes_shape,
            jax.ShapeDtypeStruct((nblk * fill * blk, blk), string_blocks.dtype),
        ],
        [
            row_halves,
            pltpu.VMEM((width, rows), f32),
            pltpu.VMEM((nblk * fill * blk, blk), string_blocks.dtype),
        ],
        work,
        size * 6,
    )(block_cols, energy, place, start, diagonal, own, *shards)
    tu = swap(tu)

    base = call(
        functools.partial(right_second_kernel, dims),
        groups,
        [smem(), smem(), whole, piece, piece, tile_spec],
        [pl.BlockSpec((rows, blk), lambda q: (0, q))] * chunks,
        [jax.ShapeDtypeStruct((rows, groups * blk), f32)] * chunks,
        [row_halves],
        work,
        size * 5,
    )(block_cols, energy, w, start, diagonal, tiles)

    y = call(
        functools.partial(left_first_kernel, dims),
        groups,
        [smem(), all_coded, tile_spec],
        pl.BlockSpec((width, width), lambda q: (0, q)),
        jax.ShapeDtypeStruct((width, strings), f32),
        [col_halves],
        work,
        size * 3,
    )(block_cols, tv, tiles)

    half = roots // 2
    slabs = exchange(cross([tv[:, width + PAD :]], half), half // 2, y)
    part = width // chunks
    half = roots // 2
    slabs = exchange(cross([tv[:, width + PAD :]], half), half // 2, y)

    def aim(q, place):
        return jnp.bitwise_xor(place[0, 1], q)

    def all_of(*shape):
        return pl.BlockSpec(shape, lambda q, s: (0,) * len(shape), pipeline_mode=once)

    coded_piece = jax.ShapeDtypeStruct((rows + PAD, part), i16)
    def left_second(k, after):
        return call(
            functools.partial(left_second_kernel, dims, masks),
            groups,
            [
                smem(),
                smem(),
                pl.BlockSpec((groups, part, rows), lambda q, s: (0, k, 0), pipeline_mode=once),
                pl.BlockSpec((groups, PAD, rows), lambda q, s: (0, width // PAD, 0), pipeline_mode=once),
                pl.BlockSpec((part, strings), lambda q, s: (k, 0), pipeline_mode=once),
                pl.BlockSpec((per * fill * blk, blk), lambda q, s: (aim(q, s), 0)),
            ]
            + [pl.BlockSpec((1, slab, part), lambda q, s: (aim(q, s), 0, k))] * roots
            + [pl.BlockSpec(memory_space=pl.ANY)],
            [pl.BlockSpec((rows + PAD, part), lambda q, s: (0, 0))] * groups,
            [coded_piece] * groups,
            [pltpu.VMEM((nblk, 2 * part, blk), jnp.bfloat16), pltpu.VMEM((rows, part), f32)],
            work // chunks,
            size * 4 // chunks,
            {},
            1,
        )(place, block_cols, energy, tu, tu, y, tiles, *slabs, after)

    seconds, crossings = [], []
    made = [left_second(0, base[0])]
    for k in range(chunks):
        pieces = list(made[k])
        if k > 1:
            pieces[1] = lax.optimization_barrier((pieces[1], *crossings[k - 2]))[0]
        for m in range(groups - 1, 0, -1):
            pieces[m] = lax.ppermute(pieces[m], "col", [(c, c ^ m) for c in range(groups)])
        if k + 1 < chunks:
            made.append(left_second(k + 1, seconds[k - 1] if k else base[0]))
        second = call(
            second_kernel,
            1,
            [smem(), all_of(rows, groups * part), pl.BlockSpec(memory_space=pl.ANY)]
            + [all_of(rows + PAD, part)] * groups,
            pl.BlockSpec((groups, rows + PAD, part), lambda q, s: (0, 0, 0)),
            jax.ShapeDtypeStruct((groups, rows + PAD, part), i16),
            [],
            0,
            1,
            {},
            1,
        )(place, weights, base[k], made[-1][0], *pieces[::-1])
        seconds.append(second)
        crossings.append(cross([second], half))
    out = []
    for k in range(chunks):
        late = seconds[k + 1] if k < chunks - 1 else out[0] if out else None
        slot = pl.BlockSpec((1, rows, part), lambda q, s, k=k: (0, 0, aim(q, s) * chunks + k))
        out = [
            call(
                functools.partial(rotate_kernel, len(out)),
                groups,
                [smem()]
                + [pl.BlockSpec(memory_space=pl.ANY)] * len(out)
                + [pl.BlockSpec((1, rows + PAD, part), lambda q, s: (q, 0, 0))] * roots,
                slot,
                jax.ShapeDtypeStruct((1, rows, strings), f32),
                [],
                0,
                1,
                {2: 0} if out else {},
                1,
            )(place, weights, *out, *exchange(crossings[k], half // 2, late))
        ]
    return out[0]


def plain_blocks(matrix, operator_blocks, block_cols):
    height, breadth = matrix.shape
    nblocks, filled = block_cols.shape
    blocksize = breadth // nblocks
    grouped = matrix.reshape(height, nblocks, blocksize)
    picked = jnp.take(grouped, block_cols, axis=1)
    tiles = operator_blocks.reshape(nblocks, filled, blocksize, blocksize).astype(jnp.float32)
    result = jnp.einsum("rifk,ifjk->rij", picked, tiles, precision=lax.Precision.HIGHEST)
    return result.reshape(height, breadth)


def plain_swap(matrix):
    height, breadth = matrix.shape
    pieces = matrix.reshape(height, breadth // height, height).transpose(1, 2, 0)
    moved = lax.all_to_all(pieces, "col", split_axis=0, concat_axis=0, tiled=True)
    return moved.transpose(1, 0, 2).reshape(height, breadth)


def plain_shards(coeffs, diagonal, shift, rotation, string_blocks, block_cols):
    start = coeffs[0]
    energy = shift[0]
    operator_blocks = lax.all_gather(string_blocks, "col", axis=0, tiled=True)

    def sigma(vector):
        beta = plain_swap(plain_blocks(plain_swap(vector), operator_blocks, block_cols))
        return plain_blocks(vector, operator_blocks, block_cols) + beta + diagonal * vector

    first = 0.5 * (sigma(start) - energy * start)
    second = sigma(first) - energy * first - start
    weights = lax.dynamic_index_in_dim(rotation, lax.axis_index("root"), 1, keepdims=False)
    terms = weights[:, None, None] * second[None]
    return lax.psum_scatter(terms, "root", scatter_dimension=0, tiled=True)


def solution(mesh):
    roots, groups = mesh.shape["root"], mesh.shape["col"]

    def shards(coeffs, diagonal, shift, rotation, string_blocks, block_cols):
        rows, strings = coeffs.shape[1:]
        blk = strings // block_cols.shape[0]
        width = strings // groups
        regular = blk % LANES == 0 and width % blk == 0 and rows == width
        regular = regular and roots > 1 and roots & (roots - 1) == 0 and width % (16 * roots) == 0
        regular = regular and groups > 1 and groups & (groups - 1) == 0 and blk % (16 * roots) == 0
        args = (coeffs, diagonal, shift, rotation, string_blocks, block_cols)
        if regular:
            return blocked_shards((roots, groups), *args)
        return plain_shards(*args)

    return jax.shard_map(
        shards,
        mesh=mesh,
        in_specs=(P("root", "col", None), P("col", None), P("root"), P(), P("col", None), P()),
        out_specs=P("root", "col", None),
        check_vma=False,
    )
```

```python
import functools

import jax
import jax.numpy as jnp
from jax import lax
from jax.experimental import pallas as pl
from jax.experimental.pallas import tpu as pltpu
from jax.sharding import PartitionSpec as P

LANES = 128
PAD = 16
TOP = 32764.0
LIMIT = 56 * 1024 * 1024


def scale_of(mantissa, exponent):
    return mantissa * jnp.exp2(exponent - 7.0) * (1.0 / TOP)


def encode(piece):
    width = piece.shape[1]
    top = jnp.maximum(jnp.max(jnp.abs(piece), axis=0, keepdims=True), 1e-25)
    exponent = jnp.floor(jnp.log2(top))
    mantissa = jnp.floor(top * jnp.exp2(7.0 - exponent)) + 1.0
    codes = jnp.floor(piece * (1.0 / scale_of(mantissa, exponent)) + 0.5)
    codes = codes.astype(jnp.int32).astype(jnp.int16)
    row = lax.broadcasted_iota(jnp.int32, (PAD, width), 0)
    tail = jnp.where(row == 0, mantissa, jnp.where(row == 1, exponent, 0.0))
    return codes, tail.astype(jnp.int32).astype(jnp.int16)


def put(ref, index, piece):
    height = piece.shape[0]
    codes, tail = encode(piece)
    ref[index, pl.ds(0, height), :] = codes
    ref[index, pl.ds(height, PAD), :] = tail


def decode(codes, tail):
    tail = tail.astype(jnp.int32).astype(jnp.float32)
    return codes.astype(jnp.int32).astype(jnp.float32) * scale_of(tail[0:1], tail[1:2])


def take(ref, index):
    height = ref.shape[1] - PAD
    return decode(ref[index, pl.ds(0, height), :], ref[index, pl.ds(height, PAD), :])


def split_into(halves, block, value):
    rows = value.shape[0]
    high = value.astype(jnp.bfloat16)
    halves[block, pl.ds(0, rows), :] = high
    low = value - high.astype(jnp.float32)
    halves[block, pl.ds(rows, rows), :] = low.astype(jnp.bfloat16)


def apply_row(halves, tiles, place, cols, block, fill, blk):
    rows = halves.shape[1] // 2
    total = jnp.zeros((2 * rows, blk), jnp.float32)
    for first in range(0, fill, 2):
        terms = range(first, min(first + 2, fill))
        left = [halves[cols[block, f]] for f in terms]
        right = tiles[pl.ds((place * fill + first) * blk, len(left) * blk), :]
        total += lax.dot_general(
            jnp.concatenate(left, axis=1),
            right,
            (((1,), (0,)), ((), ())),
            preferred_element_type=jnp.float32,
        )
    return total[:rows] + total[rows:]


def pack_kernel(here, v_ref, d_ref, out_ref):
    many, rows = out_ref.shape[0], out_ref.shape[2]
    width = v_ref.shape[1] // many
    slab = out_ref.shape[1] - width - PAD
    at = pl.multiple_of(here[0, 0] * slab, slab)
    for n in range(many):
        put(out_ref, n, v_ref[:, n * width : (n + 1) * width].T)
        mine = d_ref[pl.ds(at, slab), n * width : (n + 1) * width]
        codes = jnp.floor(mine * 32767.0 + 0.5)
        out_ref[n, pl.ds(width + PAD, slab), :] = codes.astype(jnp.int32).astype(jnp.int16)


def ring_at(spot, groups):
    return jnp.where(spot * 2 < groups, 2 * spot, 2 * (groups - 1 - spot) + 1)


def ring_spot(col, groups):
    half = jnp.right_shift(col, 1)
    return jnp.where(jnp.bitwise_and(col, 1) == 0, half, groups - 1 - half)


def right_first_kernel(dims, groups, owners, masks, cols, shift, place, v_ref, d_ref, own, *rest):
    nblk, fill, blk, per = dims
    shards, (w_ref, u_ref, more_ref, tiles_ref, halves, turned, tiles) = rest[:-7], rest[-7:]
    step = pl.program_id(0)
    size = own.shape[0]

    @pl.when(step == 0)
    def _():
        for b in range(nblk):
            split_into(halves, b, v_ref[:, b * blk : (b + 1) * blk])
        root, col = place[0, 0], place[0, 1]
        tiles[pl.ds(pl.multiple_of(col * size, size), size), :] = own[...]
        spot = ring_spot(col, groups)
        bases = [
            ring_at(lax.rem(spot + (owner + groups), groups), groups) * size
            + jnp.bitwise_xor(root, mask) * shards[0].shape[1]
            for owner in owners
            for mask in masks
        ]

        @pl.loop(0, size // blk)
        def _(b):
            for k, shard in enumerate(shards):
                share = shard.shape[1]
                at = pl.multiple_of(bases[k] + b * blk, share)
                tiles[pl.ds(at, share), :] = shard[b]

    here_tiles = tiles.at[pl.ds(pl.multiple_of(step * size, size), size), :]
    tiles_ref[...] = here_tiles[...]
    for t in range(per):
        lanes = slice(t * blk, (t + 1) * blk)
        block = step * per + t
        here = v_ref[:, pl.ds(pl.multiple_of(block * blk, blk), blk)]
        moved = apply_row(halves, here_tiles, t, cols, block, fill, blk)
        whole = moved + (d_ref[:, lanes] - shift[0, 0]) * here
        w_ref[:, lanes] = whole
        turned[lanes, :] = (moved + whole).T
    first = u_ref.shape[1] - PAD
    put(u_ref, 0, turned[:first])
    put(more_ref, 0, turned[first:])


def left_first_kernel(dims, cols, tv_ref, tiles, y_ref, halves):
    nblk, fill, blk, per = dims
    step = pl.program_id(0)

    @pl.when(step == 0)
    def _():
        for p in range(nblk // per):
            value = take(tv_ref, p)
            for t in range(per):
                split_into(halves, p * per + t, value[:, t * blk : (t + 1) * blk])

    for t in range(per):
        y_ref[:, t * blk : (t + 1) * blk] = apply_row(halves, tiles, t, cols, step * per + t, fill, blk)


def right_second_kernel(dims, cols, shift, w_ref, v_ref, d_ref, tiles, after, *rest):
    nblk, fill, blk, per = dims
    del after
    outs, halves = rest[:-1], rest[-1]
    step = pl.program_id(0)

    @pl.when(step == 0)
    def _():
        for b in range(nblk):
            split_into(halves, b, w_ref[:, b * blk : (b + 1) * blk])

    for t in range(per):
        lanes = slice(t * blk, (t + 1) * blk)
        block = step * per + t
        here = w_ref[:, pl.ds(pl.multiple_of(block * blk, blk), blk)]
        moved = apply_row(halves, tiles, t, cols, block, fill, blk)
        outs[t][...] = 0.5 * (moved + (d_ref[:, lanes] - shift[0, 0]) * here) - v_ref[:, lanes]


def left_second_kernel(dims, masks, cols, shift, place, tu_ref, tail_ref, y_ref, tiles, *rest):
    nblk, fill, blk, per = dims
    slabs, (_, out, halves, turned) = rest[:-4], rest[-4:]
    step = pl.program_id(0)
    part = y_ref.shape[0]

    @pl.when(step == 0)
    def _():
        for p in range(nblk // per):
            value = decode(tu_ref[p], tail_ref[p]) + y_ref[:, p * per * blk : (p + 1) * per * blk]
            for t in range(per):
                split_into(halves, p * per + t, value[:, t * blk : (t + 1) * blk])

    for m, slab in enumerate(slabs):
        height = slab.shape[1]
        at = pl.multiple_of(jnp.bitwise_xor(place[0, 0], masks[m]) * height, height)
        turned[pl.ds(at, height), :] = slab[0].astype(jnp.int32).astype(jnp.float32)
    done = []
    for t in range(per):
        block = step * per + t
        here = y_ref[:, pl.ds(pl.multiple_of(block * blk, blk), blk)]
        diagonal = turned[t * blk : (t + 1) * blk, :].T
        moved = apply_row(halves, tiles, t, cols, block, fill, blk)
        done.append((0.5 * (moved + (diagonal * (1.0 / 32767.0) - shift[0, 0]) * here)).T)
    put(out, 0, jnp.concatenate(done, axis=0))


def second_kernel(weights, z_ref, p_ref, out_ref):
    del weights
    part = z_ref.shape[2]
    for n in range(z_ref.shape[0]):
        put(out_ref, n, take(z_ref, n) + p_ref[:, n * part : (n + 1) * part])


def rotate_kernel(aliased, weights, *refs):
    ins, out_ref = refs[aliased:-1], refs[-1]
    total = weights[0, 0] * take(ins[0], 0)
    for m in range(1, len(ins)):
        total += weights[0, m] * take(ins[m], 0)
    out_ref[0] = total


def smem():
    return pl.BlockSpec(memory_space=pltpu.SMEM)


def call(kernel, grid, in_specs, out_specs, out_shape, scratch, flops, moved, aliases={}):
    return pl.pallas_call(
        kernel,
        grid=(grid,),
        in_specs=in_specs,
        out_specs=out_specs,
        out_shape=out_shape,
        scratch_shapes=scratch,
        input_output_aliases=aliases,
        compiler_params=pltpu.CompilerParams(
            dimension_semantics=("arbitrary",), vmem_limit_bytes=LIMIT
        ),
        cost_estimate=pl.CostEstimate(flops=flops, bytes_accessed=moved, transcendentals=0),
    )


def blocked_shards(sizes, coeffs, diagonal, shift, rotation, string_blocks, block_cols):
    roots, groups = sizes
    start = coeffs[0]
    rows, strings = start.shape
    nblk, fill = block_cols.shape
    blk = strings // nblk
    width = strings // groups
    per = width // blk
    chunks = per
    dims = (nblk, fill, blk, per)
    energy = shift.reshape(1, 1)
    root = lax.axis_index("root")
    f32, i16 = jnp.float32, jnp.int16

    def swap(pieces):
        return lax.all_to_all(pieces, "col", split_axis=0, concat_axis=0, tiled=True)

    piece = pl.BlockSpec((rows, width), lambda q: (0, q))
    whole = pl.BlockSpec((rows, strings), lambda q: (0, 0), pipeline_mode=pl.Buffered(1))
    coded = pl.BlockSpec((1, width + PAD, rows), lambda q: (q, 0, 0))
    all_coded = pl.BlockSpec((groups, width + PAD, rows), lambda q: (0, 0, 0), pipeline_mode=pl.Buffered(1))
    tile_spec = pl.BlockSpec((per * fill * blk, blk), lambda q: (q, 0))
    codes_shape = jax.ShapeDtypeStruct((groups, width + PAD, rows), i16)
    row_shape = jax.ShapeDtypeStruct((rows, strings), f32)
    row_halves = pltpu.VMEM((nblk, 2 * rows, blk), jnp.bfloat16)
    col_halves = pltpu.VMEM((nblk, 2 * width, blk), jnp.bfloat16)
    work = 2 * 2 * rows * strings * fill * blk
    size = 4 * rows * strings

    def cross(have, bit):
        pairs = [(r, r ^ bit) for r in range(roots)]
        return have + [lax.ppermute(h, "root", pairs) for h in have]

    def exchange(have, bit=roots // 2, late=None):
        if late is not None:
            have = list(lax.optimization_barrier((*have, late)))[:-1]
        while bit:
            have = cross(have, bit)
            bit //= 2
        return have

    masks, bit = [0], roots // 2
    while bit:
        masks = masks + [m ^ bit for m in masks]
        bit //= 2
    far = jnp.bitwise_xor(root, jnp.array(masks, jnp.int32))
    weights = rotation[root][far].reshape(1, -1)
    place = jnp.stack([root, lax.axis_index("col")]).astype(jnp.int32).reshape(1, 2)

    ring = list(range(0, groups, 2)) + list(range(1, groups, 2))[::-1]
    share = blk // roots
    owners = []
    for hop in range(1, groups // 2 + 1):
        owners += [-hop, hop] if 2 * hop < groups else [-hop]

    slab = rows // roots
    height = width + PAD + slab

    def pack(start, diagonal):
        pair = 2 if groups % 2 == 0 else 1
        pieces = pl.BlockSpec((rows, pair * width), lambda q: (0, q))
        return call(
            pack_kernel,
            groups // pair,
            [smem(), pieces, pieces],
            pl.BlockSpec((pair, height, rows), lambda q: (q, 0, 0)),
            jax.ShapeDtypeStruct((groups, height, rows), i16),
            [],
            0,
            size * 3,
        )(place, start, diagonal)

    own = jnp.swapaxes(string_blocks.reshape(-1, blk, blk), 1, 2)
    mine = lax.dynamic_slice_in_dim(own, root * share, share, 1)
    shards, crossed, tv, forth, back = [], [], None, mine, mine
    for hop in range(1, groups // 2 + 1):
        if hop == 3:
            forth, back = lax.optimization_barrier((forth, back, tv, *crossed[:2]))[:2]
        for way in (1, -1) if 2 * hop < groups else (1,):
            pairs = [(ring[s], ring[(s + way) % groups]) for s in range(groups)]
            moved = lax.ppermute(forth if way == 1 else back, "col", pairs)
            forth, back = (moved, back) if way == 1 else (forth, moved)
            shards += exchange([moved])
            crossed.append(shards[1 - roots])
        if hop == 1:
            tv = pack(*lax.optimization_barrier((start, diagonal, forth, back))[:2])
    tv = swap(lax.optimization_barrier((tv, forth, back))[0])
    own = own.reshape(string_blocks.shape)

    once = pl.Buffered(1)
    shard_spec = pl.BlockSpec(mine.shape, lambda q: (0, 0, 0), pipeline_mode=once)
    part = width // chunks
    w, tu, more, tiles = call(
        functools.partial(right_first_kernel, dims, groups, owners, masks),
        groups,
        [smem(), smem(), smem(), whole, piece]
        + [pl.BlockSpec(string_blocks.shape, lambda q: (0, 0), pipeline_mode=once)]
        + [shard_spec] * len(shards),
        [piece]
        + [pl.BlockSpec((1, n + PAD, rows), lambda q: (q, 0, 0)) for n in (part, width - part)]
        + [tile_spec],
        [
            row_shape,
            jax.ShapeDtypeStruct((groups, part + PAD, rows), i16),
            jax.ShapeDtypeStruct((groups, width - part + PAD, rows), i16),
            jax.ShapeDtypeStruct((nblk * fill * blk, blk), string_blocks.dtype),
        ],
        [
            row_halves,
            pltpu.VMEM((width, rows), f32),
            pltpu.VMEM((nblk * fill * blk, blk), string_blocks.dtype),
        ],
        work,
        size * 6,
    )(block_cols, energy, place, start, diagonal, own, *shards)
    tu = swap(tu)
    more = swap(lax.optimization_barrier((more, tu))[0])

    base = call(
        functools.partial(right_second_kernel, dims),
        groups,
        [smem(), smem(), whole, piece, piece, tile_spec, pl.BlockSpec(memory_space=pl.ANY)],
        [pl.BlockSpec((rows, blk), lambda q: (0, q))] * chunks,
        [jax.ShapeDtypeStruct((rows, groups * blk), f32)] * chunks,
        [row_halves],
        work,
        size * 5,
    )(block_cols, energy, w, start, diagonal, tiles, tu)

    y = call(
        functools.partial(left_first_kernel, dims),
        groups,
        [smem(), all_coded, tile_spec],
        pl.BlockSpec((width, width), lambda q: (0, q)),
        jax.ShapeDtypeStruct((width, strings), f32),
        [col_halves],
        work,
        size * 3,
    )(block_cols, tv, tiles)

    half = roots // 2
    slabs = exchange(cross([tv[:, width + PAD :]], half), half // 2, y)
    chunk_coded = pl.BlockSpec((1, rows + PAD, part), lambda q: (q, 0, 0))
    many = 4 if groups % 4 == 0 else 1
    many_coded = pl.BlockSpec((many, rows + PAD, part), lambda q: (q, 0, 0))
    seconds, crossings = [], []
    for k in range(chunks):
        source, at, n = (more, k - 1, width - part) if k else (tu, 0, part)
        z = call(
            functools.partial(left_second_kernel, dims, masks),
            groups,
            [
                smem(),
                smem(),
                smem(),
                pl.BlockSpec((groups, part, rows), lambda q, at=at: (0, at, 0), pipeline_mode=once),
                pl.BlockSpec((groups, PAD, rows), lambda q, n=n: (0, n // PAD, 0), pipeline_mode=once),
                pl.BlockSpec((part, strings), lambda q, k=k: (k, 0), pipeline_mode=once),
                tile_spec,
            ]
            + [pl.BlockSpec((1, slab, part), lambda q, k=k: (q, 0, k))] * roots
            + [pl.BlockSpec(memory_space=pl.ANY)],
            chunk_coded,
            jax.ShapeDtypeStruct((groups, rows + PAD, part), i16),
            [pltpu.VMEM((nblk, 2 * part, blk), jnp.bfloat16), pltpu.VMEM((rows, part), f32)],
            work // chunks,
            size * 4 // chunks,
        )(block_cols, energy, place, source, source, y, tiles, *slabs, base[0] if k < 2 else seconds[k - 2])
        if k > 1:
            z = lax.optimization_barrier((z, *crossings[k - 2]))[0]
        second = call(
            second_kernel,
            groups // many,
            [smem(), many_coded, pl.BlockSpec((rows, many * part), lambda q: (0, q))],
            many_coded,
            jax.ShapeDtypeStruct((groups, rows + PAD, part), i16),
            [],
            0,
            1,
        )(weights, swap(z), base[k])
        seconds.append(second)
        crossings.append(cross([second], half))
    out = []
    for k in range(chunks):
        late = seconds[k + 1] if k < chunks - 1 else out[0] if out else None
        slot = pl.BlockSpec((1, rows, part), lambda q, k=k: (0, 0, q * chunks + k))
        out = [
            call(
                functools.partial(rotate_kernel, len(out)),
                groups,
                [smem()] + [pl.BlockSpec(memory_space=pl.ANY)] * len(out) + [chunk_coded] * roots,
                slot,
                jax.ShapeDtypeStruct((1, rows, strings), f32),
                [],
                0,
                1,
                {1: 0} if out else {},
            )(weights, *out, *exchange(crossings[k], half // 2, late))
        ]
    return out[0]


def plain_blocks(matrix, operator_blocks, block_cols):
    height, breadth = matrix.shape
    nblocks, filled = block_cols.shape
    blocksize = breadth // nblocks
    grouped = matrix.reshape(height, nblocks, blocksize)
    picked = jnp.take(grouped, block_cols, axis=1)
    tiles = operator_blocks.reshape(nblocks, filled, blocksize, blocksize).astype(jnp.float32)
    result = jnp.einsum("rifk,ifjk->rij", picked, tiles, precision=lax.Precision.HIGHEST)
    return result.reshape(height, breadth)


def plain_swap(matrix):
    height, breadth = matrix.shape
    pieces = matrix.reshape(height, breadth // height, height).transpose(1, 2, 0)
    moved = lax.all_to_all(pieces, "col", split_axis=0, concat_axis=0, tiled=True)
    return moved.transpose(1, 0, 2).reshape(height, breadth)


def plain_shards(coeffs, diagonal, shift, rotation, string_blocks, block_cols):
    start = coeffs[0]
    energy = shift[0]
    operator_blocks = lax.all_gather(string_blocks, "col", axis=0, tiled=True)

    def sigma(vector):
        beta = plain_swap(plain_blocks(plain_swap(vector), operator_blocks, block_cols))
        return plain_blocks(vector, operator_blocks, block_cols) + beta + diagonal * vector

    first = 0.5 * (sigma(start) - energy * start)
    second = sigma(first) - energy * first - start
    weights = lax.dynamic_index_in_dim(rotation, lax.axis_index("root"), 1, keepdims=False)
    terms = weights[:, None, None] * second[None]
    return lax.psum_scatter(terms, "root", scatter_dimension=0, tiled=True)


def solution(mesh):
    roots, groups = mesh.shape["root"], mesh.shape["col"]

    def shards(coeffs, diagonal, shift, rotation, string_blocks, block_cols):
        rows, strings = coeffs.shape[1:]
        blk = strings // block_cols.shape[0]
        width = strings // groups
        regular = blk % LANES == 0 and width % blk == 0 and rows == width > blk
        regular = regular and roots > 1 and roots & (roots - 1) == 0 and width % (16 * roots) == 0
        regular = regular and groups % 2 == 0 and blk % (16 * roots) == 0
        args = (coeffs, diagonal, shift, rotation, string_blocks, block_cols)
        if regular:
            return blocked_shards((roots, groups), *args)
        return plain_shards(*args)

    return jax.shard_map(
        shards,
        mesh=mesh,
        in_specs=(P("root", "col", None), P("col", None), P("root"), P(), P("col", None), P()),
        out_specs=P("root", "col", None),
        check_vma=False,
    )
```

```python
import functools

import jax
import jax.numpy as jnp
from jax import lax
from jax.experimental import pallas as pl
from jax.experimental.pallas import tpu as pltpu
from jax.sharding import PartitionSpec as P

LANES = 128
PAD = 16
TOP = 32764.0
LIMIT = 56 * 1024 * 1024


def scale_of(mantissa, exponent):
    return mantissa * jnp.exp2(exponent - 7.0) * (1.0 / TOP)


def encode(piece):
    width = piece.shape[1]
    top = jnp.maximum(jnp.max(jnp.abs(piece), axis=0, keepdims=True), 1e-25)
    exponent = jnp.floor(jnp.log2(top))
    mantissa = jnp.floor(top * jnp.exp2(7.0 - exponent)) + 1.0
    codes = jnp.floor(piece * (1.0 / scale_of(mantissa, exponent)) + 0.5)
    codes = codes.astype(jnp.int32).astype(jnp.int16)
    row = lax.broadcasted_iota(jnp.int32, (PAD, width), 0)
    tail = jnp.where(row == 0, mantissa, jnp.where(row == 1, exponent, 0.0))
    return codes, tail.astype(jnp.int32).astype(jnp.int16)


def put(ref, index, piece):
    height = piece.shape[0]
    codes, tail = encode(piece)
    ref[index, pl.ds(0, height), :] = codes
    ref[index, pl.ds(height, PAD), :] = tail


def decode(codes, tail):
    tail = tail.astype(jnp.int32).astype(jnp.float32)
    return codes.astype(jnp.int32).astype(jnp.float32) * scale_of(tail[0:1], tail[1:2])


def take(ref, index):
    height = ref.shape[1] - PAD
    return decode(ref[index, pl.ds(0, height), :], ref[index, pl.ds(height, PAD), :])


def split_into(halves, block, value):
    rows = value.shape[0]
    high = value.astype(jnp.bfloat16)
    halves[block, pl.ds(0, rows), :] = high
    low = value - high.astype(jnp.float32)
    halves[block, pl.ds(rows, rows), :] = low.astype(jnp.bfloat16)


def apply_row(halves, tiles, place, cols, block, fill, blk):
    rows = halves.shape[1] // 2
    total = jnp.zeros((2 * rows, blk), jnp.float32)
    for first in range(0, fill, 2):
        terms = range(first, min(first + 2, fill))
        left = [halves[cols[block, f]] for f in terms]
        right = tiles[pl.ds((place * fill + first) * blk, len(left) * blk), :]
        total += lax.dot_general(
            jnp.concatenate(left, axis=1),
            right,
            (((1,), (0,)), ((), ())),
            preferred_element_type=jnp.float32,
        )
    return total[:rows] + total[rows:]


def pack_kernel(here, v_ref, d_ref, out_ref):
    many, rows = out_ref.shape[0], out_ref.shape[2]
    width = v_ref.shape[1] // many
    slab = out_ref.shape[1] - width - PAD
    at = pl.multiple_of(here[0, 0] * slab, slab)
    for n in range(many):
        put(out_ref, n, v_ref[:, n * width : (n + 1) * width].T)
        mine = d_ref[pl.ds(at, slab), n * width : (n + 1) * width]
        codes = jnp.floor(mine * 32767.0 + 0.5)
        out_ref[n, pl.ds(width + PAD, slab), :] = codes.astype(jnp.int32).astype(jnp.int16)


def ring_at(spot, groups):
    return jnp.where(spot * 2 < groups, 2 * spot, 2 * (groups - 1 - spot) + 1)


def ring_spot(col, groups):
    half = jnp.right_shift(col, 1)
    return jnp.where(jnp.bitwise_and(col, 1) == 0, half, groups - 1 - half)


def right_first_kernel(dims, groups, owners, masks, cols, shift, place, v_ref, d_ref, own, *rest):
    nblk, fill, blk, per = dims
    shards, (w_ref, u_ref, more_ref, tiles_ref, halves, turned, tiles) = rest[:-7], rest[-7:]
    step = pl.program_id(0)
    size = own.shape[0]

    @pl.when(step == 0)
    def _():
        for b in range(nblk):
            split_into(halves, b, v_ref[:, b * blk : (b + 1) * blk])
        root, col = place[0, 0], place[0, 1]
        tiles[pl.ds(pl.multiple_of(col * size, size), size), :] = own[...]
        spot = ring_spot(col, groups)
        bases = [
            ring_at(lax.rem(spot + (owner + groups), groups), groups) * size
            + jnp.bitwise_xor(root, mask) * shards[0].shape[1]
            for owner in owners
            for mask in masks
        ]

        @pl.loop(0, size // blk)
        def _(b):
            for k, shard in enumerate(shards):
                share = shard.shape[1]
                at = pl.multiple_of(bases[k] + b * blk, share)
                tiles[pl.ds(at, share), :] = shard[b]

    here_tiles = tiles.at[pl.ds(pl.multiple_of(step * size, size), size), :]
    tiles_ref[...] = here_tiles[...]
    for t in range(per):
        lanes = slice(t * blk, (t + 1) * blk)
        block = step * per + t
        here = v_ref[:, pl.ds(pl.multiple_of(block * blk, blk), blk)]
        moved = apply_row(halves, here_tiles, t, cols, block, fill, blk)
        whole = moved + (d_ref[:, lanes] - shift[0, 0]) * here
        w_ref[:, lanes] = whole
        turned[lanes, :] = (moved + whole).T
    first = u_ref.shape[1] - PAD
    put(u_ref, 0, turned[:first])
    put(more_ref, 0, turned[first:])


def left_first_kernel(dims, cols, tv_ref, tiles, y_ref, halves):
    nblk, fill, blk, per = dims
    step = pl.program_id(0)

    @pl.when(step == 0)
    def _():
        for p in range(nblk // per):
            value = take(tv_ref, p)
            for t in range(per):
                split_into(halves, p * per + t, value[:, t * blk : (t + 1) * blk])

    for t in range(per):
        y_ref[:, t * blk : (t + 1) * blk] = apply_row(halves, tiles, t, cols, step * per + t, fill, blk)


def right_second_kernel(dims, cols, shift, w_ref, v_ref, d_ref, tiles, after, *rest):
    nblk, fill, blk, per = dims
    del after
    outs, halves = rest[:-1], rest[-1]
    step = pl.program_id(0)

    @pl.when(step == 0)
    def _():
        for b in range(nblk):
            split_into(halves, b, w_ref[:, b * blk : (b + 1) * blk])

    for t in range(per):
        lanes = slice(t * blk, (t + 1) * blk)
        block = step * per + t
        here = w_ref[:, pl.ds(pl.multiple_of(block * blk, blk), blk)]
        moved = apply_row(halves, tiles, t, cols, block, fill, blk)
        outs[t][...] = 0.5 * (moved + (d_ref[:, lanes] - shift[0, 0]) * here) - v_ref[:, lanes]


def left_second_kernel(dims, masks, cols, shift, place, tu_ref, tail_ref, y_ref, tiles, *rest):
    nblk, fill, blk, per = dims
    slabs, (_, out, halves, turned) = rest[:-4], rest[-4:]
    step = pl.program_id(0)
    part = y_ref.shape[0]

    @pl.when(step == 0)
    def _():
        for p in range(nblk // per):
            value = decode(tu_ref[p], tail_ref[p]) + y_ref[:, p * per * blk : (p + 1) * per * blk]
            for t in range(per):
                split_into(halves, p * per + t, value[:, t * blk : (t + 1) * blk])

    for m, slab in enumerate(slabs):
        height = slab.shape[1]
        at = pl.multiple_of(jnp.bitwise_xor(place[0, 0], masks[m]) * height, height)
        turned[pl.ds(at, height), :] = slab[0].astype(jnp.int32).astype(jnp.float32)
    done = []
    for t in range(per):
        block = step * per + t
        here = y_ref[:, pl.ds(pl.multiple_of(block * blk, blk), blk)]
        diagonal = turned[t * blk : (t + 1) * blk, :].T
        moved = apply_row(halves, tiles, t, cols, block, fill, blk)
        done.append((0.5 * (moved + (diagonal * (1.0 / 32767.0) - shift[0, 0]) * here)).T)
    put(out, 0, jnp.concatenate(done, axis=0))


def second_kernel(weights, z_ref, p_ref, out_ref):
    del weights
    part = z_ref.shape[2]
    for n in range(z_ref.shape[0]):
        put(out_ref, n, take(z_ref, n) + p_ref[:, n * part : (n + 1) * part])


def rotate_kernel(aliased, weights, *refs):
    ins, out_ref = refs[aliased:-1], refs[-1]
    total = weights[0, 0] * take(ins[0], 0)
    for m in range(1, len(ins)):
        total += weights[0, m] * take(ins[m], 0)
    out_ref[0] = total


def smem():
    return pl.BlockSpec(memory_space=pltpu.SMEM)


def call(kernel, grid, in_specs, out_specs, out_shape, scratch, flops, moved, aliases={}):
    return pl.pallas_call(
        kernel,
        grid=(grid,),
        in_specs=in_specs,
        out_specs=out_specs,
        out_shape=out_shape,
        scratch_shapes=scratch,
        input_output_aliases=aliases,
        compiler_params=pltpu.CompilerParams(
            dimension_semantics=("arbitrary",), vmem_limit_bytes=LIMIT
        ),
        cost_estimate=pl.CostEstimate(flops=flops, bytes_accessed=moved, transcendentals=0),
    )


def blocked_shards(sizes, coeffs, diagonal, shift, rotation, string_blocks, block_cols):
    roots, groups = sizes
    start = coeffs[0]
    rows, strings = start.shape
    nblk, fill = block_cols.shape
    blk = strings // nblk
    width = strings // groups
    per = width // blk
    chunks = per
    dims = (nblk, fill, blk, per)
    energy = shift.reshape(1, 1)
    root = lax.axis_index("root")
    f32, i16 = jnp.float32, jnp.int16

    def swap(pieces):
        return lax.all_to_all(pieces, "col", split_axis=0, concat_axis=0, tiled=True)

    piece = pl.BlockSpec((rows, width), lambda q: (0, q))
    whole = pl.BlockSpec((rows, strings), lambda q: (0, 0), pipeline_mode=pl.Buffered(1))
    coded = pl.BlockSpec((1, width + PAD, rows), lambda q: (q, 0, 0))
    all_coded = pl.BlockSpec((groups, width + PAD, rows), lambda q: (0, 0, 0), pipeline_mode=pl.Buffered(1))
    tile_spec = pl.BlockSpec((per * fill * blk, blk), lambda q: (q, 0))
    codes_shape = jax.ShapeDtypeStruct((groups, width + PAD, rows), i16)
    row_shape = jax.ShapeDtypeStruct((rows, strings), f32)
    row_halves = pltpu.VMEM((nblk, 2 * rows, blk), jnp.bfloat16)
    col_halves = pltpu.VMEM((nblk, 2 * width, blk), jnp.bfloat16)
    work = 2 * 2 * rows * strings * fill * blk
    size = 4 * rows * strings

    def cross(have, bit):
        pairs = [(r, r ^ bit) for r in range(roots)]
        return have + [lax.ppermute(h, "root", pairs) for h in have]

    def exchange(have, bit=roots // 2, late=None):
        if late is not None:
            have = have[:1] + list(lax.optimization_barrier((*have[1:], late)))[:-1]
        while bit:
            have = cross(have, bit)
            bit //= 2
        return have

    masks, bit = [0], roots // 2
    while bit:
        masks = masks + [m ^ bit for m in masks]
        bit //= 2
    far = jnp.bitwise_xor(root, jnp.array(masks, jnp.int32))
    weights = rotation[root][far].reshape(1, -1)
    place = jnp.stack([root, lax.axis_index("col")]).astype(jnp.int32).reshape(1, 2)

    ring = list(range(0, groups, 2)) + list(range(1, groups, 2))[::-1]
    share = blk // roots
    owners = []
    for hop in range(1, groups // 2 + 1):
        owners += [-hop, hop] if 2 * hop < groups else [-hop]

    slab = rows // roots
    height = width + PAD + slab

    def pack(start, diagonal):
        pair = 2 if groups % 2 == 0 else 1
        pieces = pl.BlockSpec((rows, pair * width), lambda q: (0, q))
        return call(
            pack_kernel,
            groups // pair,
            [smem(), pieces, pieces],
            pl.BlockSpec((pair, height, rows), lambda q: (q, 0, 0)),
            jax.ShapeDtypeStruct((groups, height, rows), i16),
            [],
            0,
            size * 3,
        )(place, start, diagonal)

    own = jnp.swapaxes(string_blocks.reshape(-1, blk, blk), 1, 2)
    mine = lax.dynamic_slice_in_dim(own, root * share, share, 1)
    shards, crossed, tv, forth, back = [], [], None, mine, mine
    for hop in range(1, groups // 2 + 1):
        if hop == 3:
            forth, back = lax.optimization_barrier((forth, back, tv, *crossed[:2]))[:2]
        for way in (1, -1) if 2 * hop < groups else (1,):
            pairs = [(ring[s], ring[(s + way) % groups]) for s in range(groups)]
            moved = lax.ppermute(forth if way == 1 else back, "col", pairs)
            forth, back = (moved, back) if way == 1 else (forth, moved)
            shards += exchange([moved])
            crossed.append(shards[1 - roots])
        if hop == 1:
            tv = pack(*lax.optimization_barrier((start, diagonal, forth, back))[:2])
    tv = swap(lax.optimization_barrier((tv, forth, back))[0])
    own = own.reshape(string_blocks.shape)

    once = pl.Buffered(1)
    shard_spec = pl.BlockSpec(mine.shape, lambda q: (0, 0, 0), pipeline_mode=once)
    part = width // chunks
    w, tu, more, tiles = call(
        functools.partial(right_first_kernel, dims, groups, owners, masks),
        groups,
        [smem(), smem(), smem(), whole, piece]
        + [pl.BlockSpec(string_blocks.shape, lambda q: (0, 0), pipeline_mode=once)]
        + [shard_spec] * len(shards),
        [piece]
        + [pl.BlockSpec((1, n + PAD, rows), lambda q: (q, 0, 0)) for n in (part, width - part)]
        + [tile_spec],
        [
            row_shape,
            jax.ShapeDtypeStruct((groups, part + PAD, rows), i16),
            jax.ShapeDtypeStruct((groups, width - part + PAD, rows), i16),
            jax.ShapeDtypeStruct((nblk * fill * blk, blk), string_blocks.dtype),
        ],
        [
            row_halves,
            pltpu.VMEM((width, rows), f32),
            pltpu.VMEM((nblk * fill * blk, blk), string_blocks.dtype),
        ],
        work,
        size * 6,
    )(block_cols, energy, place, start, diagonal, own, *shards)
    tu = swap(lax.optimization_barrier((tu, tv))[0])

    y = call(
        functools.partial(left_first_kernel, dims),
        groups,
        [smem(), all_coded, tile_spec],
        pl.BlockSpec((width, width), lambda q: (0, q)),
        jax.ShapeDtypeStruct((width, strings), f32),
        [col_halves],
        work,
        size * 3,
    )(block_cols, tv, tiles)
    more = swap(lax.optimization_barrier((more, tu, y))[0])

    base = call(
        functools.partial(right_second_kernel, dims),
        groups,
        [smem(), smem(), whole, piece, piece, tile_spec, pl.BlockSpec(memory_space=pl.ANY)],
        [pl.BlockSpec((rows, blk), lambda q: (0, q))] * chunks,
        [jax.ShapeDtypeStruct((rows, groups * blk), f32)] * chunks,
        [row_halves],
        work,
        size * 5,
    )(block_cols, energy, w, start, diagonal, tiles, tu)

    half = roots // 2
    slabs = exchange(cross([tv[:, width + PAD :]], half), half // 2, y)
    chunk_coded = pl.BlockSpec((1, rows + PAD, part), lambda q: (q, 0, 0))
    many = 4 if groups % 4 == 0 else 1
    many_coded = pl.BlockSpec((many, rows + PAD, part), lambda q: (q, 0, 0))
    seconds, crossings = [], []
    for k in range(chunks):
        source, at, n = (more, k - 1, width - part) if k else (tu, 0, part)
        z = call(
            functools.partial(left_second_kernel, dims, masks),
            groups,
            [
                smem(),
                smem(),
                smem(),
                pl.BlockSpec((groups, part, rows), lambda q, at=at: (0, at, 0), pipeline_mode=once),
                pl.BlockSpec((groups, PAD, rows), lambda q, n=n: (0, n // PAD, 0), pipeline_mode=once),
                pl.BlockSpec((part, strings), lambda q, k=k: (k, 0), pipeline_mode=once),
                tile_spec,
            ]
            + [pl.BlockSpec((1, slab, part), lambda q, k=k: (q, 0, k))] * roots
            + [pl.BlockSpec(memory_space=pl.ANY)],
            chunk_coded,
            jax.ShapeDtypeStruct((groups, rows + PAD, part), i16),
            [pltpu.VMEM((nblk, 2 * part, blk), jnp.bfloat16), pltpu.VMEM((rows, part), f32)],
            work // chunks,
            size * 4 // chunks,
        )(block_cols, energy, place, source, source, y, tiles, *slabs, base[0] if k < 2 else seconds[k - 2])
        if k > 1:
            z = lax.optimization_barrier((z, *crossings[k - 2]))[0]
        second = call(
            second_kernel,
            groups // many,
            [smem(), many_coded, pl.BlockSpec((rows, many * part), lambda q: (0, q))],
            many_coded,
            jax.ShapeDtypeStruct((groups, rows + PAD, part), i16),
            [],
            0,
            1,
        )(weights, swap(z), base[k])
        seconds.append(second)
        crossings.append(cross([second], half))
    out = []
    for k in range(chunks):
        late = seconds[k + 1] if k < chunks - 1 else out[0] if out else None
        slot = pl.BlockSpec((1, rows, part), lambda q, k=k: (0, 0, q * chunks + k))
        out = [
            call(
                functools.partial(rotate_kernel, len(out)),
                groups,
                [smem()] + [pl.BlockSpec(memory_space=pl.ANY)] * len(out) + [chunk_coded] * roots,
                slot,
                jax.ShapeDtypeStruct((1, rows, strings), f32),
                [],
                0,
                1,
                {1: 0} if out else {},
            )(weights, *out, *exchange(crossings[k], half // 2, late))
        ]
    return out[0]


def plain_blocks(matrix, operator_blocks, block_cols):
    height, breadth = matrix.shape
    nblocks, filled = block_cols.shape
    blocksize = breadth // nblocks
    grouped = matrix.reshape(height, nblocks, blocksize)
    picked = jnp.take(grouped, block_cols, axis=1)
    tiles = operator_blocks.reshape(nblocks, filled, blocksize, blocksize).astype(jnp.float32)
    result = jnp.einsum("rifk,ifjk->rij", picked, tiles, precision=lax.Precision.HIGHEST)
    return result.reshape(height, breadth)


def plain_swap(matrix):
    height, breadth = matrix.shape
    pieces = matrix.reshape(height, breadth // height, height).transpose(1, 2, 0)
    moved = lax.all_to_all(pieces, "col", split_axis=0, concat_axis=0, tiled=True)
    return moved.transpose(1, 0, 2).reshape(height, breadth)


def plain_shards(coeffs, diagonal, shift, rotation, string_blocks, block_cols):
    start = coeffs[0]
    energy = shift[0]
    operator_blocks = lax.all_gather(string_blocks, "col", axis=0, tiled=True)

    def sigma(vector):
        beta = plain_swap(plain_blocks(plain_swap(vector), operator_blocks, block_cols))
        return plain_blocks(vector, operator_blocks, block_cols) + beta + diagonal * vector

    first = 0.5 * (sigma(start) - energy * start)
    second = sigma(first) - energy * first - start
    weights = lax.dynamic_index_in_dim(rotation, lax.axis_index("root"), 1, keepdims=False)
    terms = weights[:, None, None] * second[None]
    return lax.psum_scatter(terms, "root", scatter_dimension=0, tiled=True)


def solution(mesh):
    roots, groups = mesh.shape["root"], mesh.shape["col"]

    def shards(coeffs, diagonal, shift, rotation, string_blocks, block_cols):
        rows, strings = coeffs.shape[1:]
        blk = strings // block_cols.shape[0]
        width = strings // groups
        regular = blk % LANES == 0 and width % blk == 0 and rows == width > blk
        regular = regular and roots > 1 and roots & (roots - 1) == 0 and width % (16 * roots) == 0
        regular = regular and groups % 2 == 0 and blk % (16 * roots) == 0
        args = (coeffs, diagonal, shift, rotation, string_blocks, block_cols)
        if regular:
            return blocked_shards((roots, groups), *args)
        return plain_shards(*args)

    return jax.shard_map(
        shards,
        mesh=mesh,
        in_specs=(P("root", "col", None), P("col", None), P("root"), P(), P("col", None), P()),
        out_specs=P("root", "col", None),
        check_vma=False,
    )
```

```python
import functools

import jax
import jax.numpy as jnp
from jax import lax
from jax.experimental import pallas as pl
from jax.experimental.pallas import tpu as pltpu
from jax.sharding import PartitionSpec as P

LANES = 128
PAD = 16
TOP = 32764.0
LIMIT = 56 * 1024 * 1024


def scale_of(mantissa, exponent):
    return mantissa * jnp.exp2(exponent - 7.0) * (1.0 / TOP)


def encode(piece):
    width = piece.shape[1]
    top = jnp.maximum(jnp.max(jnp.abs(piece), axis=0, keepdims=True), 1e-25)
    exponent = jnp.floor(jnp.log2(top))
    mantissa = jnp.floor(top * jnp.exp2(7.0 - exponent)) + 1.0
    codes = jnp.floor(piece * (1.0 / scale_of(mantissa, exponent)) + 0.5)
    codes = codes.astype(jnp.int32).astype(jnp.int16)
    row = lax.broadcasted_iota(jnp.int32, (PAD, width), 0)
    tail = jnp.where(row == 0, mantissa, jnp.where(row == 1, exponent, 0.0))
    return codes, tail.astype(jnp.int32).astype(jnp.int16)


def put(ref, index, piece):
    height = piece.shape[0]
    codes, tail = encode(piece)
    ref[index, pl.ds(0, height), :] = codes
    ref[index, pl.ds(height, PAD), :] = tail


def decode(codes, tail):
    tail = tail.astype(jnp.int32).astype(jnp.float32)
    return codes.astype(jnp.int32).astype(jnp.float32) * scale_of(tail[0:1], tail[1:2])


def take(ref, index):
    height = ref.shape[1] - PAD
    return decode(ref[index, pl.ds(0, height), :], ref[index, pl.ds(height, PAD), :])


def split_into(halves, block, value):
    rows = value.shape[0]
    high = value.astype(jnp.bfloat16)
    halves[block, pl.ds(0, rows), :] = high
    low = value - high.astype(jnp.float32)
    halves[block, pl.ds(rows, rows), :] = low.astype(jnp.bfloat16)


def apply_row(halves, tiles, place, cols, block, fill, blk):
    rows = halves.shape[1] // 2
    total = jnp.zeros((2 * rows, blk), jnp.float32)
    for first in range(0, fill, 2):
        terms = range(first, min(first + 2, fill))
        left = [halves[cols[block, f]] for f in terms]
        right = tiles[pl.ds((place * fill + first) * blk, len(left) * blk), :]
        total += lax.dot_general(
            jnp.concatenate(left, axis=1),
            right,
            (((1,), (0,)), ((), ())),
            preferred_element_type=jnp.float32,
        )
    return total[:rows] + total[rows:]


def pack_kernel(here, v_ref, d_ref, out_ref):
    many, rows = out_ref.shape[0], out_ref.shape[2]
    width = v_ref.shape[1] // many
    slab = out_ref.shape[1] - width - PAD
    at = pl.multiple_of(here[0, 0] * slab, slab)
    for n in range(many):
        put(out_ref, n, v_ref[:, n * width : (n + 1) * width].T)
        mine = d_ref[pl.ds(at, slab), n * width : (n + 1) * width]
        codes = jnp.floor(mine * 32767.0 + 0.5)
        out_ref[n, pl.ds(width + PAD, slab), :] = codes.astype(jnp.int32).astype(jnp.int16)


def ring_at(spot, groups):
    return jnp.where(spot * 2 < groups, 2 * spot, 2 * (groups - 1 - spot) + 1)


def ring_spot(col, groups):
    half = jnp.right_shift(col, 1)
    return jnp.where(jnp.bitwise_and(col, 1) == 0, half, groups - 1 - half)


def right_first_kernel(dims, groups, owners, masks, cols, shift, place, v_ref, d_ref, own, *rest):
    nblk, fill, blk, per = dims
    shards, (w_ref, u_ref, more_ref, tiles_ref, halves, turned, tiles) = rest[:-7], rest[-7:]
    step = pl.program_id(0)
    size = own.shape[0]

    @pl.when(step == 0)
    def _():
        for b in range(nblk):
            split_into(halves, b, v_ref[:, b * blk : (b + 1) * blk])
        root, col = place[0, 0], place[0, 1]
        tiles[pl.ds(pl.multiple_of(col * size, size), size), :] = own[...]
        spot = ring_spot(col, groups)
        bases = [
            ring_at(lax.rem(spot + (owner + groups), groups), groups) * size
            + jnp.bitwise_xor(root, mask) * shards[0].shape[1]
            for owner in owners
            for mask in masks
        ]

        @pl.loop(0, size // blk)
        def _(b):
            for k, shard in enumerate(shards):
                share = shard.shape[1]
                at = pl.multiple_of(bases[k] + b * blk, share)
                tiles[pl.ds(at, share), :] = shard[b]

    here_tiles = tiles.at[pl.ds(pl.multiple_of(step * size, size), size), :]
    tiles_ref[...] = here_tiles[...]
    for t in range(per):
        lanes = slice(t * blk, (t + 1) * blk)
        block = step * per + t
        here = v_ref[:, pl.ds(pl.multiple_of(block * blk, blk), blk)]
        moved = apply_row(halves, here_tiles, t, cols, block, fill, blk)
        whole = moved + (d_ref[:, lanes] - shift[0, 0]) * here
        w_ref[:, lanes] = whole
        turned[lanes, :] = (moved + whole).T
    first = u_ref.shape[1] - PAD
    put(u_ref, 0, turned[:first])
    put(more_ref, 0, turned[first:])


def left_first_kernel(dims, cols, tv_ref, tiles, y_ref, halves):
    nblk, fill, blk, per = dims
    step = pl.program_id(0)

    @pl.when(step == 0)
    def _():
        for p in range(nblk // per):
            value = take(tv_ref, p)
            for t in range(per):
                split_into(halves, p * per + t, value[:, t * blk : (t + 1) * blk])

    for t in range(per):
        y_ref[:, t * blk : (t + 1) * blk] = apply_row(halves, tiles, t, cols, step * per + t, fill, blk)


def right_second_kernel(dims, cols, shift, w_ref, v_ref, d_ref, tiles, after, *rest):
    nblk, fill, blk, per = dims
    del after
    outs, halves = rest[:-1], rest[-1]
    step = pl.program_id(0)

    @pl.when(step == 0)
    def _():
        for b in range(nblk):
            split_into(halves, b, w_ref[:, b * blk : (b + 1) * blk])

    for t in range(per):
        lanes = slice(t * blk, (t + 1) * blk)
        block = step * per + t
        here = w_ref[:, pl.ds(pl.multiple_of(block * blk, blk), blk)]
        moved = apply_row(halves, tiles, t, cols, block, fill, blk)
        outs[t][...] = 0.5 * (moved + (d_ref[:, lanes] - shift[0, 0]) * here) - v_ref[:, lanes]


def left_second_kernel(dims, masks, cols, shift, place, tu_ref, tail_ref, y_ref, tiles, *rest):
    nblk, fill, blk, per = dims
    slabs, (_, out, halves, turned) = rest[:-4], rest[-4:]
    step = pl.program_id(0)
    part = y_ref.shape[0]

    @pl.when(step == 0)
    def _():
        for p in range(nblk // per):
            value = decode(tu_ref[p], tail_ref[p]) + y_ref[:, p * per * blk : (p + 1) * per * blk]
            for t in range(per):
                split_into(halves, p * per + t, value[:, t * blk : (t + 1) * blk])

    for m, slab in enumerate(slabs):
        height = slab.shape[1]
        at = pl.multiple_of(jnp.bitwise_xor(place[0, 0], masks[m]) * height, height)
        turned[pl.ds(at, height), :] = slab[0].astype(jnp.int32).astype(jnp.float32)
    done = []
    for t in range(per):
        block = step * per + t
        here = y_ref[:, pl.ds(pl.multiple_of(block * blk, blk), blk)]
        diagonal = turned[t * blk : (t + 1) * blk, :].T
        moved = apply_row(halves, tiles, t, cols, block, fill, blk)
        done.append((0.5 * (moved + (diagonal * (1.0 / 32767.0) - shift[0, 0]) * here)).T)
    put(out, 0, jnp.concatenate(done, axis=0))


def second_kernel(weights, z_ref, p_ref, out_ref):
    del weights
    part = z_ref.shape[2]
    for n in range(z_ref.shape[0]):
        put(out_ref, n, take(z_ref, n) + p_ref[:, n * part : (n + 1) * part])


def rotate_kernel(aliased, weights, *refs):
    ins, out_ref = refs[aliased:-1], refs[-1]
    total = weights[0, 0] * take(ins[0], 0)
    for m in range(1, len(ins)):
        total += weights[0, m] * take(ins[m], 0)
    out_ref[0] = total


def smem():
    return pl.BlockSpec(memory_space=pltpu.SMEM)


def call(kernel, grid, in_specs, out_specs, out_shape, scratch, flops, moved, aliases={}):
    return pl.pallas_call(
        kernel,
        grid=(grid,),
        in_specs=in_specs,
        out_specs=out_specs,
        out_shape=out_shape,
        scratch_shapes=scratch,
        input_output_aliases=aliases,
        compiler_params=pltpu.CompilerParams(
            dimension_semantics=("arbitrary",), vmem_limit_bytes=LIMIT
        ),
        cost_estimate=pl.CostEstimate(flops=flops, bytes_accessed=moved, transcendentals=0),
    )


def blocked_shards(sizes, coeffs, diagonal, shift, rotation, string_blocks, block_cols):
    roots, groups = sizes
    start = coeffs[0]
    rows, strings = start.shape
    nblk, fill = block_cols.shape
    blk = strings // nblk
    width = strings // groups
    per = width // blk
    chunks = per
    dims = (nblk, fill, blk, per)
    energy = shift.reshape(1, 1)
    root = lax.axis_index("root")
    f32, i16 = jnp.float32, jnp.int16

    def swap(pieces):
        return lax.all_to_all(pieces, "col", split_axis=0, concat_axis=0, tiled=True)

    piece = pl.BlockSpec((rows, width), lambda q: (0, q))
    whole = pl.BlockSpec((rows, strings), lambda q: (0, 0), pipeline_mode=pl.Buffered(1))
    coded = pl.BlockSpec((1, width + PAD, rows), lambda q: (q, 0, 0))
    all_coded = pl.BlockSpec((groups, width + PAD, rows), lambda q: (0, 0, 0), pipeline_mode=pl.Buffered(1))
    tile_spec = pl.BlockSpec((per * fill * blk, blk), lambda q: (q, 0))
    codes_shape = jax.ShapeDtypeStruct((groups, width + PAD, rows), i16)
    row_shape = jax.ShapeDtypeStruct((rows, strings), f32)
    row_halves = pltpu.VMEM((nblk, 2 * rows, blk), jnp.bfloat16)
    col_halves = pltpu.VMEM((nblk, 2 * width, blk), jnp.bfloat16)
    work = 2 * 2 * rows * strings * fill * blk
    size = 4 * rows * strings

    def cross(have, bit):
        pairs = [(r, r ^ bit) for r in range(roots)]
        return have + [lax.ppermute(h, "root", pairs) for h in have]

    def exchange(have, bit=roots // 2, late=None):
        if late is not None:
            have = have[:1] + list(lax.optimization_barrier((*have[1:], late)))[:-1]
        while bit:
            have = cross(have, bit)
            bit //= 2
        return have

    masks, bit = [0], roots // 2
    while bit:
        masks = masks + [m ^ bit for m in masks]
        bit //= 2
    far = jnp.bitwise_xor(root, jnp.array(masks, jnp.int32))
    weights = rotation[root][far].reshape(1, -1)
    place = jnp.stack([root, lax.axis_index("col")]).astype(jnp.int32).reshape(1, 2)

    ring = list(range(0, groups, 2)) + list(range(1, groups, 2))[::-1]
    share = blk // roots
    owners = []
    for hop in range(1, groups // 2 + 1):
        owners += [-hop, hop] if 2 * hop < groups else [-hop]

    slab = rows // roots
    height = width + PAD + slab

    def pack(start, diagonal):
        pair = 2 if groups % 2 == 0 else 1
        pieces = pl.BlockSpec((rows, pair * width), lambda q: (0, q))
        return call(
            pack_kernel,
            groups // pair,
            [smem(), pieces, pieces],
            pl.BlockSpec((pair, height, rows), lambda q: (q, 0, 0)),
            jax.ShapeDtypeStruct((groups, height, rows), i16),
            [],
            0,
            size * 3,
        )(place, start, diagonal)

    own = jnp.swapaxes(string_blocks.reshape(-1, blk, blk), 1, 2)
    mine = lax.dynamic_slice_in_dim(own, root * share, share, 1)
    shards, crossed, tv, forth, back = [], [], None, mine, mine
    for hop in range(1, groups // 2 + 1):
        if hop == 3:
            forth, back = lax.optimization_barrier((forth, back, tv, *crossed[:2]))[:2]
        for way in (1, -1) if 2 * hop < groups else (1,):
            pairs = [(ring[s], ring[(s + way) % groups]) for s in range(groups)]
            moved = lax.ppermute(forth if way == 1 else back, "col", pairs)
            forth, back = (moved, back) if way == 1 else (forth, moved)
            shards += exchange([moved])
            crossed.append(shards[1 - roots])
        if hop == 1:
            tv = pack(*lax.optimization_barrier((start, diagonal, forth, back))[:2])
    tv = swap(lax.optimization_barrier((tv, forth, back))[0])
    own = own.reshape(string_blocks.shape)

    once = pl.Buffered(1)
    shard_spec = pl.BlockSpec(mine.shape, lambda q: (0, 0, 0), pipeline_mode=once)
    part = width // chunks
    w, tu, more, tiles = call(
        functools.partial(right_first_kernel, dims, groups, owners, masks),
        groups,
        [smem(), smem(), smem(), whole, piece]
        + [pl.BlockSpec(string_blocks.shape, lambda q: (0, 0), pipeline_mode=once)]
        + [shard_spec] * len(shards),
        [piece]
        + [pl.BlockSpec((1, n + PAD, rows), lambda q: (q, 0, 0)) for n in (part, width - part)]
        + [tile_spec],
        [
            row_shape,
            jax.ShapeDtypeStruct((groups, part + PAD, rows), i16),
            jax.ShapeDtypeStruct((groups, width - part + PAD, rows), i16),
            jax.ShapeDtypeStruct((nblk * fill * blk, blk), string_blocks.dtype),
        ],
        [
            row_halves,
            pltpu.VMEM((width, rows), f32),
            pltpu.VMEM((nblk * fill * blk, blk), string_blocks.dtype),
        ],
        work,
        size * 6,
    )(block_cols, energy, place, start, diagonal, own, *shards)
    tu = swap(lax.optimization_barrier((tu, tv))[0])

    y = call(
        functools.partial(left_first_kernel, dims),
        groups,
        [smem(), all_coded, tile_spec],
        pl.BlockSpec((width, width), lambda q: (0, q)),
        jax.ShapeDtypeStruct((width, strings), f32),
        [col_halves],
        work,
        size * 3,
    )(block_cols, tv, tiles)
    more = swap(lax.optimization_barrier((more, tu, y))[0])

    base = call(
        functools.partial(right_second_kernel, dims),
        groups,
        [smem(), smem(), whole, piece, piece, tile_spec, pl.BlockSpec(memory_space=pl.ANY)],
        [pl.BlockSpec((rows, blk), lambda q: (0, q))] * chunks,
        [jax.ShapeDtypeStruct((rows, groups * blk), f32)] * chunks,
        [row_halves],
        work,
        size * 5,
    )(block_cols, energy, w, start, diagonal, tiles, tu)

    half = roots // 2
    slabs = exchange(cross([tv[:, width + PAD :]], half), half // 2, base[0])
    chunk_coded = pl.BlockSpec((1, rows + PAD, part), lambda q: (q, 0, 0))
    many = 4 if groups % 4 == 0 else 1
    many_coded = pl.BlockSpec((many, rows + PAD, part), lambda q: (q, 0, 0))
    seconds, crossings = [], []
    for k in range(chunks):
        source, at, n = (more, k - 1, width - part) if k else (tu, 0, part)
        z = call(
            functools.partial(left_second_kernel, dims, masks),
            groups,
            [
                smem(),
                smem(),
                smem(),
                pl.BlockSpec((groups, part, rows), lambda q, at=at: (0, at, 0), pipeline_mode=once),
                pl.BlockSpec((groups, PAD, rows), lambda q, n=n: (0, n // PAD, 0), pipeline_mode=once),
                pl.BlockSpec((part, strings), lambda q, k=k: (k, 0), pipeline_mode=once),
                tile_spec,
            ]
            + [pl.BlockSpec((1, slab, part), lambda q, k=k: (q, 0, k))] * roots
            + [pl.BlockSpec(memory_space=pl.ANY)],
            chunk_coded,
            jax.ShapeDtypeStruct((groups, rows + PAD, part), i16),
            [pltpu.VMEM((nblk, 2 * part, blk), jnp.bfloat16), pltpu.VMEM((rows, part), f32)],
            work // chunks,
            size * 4 // chunks,
        )(block_cols, energy, place, source, source, y, tiles, *slabs, base[0] if k < 2 else seconds[k - 2])
        if k > 1:
            z = lax.optimization_barrier((z, *crossings[k - 2]))[0]
        second = call(
            second_kernel,
            groups // many,
            [smem(), many_coded, pl.BlockSpec((rows, many * part), lambda q: (0, q))],
            many_coded,
            jax.ShapeDtypeStruct((groups, rows + PAD, part), i16),
            [],
            0,
            1,
        )(weights, swap(z), base[k])
        seconds.append(second)
        crossings.append(cross([second], half))
    out = []
    for k in range(chunks):
        late = seconds[k + 1] if k < chunks - 1 else out[0] if out else None
        slot = pl.BlockSpec((1, rows, part), lambda q, k=k: (0, 0, q * chunks + k))
        out = [
            call(
                functools.partial(rotate_kernel, len(out)),
                groups,
                [smem()] + [pl.BlockSpec(memory_space=pl.ANY)] * len(out) + [chunk_coded] * roots,
                slot,
                jax.ShapeDtypeStruct((1, rows, strings), f32),
                [],
                0,
                1,
                {1: 0} if out else {},
            )(weights, *out, *exchange(crossings[k], half // 2, late))
        ]
    return out[0]


def plain_blocks(matrix, operator_blocks, block_cols):
    height, breadth = matrix.shape
    nblocks, filled = block_cols.shape
    blocksize = breadth // nblocks
    grouped = matrix.reshape(height, nblocks, blocksize)
    picked = jnp.take(grouped, block_cols, axis=1)
    tiles = operator_blocks.reshape(nblocks, filled, blocksize, blocksize).astype(jnp.float32)
    result = jnp.einsum("rifk,ifjk->rij", picked, tiles, precision=lax.Precision.HIGHEST)
    return result.reshape(height, breadth)


def plain_swap(matrix):
    height, breadth = matrix.shape
    pieces = matrix.reshape(height, breadth // height, height).transpose(1, 2, 0)
    moved = lax.all_to_all(pieces, "col", split_axis=0, concat_axis=0, tiled=True)
    return moved.transpose(1, 0, 2).reshape(height, breadth)


def plain_shards(coeffs, diagonal, shift, rotation, string_blocks, block_cols):
    start = coeffs[0]
    energy = shift[0]
    operator_blocks = lax.all_gather(string_blocks, "col", axis=0, tiled=True)

    def sigma(vector):
        beta = plain_swap(plain_blocks(plain_swap(vector), operator_blocks, block_cols))
        return plain_blocks(vector, operator_blocks, block_cols) + beta + diagonal * vector

    first = 0.5 * (sigma(start) - energy * start)
    second = sigma(first) - energy * first - start
    weights = lax.dynamic_index_in_dim(rotation, lax.axis_index("root"), 1, keepdims=False)
    terms = weights[:, None, None] * second[None]
    return lax.psum_scatter(terms, "root", scatter_dimension=0, tiled=True)


def solution(mesh):
    roots, groups = mesh.shape["root"], mesh.shape["col"]

    def shards(coeffs, diagonal, shift, rotation, string_blocks, block_cols):
        rows, strings = coeffs.shape[1:]
        blk = strings // block_cols.shape[0]
        width = strings // groups
        regular = blk % LANES == 0 and width % blk == 0 and rows == width > blk
        regular = regular and roots > 1 and roots & (roots - 1) == 0 and width % (16 * roots) == 0
        regular = regular and groups % 2 == 0 and blk % (16 * roots) == 0
        args = (coeffs, diagonal, shift, rotation, string_blocks, block_cols)
        if regular:
            return blocked_shards((roots, groups), *args)
        return plain_shards(*args)

    return jax.shard_map(
        shards,
        mesh=mesh,
        in_specs=(P("root", "col", None), P("col", None), P("root"), P(), P("col", None), P()),
        out_specs=P("root", "col", None),
        check_vma=False,
    )
```

```python
import functools

import jax
import jax.numpy as jnp
from jax import lax
from jax.experimental import pallas as pl
from jax.experimental.pallas import tpu as pltpu
from jax.sharding import PartitionSpec as P

LANES = 128
PAD = 16
TOP = 32764.0
LIMIT = 56 * 1024 * 1024


def scale_of(mantissa, exponent):
    return mantissa * jnp.exp2(exponent - 7.0) * (1.0 / TOP)


def encode(piece):
    width = piece.shape[1]
    top = jnp.maximum(jnp.max(jnp.abs(piece), axis=0, keepdims=True), 1e-25)
    exponent = jnp.floor(jnp.log2(top))
    mantissa = jnp.floor(top * jnp.exp2(7.0 - exponent)) + 1.0
    codes = jnp.floor(piece * (1.0 / scale_of(mantissa, exponent)) + 0.5)
    codes = codes.astype(jnp.int32).astype(jnp.int16)
    row = lax.broadcasted_iota(jnp.int32, (PAD, width), 0)
    tail = jnp.where(row == 0, mantissa, jnp.where(row == 1, exponent, 0.0))
    return codes, tail.astype(jnp.int32).astype(jnp.int16)


def put(ref, index, piece):
    height = piece.shape[0]
    codes, tail = encode(piece)
    ref[index, pl.ds(0, height), :] = codes
    ref[index, pl.ds(height, PAD), :] = tail


def decode(codes, tail):
    tail = tail.astype(jnp.int32).astype(jnp.float32)
    return codes.astype(jnp.int32).astype(jnp.float32) * scale_of(tail[0:1], tail[1:2])


def take(ref, index):
    height = ref.shape[1] - PAD
    return decode(ref[index, pl.ds(0, height), :], ref[index, pl.ds(height, PAD), :])


def split_into(halves, block, value):
    rows = value.shape[0]
    high = value.astype(jnp.bfloat16)
    halves[block, pl.ds(0, rows), :] = high
    low = value - high.astype(jnp.float32)
    halves[block, pl.ds(rows, rows), :] = low.astype(jnp.bfloat16)


def apply_row(halves, tiles, place, cols, block, fill, blk):
    rows = halves.shape[1] // 2
    total = jnp.zeros((2 * rows, blk), jnp.float32)
    for first in range(0, fill, 2):
        terms = range(first, min(first + 2, fill))
        left = [halves[cols[block, f]] for f in terms]
        right = tiles[pl.ds((place * fill + first) * blk, len(left) * blk), :]
        total += lax.dot_general(
            jnp.concatenate(left, axis=1),
            right,
            (((1,), (0,)), ((), ())),
            preferred_element_type=jnp.float32,
        )
    return total[:rows] + total[rows:]


def pack_kernel(here, v_ref, d_ref, out_ref):
    many, rows = out_ref.shape[0], out_ref.shape[2]
    width = v_ref.shape[1] // many
    slab = out_ref.shape[1] - width - PAD
    at = pl.multiple_of(here[0, 0] * slab, slab)
    for n in range(many):
        put(out_ref, n, v_ref[:, n * width : (n + 1) * width].T)
        mine = d_ref[pl.ds(at, slab), n * width : (n + 1) * width]
        codes = jnp.floor(mine * 32767.0 + 0.5)
        out_ref[n, pl.ds(width + PAD, slab), :] = codes.astype(jnp.int32).astype(jnp.int16)


def ring_at(spot, groups):
    return jnp.where(spot * 2 < groups, 2 * spot, 2 * (groups - 1 - spot) + 1)


def ring_spot(col, groups):
    half = jnp.right_shift(col, 1)
    return jnp.where(jnp.bitwise_and(col, 1) == 0, half, groups - 1 - half)


def right_first_kernel(dims, groups, owners, masks, cols, shift, place, v_ref, d_ref, own, *rest):
    nblk, fill, blk, per = dims
    shards, (w_ref, u_ref, more_ref, tiles_ref, halves, turned, tiles) = rest[:-7], rest[-7:]
    step = pl.program_id(0)
    size = own.shape[0]

    @pl.when(step == 0)
    def _():
        for b in range(nblk):
            split_into(halves, b, v_ref[:, b * blk : (b + 1) * blk])
        root, col = place[0, 0], place[0, 1]
        tiles[pl.ds(pl.multiple_of(col * size, size), size), :] = own[...]
        spot = ring_spot(col, groups)
        bases = [
            ring_at(lax.rem(spot + (owner + groups), groups), groups) * size
            + jnp.bitwise_xor(root, mask) * shards[0].shape[1]
            for owner in owners
            for mask in masks
        ]

        @pl.loop(0, size // blk)
        def _(b):
            for k, shard in enumerate(shards):
                share = shard.shape[1]
                at = pl.multiple_of(bases[k] + b * blk, share)
                tiles[pl.ds(at, share), :] = shard[b]

    here_tiles = tiles.at[pl.ds(pl.multiple_of(step * size, size), size), :]
    tiles_ref[...] = here_tiles[...]
    for t in range(per):
        lanes = slice(t * blk, (t + 1) * blk)
        block = step * per + t
        here = v_ref[:, pl.ds(pl.multiple_of(block * blk, blk), blk)]
        moved = apply_row(halves, here_tiles, t, cols, block, fill, blk)
        whole = moved + (d_ref[:, lanes] - shift[0, 0]) * here
        w_ref[:, lanes] = whole
        turned[lanes, :] = (moved + whole).T
    first = u_ref.shape[1] - PAD
    put(u_ref, 0, turned[:first])
    put(more_ref, 0, turned[first:])


def left_first_kernel(dims, cols, tv_ref, tiles, y_ref, halves):
    nblk, fill, blk, per = dims
    step = pl.program_id(0)

    @pl.when(step == 0)
    def _():
        for p in range(nblk // per):
            value = take(tv_ref, p)
            for t in range(per):
                split_into(halves, p * per + t, value[:, t * blk : (t + 1) * blk])

    for t in range(per):
        y_ref[:, t * blk : (t + 1) * blk] = apply_row(halves, tiles, t, cols, step * per + t, fill, blk)


def right_second_kernel(dims, cols, shift, w_ref, v_ref, d_ref, tiles, after, *rest):
    nblk, fill, blk, per = dims
    del after
    outs, halves = rest[:-1], rest[-1]
    step = pl.program_id(0)

    @pl.when(step == 0)
    def _():
        for b in range(nblk):
            split_into(halves, b, w_ref[:, b * blk : (b + 1) * blk])

    for t in range(per):
        lanes = slice(t * blk, (t + 1) * blk)
        block = step * per + t
        here = w_ref[:, pl.ds(pl.multiple_of(block * blk, blk), blk)]
        moved = apply_row(halves, tiles, t, cols, block, fill, blk)
        outs[t][...] = 0.5 * (moved + (d_ref[:, lanes] - shift[0, 0]) * here) - v_ref[:, lanes]


def left_second_kernel(dims, masks, cols, shift, place, tu_ref, tail_ref, y_ref, tiles, *rest):
    nblk, fill, blk, per = dims
    slabs, (_, out, halves, turned) = rest[:-4], rest[-4:]
    step = pl.program_id(0)
    part = y_ref.shape[0]

    @pl.when(step == 0)
    def _():
        for p in range(nblk // per):
            value = decode(tu_ref[p], tail_ref[p]) + y_ref[:, p * per * blk : (p + 1) * per * blk]
            for t in range(per):
                split_into(halves, p * per + t, value[:, t * blk : (t + 1) * blk])

    for m, slab in enumerate(slabs):
        height = slab.shape[1]
        at = pl.multiple_of(jnp.bitwise_xor(place[0, 0], masks[m]) * height, height)
        turned[pl.ds(at, height), :] = slab[0].astype(jnp.int32).astype(jnp.float32)
    done = []
    for t in range(per):
        block = step * per + t
        here = y_ref[:, pl.ds(pl.multiple_of(block * blk, blk), blk)]
        diagonal = turned[t * blk : (t + 1) * blk, :].T
        moved = apply_row(halves, tiles, t, cols, block, fill, blk)
        done.append((0.5 * (moved + (diagonal * (1.0 / 32767.0) - shift[0, 0]) * here)).T)
    put(out, 0, jnp.concatenate(done, axis=0))


def second_kernel(weights, z_ref, p_ref, out_ref):
    del weights
    part = z_ref.shape[2]
    for n in range(z_ref.shape[0]):
        put(out_ref, n, take(z_ref, n) + p_ref[:, n * part : (n + 1) * part])


def rotate_kernel(aliased, weights, *refs):
    ins, out_ref = refs[aliased:-1], refs[-1]
    total = weights[0, 0] * take(ins[0], 0)
    for m in range(1, len(ins)):
        total += weights[0, m] * take(ins[m], 0)
    out_ref[0] = total


def smem():
    return pl.BlockSpec(memory_space=pltpu.SMEM)


def call(kernel, grid, in_specs, out_specs, out_shape, scratch, flops, moved, aliases={}):
    return pl.pallas_call(
        kernel,
        grid=(grid,),
        in_specs=in_specs,
        out_specs=out_specs,
        out_shape=out_shape,
        scratch_shapes=scratch,
        input_output_aliases=aliases,
        compiler_params=pltpu.CompilerParams(
            dimension_semantics=("arbitrary",), vmem_limit_bytes=LIMIT
        ),
        cost_estimate=pl.CostEstimate(flops=flops, bytes_accessed=moved, transcendentals=0),
    )


def blocked_shards(sizes, coeffs, diagonal, shift, rotation, string_blocks, block_cols):
    roots, groups = sizes
    start = coeffs[0]
    rows, strings = start.shape
    nblk, fill = block_cols.shape
    blk = strings // nblk
    width = strings // groups
    per = width // blk
    chunks = per
    dims = (nblk, fill, blk, per)
    energy = shift.reshape(1, 1)
    root = lax.axis_index("root")
    f32, i16 = jnp.float32, jnp.int16

    def swap(pieces):
        return lax.all_to_all(pieces, "col", split_axis=0, concat_axis=0, tiled=True)

    piece = pl.BlockSpec((rows, width), lambda q: (0, q))
    whole = pl.BlockSpec((rows, strings), lambda q: (0, 0), pipeline_mode=pl.Buffered(1))
    coded = pl.BlockSpec((1, width + PAD, rows), lambda q: (q, 0, 0))
    all_coded = pl.BlockSpec((groups, width + PAD, rows), lambda q: (0, 0, 0), pipeline_mode=pl.Buffered(1))
    tile_spec = pl.BlockSpec((per * fill * blk, blk), lambda q: (q, 0))
    codes_shape = jax.ShapeDtypeStruct((groups, width + PAD, rows), i16)
    row_shape = jax.ShapeDtypeStruct((rows, strings), f32)
    row_halves = pltpu.VMEM((nblk, 2 * rows, blk), jnp.bfloat16)
    col_halves = pltpu.VMEM((nblk, 2 * width, blk), jnp.bfloat16)
    work = 2 * 2 * rows * strings * fill * blk
    size = 4 * rows * strings

    def cross(have, bit):
        pairs = [(r, r ^ bit) for r in range(roots)]
        return have + [lax.ppermute(h, "root", pairs) for h in have]

    def exchange(have, bit=roots // 2, late=None):
        if late is not None:
            have = have[:1] + list(lax.optimization_barrier((*have[1:], late)))[:-1]
        while bit:
            have = cross(have, bit)
            bit //= 2
        return have

    masks, bit = [0], roots // 2
    while bit:
        masks = masks + [m ^ bit for m in masks]
        bit //= 2
    far = jnp.bitwise_xor(root, jnp.array(masks, jnp.int32))
    weights = rotation[root][far].reshape(1, -1)
    place = jnp.stack([root, lax.axis_index("col")]).astype(jnp.int32).reshape(1, 2)

    ring = list(range(0, groups, 2)) + list(range(1, groups, 2))[::-1]
    share = blk // roots
    owners = []
    for hop in range(1, groups // 2 + 1):
        owners += [-hop, hop] if 2 * hop < groups else [-hop]

    slab = rows // roots
    height = width + PAD + slab

    def pack(start, diagonal):
        pair = 4 if groups % 4 == 0 else 1
        pieces = pl.BlockSpec((rows, pair * width), lambda q: (0, q))
        return call(
            pack_kernel,
            groups // pair,
            [smem(), pieces, pieces],
            pl.BlockSpec((pair, height, rows), lambda q: (q, 0, 0)),
            jax.ShapeDtypeStruct((groups, height, rows), i16),
            [],
            0,
            size * 3,
        )(place, start, diagonal)

    own = jnp.swapaxes(string_blocks.reshape(-1, blk, blk), 1, 2)
    mine = lax.dynamic_slice_in_dim(own, root * share, share, 1)
    shards, crossed, tv, forth, back = [], [], None, mine, mine
    for hop in range(1, groups // 2 + 1):
        if hop == 3:
            forth, back = lax.optimization_barrier((forth, back, tv, *crossed[:2]))[:2]
        for way in (1, -1) if 2 * hop < groups else (1,):
            pairs = [(ring[s], ring[(s + way) % groups]) for s in range(groups)]
            moved = lax.ppermute(forth if way == 1 else back, "col", pairs)
            forth, back = (moved, back) if way == 1 else (forth, moved)
            shards += exchange([moved])
            crossed.append(shards[1 - roots])
        if hop == 1:
            tv = pack(*lax.optimization_barrier((start, diagonal, forth, back))[:2])
    tv = swap(lax.optimization_barrier((tv, forth, back))[0])
    own = own.reshape(string_blocks.shape)

    once = pl.Buffered(1)
    shard_spec = pl.BlockSpec(mine.shape, lambda q: (0, 0, 0), pipeline_mode=once)
    part = width // chunks
    w, tu, more, tiles = call(
        functools.partial(right_first_kernel, dims, groups, owners, masks),
        groups,
        [smem(), smem(), smem(), whole, piece]
        + [pl.BlockSpec(string_blocks.shape, lambda q: (0, 0), pipeline_mode=once)]
        + [shard_spec] * len(shards),
        [piece]
        + [pl.BlockSpec((1, n + PAD, rows), lambda q: (q, 0, 0)) for n in (part, width - part)]
        + [tile_spec],
        [
            row_shape,
            jax.ShapeDtypeStruct((groups, part + PAD, rows), i16),
            jax.ShapeDtypeStruct((groups, width - part + PAD, rows), i16),
            jax.ShapeDtypeStruct((nblk * fill * blk, blk), string_blocks.dtype),
        ],
        [
            row_halves,
            pltpu.VMEM((width, rows), f32),
            pltpu.VMEM((nblk * fill * blk, blk), string_blocks.dtype),
        ],
        work,
        size * 6,
    )(block_cols, energy, place, start, diagonal, own, *shards)
    tu = swap(lax.optimization_barrier((tu, tv))[0])

    y = call(
        functools.partial(left_first_kernel, dims),
        groups,
        [smem(), all_coded, tile_spec],
        pl.BlockSpec((width, width), lambda q: (0, q)),
        jax.ShapeDtypeStruct((width, strings), f32),
        [col_halves],
        work,
        size * 3,
    )(block_cols, tv, tiles)
    more = swap(lax.optimization_barrier((more, tu, y))[0])

    base = call(
        functools.partial(right_second_kernel, dims),
        groups,
        [smem(), smem(), whole, piece, piece, tile_spec, pl.BlockSpec(memory_space=pl.ANY)],
        [pl.BlockSpec((rows, blk), lambda q: (0, q))] * chunks,
        [jax.ShapeDtypeStruct((rows, groups * blk), f32)] * chunks,
        [row_halves],
        work,
        size * 5,
    )(block_cols, energy, w, start, diagonal, tiles, tu)

    half = roots // 2
    slabs = exchange(cross([tv[:, width + PAD :]], half), half // 2, base[0])
    chunk_coded = pl.BlockSpec((1, rows + PAD, part), lambda q: (q, 0, 0))
    many = 4 if groups % 4 == 0 else 1
    many_coded = pl.BlockSpec((many, rows + PAD, part), lambda q: (q, 0, 0))
    seconds, crossings = [], []
    for k in range(chunks):
        source, at, n = (more, k - 1, width - part) if k else (tu, 0, part)
        z = call(
            functools.partial(left_second_kernel, dims, masks),
            groups,
            [
                smem(),
                smem(),
                smem(),
                pl.BlockSpec((groups, part, rows), lambda q, at=at: (0, at, 0), pipeline_mode=once),
                pl.BlockSpec((groups, PAD, rows), lambda q, n=n: (0, n // PAD, 0), pipeline_mode=once),
                pl.BlockSpec((part, strings), lambda q, k=k: (k, 0), pipeline_mode=once),
                tile_spec,
            ]
            + [pl.BlockSpec((1, slab, part), lambda q, k=k: (q, 0, k))] * roots
            + [pl.BlockSpec(memory_space=pl.ANY)],
            chunk_coded,
            jax.ShapeDtypeStruct((groups, rows + PAD, part), i16),
            [pltpu.VMEM((nblk, 2 * part, blk), jnp.bfloat16), pltpu.VMEM((rows, part), f32)],
            work // chunks,
            size * 4 // chunks,
        )(block_cols, energy, place, source, source, y, tiles, *slabs, base[0] if k < 2 else seconds[k - 2])
        if k > 1:
            z = lax.optimization_barrier((z, *crossings[k - 2]))[0]
        second = call(
            second_kernel,
            groups // many,
            [smem(), many_coded, pl.BlockSpec((rows, many * part), lambda q: (0, q))],
            many_coded,
            jax.ShapeDtypeStruct((groups, rows + PAD, part), i16),
            [],
            0,
            1,
        )(weights, swap(z), base[k])
        seconds.append(second)
        crossings.append(cross([second], half))
    out = []
    for k in range(chunks):
        late = seconds[k + 1] if k < chunks - 1 else out[0] if out else None
        slot = pl.BlockSpec((1, rows, part), lambda q, k=k: (0, 0, q * chunks + k))
        out = [
            call(
                functools.partial(rotate_kernel, len(out)),
                groups,
                [smem()] + [pl.BlockSpec(memory_space=pl.ANY)] * len(out) + [chunk_coded] * roots,
                slot,
                jax.ShapeDtypeStruct((1, rows, strings), f32),
                [],
                0,
                1,
                {1: 0} if out else {},
            )(weights, *out, *exchange(crossings[k], half // 2, late))
        ]
    return out[0]


def plain_blocks(matrix, operator_blocks, block_cols):
    height, breadth = matrix.shape
    nblocks, filled = block_cols.shape
    blocksize = breadth // nblocks
    grouped = matrix.reshape(height, nblocks, blocksize)
    picked = jnp.take(grouped, block_cols, axis=1)
    tiles = operator_blocks.reshape(nblocks, filled, blocksize, blocksize).astype(jnp.float32)
    result = jnp.einsum("rifk,ifjk->rij", picked, tiles, precision=lax.Precision.HIGHEST)
    return result.reshape(height, breadth)


def plain_swap(matrix):
    height, breadth = matrix.shape
    pieces = matrix.reshape(height, breadth // height, height).transpose(1, 2, 0)
    moved = lax.all_to_all(pieces, "col", split_axis=0, concat_axis=0, tiled=True)
    return moved.transpose(1, 0, 2).reshape(height, breadth)


def plain_shards(coeffs, diagonal, shift, rotation, string_blocks, block_cols):
    start = coeffs[0]
    energy = shift[0]
    operator_blocks = lax.all_gather(string_blocks, "col", axis=0, tiled=True)

    def sigma(vector):
        beta = plain_swap(plain_blocks(plain_swap(vector), operator_blocks, block_cols))
        return plain_blocks(vector, operator_blocks, block_cols) + beta + diagonal * vector

    first = 0.5 * (sigma(start) - energy * start)
    second = sigma(first) - energy * first - start
    weights = lax.dynamic_index_in_dim(rotation, lax.axis_index("root"), 1, keepdims=False)
    terms = weights[:, None, None] * second[None]
    return lax.psum_scatter(terms, "root", scatter_dimension=0, tiled=True)


def solution(mesh):
    roots, groups = mesh.shape["root"], mesh.shape["col"]

    def shards(coeffs, diagonal, shift, rotation, string_blocks, block_cols):
        rows, strings = coeffs.shape[1:]
        blk = strings // block_cols.shape[0]
        width = strings // groups
        regular = blk % LANES == 0 and width % blk == 0 and rows == width > blk
        regular = regular and roots > 1 and roots & (roots - 1) == 0 and width % (16 * roots) == 0
        regular = regular and groups % 2 == 0 and blk % (16 * roots) == 0
        args = (coeffs, diagonal, shift, rotation, string_blocks, block_cols)
        if regular:
            return blocked_shards((roots, groups), *args)
        return plain_shards(*args)

    return jax.shard_map(
        shards,
        mesh=mesh,
        in_specs=(P("root", "col", None), P("col", None), P("root"), P(), P("col", None), P()),
        out_specs=P("root", "col", None),
        check_vma=False,
    )
```
